32 devices in a mesh: tm: 8 (over y, x, core), space: 4 (over z).
Axes of the slice: x: 2, y: 2, z: 4, core: 2. Of those that a mesh axis runs over, the one named last changes fastest.
Arguments:
- sep_block: float32 [8, 1536, 1536], P('tm', 'space'), may hold values from -1 to 10, as said below
- own_couple: bfloat16 [8, 1536, 1536], P('tm', 'space'), may hold values from -0.1875 to 0.1875
- prev_couple: bfloat16 [8, 1536, 1536], P('tm', 'space'), may hold values from -0.1875 to 0.1875
- inner_diag: float32 [8, 1536], P('tm'), may hold values from 0.5 to 4
Outputs:
- reduced_blocks: float32 [8, 1536, 1536], P('tm', 'space')
- left_links: bfloat16 [8, 1536, 1536], P('tm', 'space')
The draws below stay inside these ranges and needn't reach their ends.
Inputs may be any that keep to these rules, and one draw needn't show every extreme that they name: sep_block is symmetric in its last two dimensions; its diagonal entries lie between 3.5 and 10.
All inputs are finite; a program needn't handle non-finite values.
Results may differ from the reference program's by a relative error of at most 0.0083.
Values may be sent and summed in bfloat16 or wider, within the bound.
No kernel may reach another device: no remote copies, remote signals or barrier semaphores. Data moves between devices by JAX's collectives and lax.ppermute only.
A program may use at most 64 MiB of HBM per device.

```python
import math
import jax
import jax.numpy as jnp
from jax import lax

BLOCK = 1536
PARTS_SIZE = 8


def draw_sep_block(key, part):
    noise_key, level_key = jax.random.split(jax.random.fold_in(key, 17))
    full_shape = (PARTS_SIZE, BLOCK, BLOCK)
    noise_field = jnp.clip(jax.random.normal(noise_key, full_shape, jnp.float32), -4.0, 4.0)
    diag_values = jax.random.uniform(level_key, (PARTS_SIZE, BLOCK), jnp.float32, 3.5, 10.0)
    off_diagonal = (noise_field + jnp.swapaxes(noise_field, 1, 2)) * (0.7071 / math.sqrt(BLOCK))
    diagonal_mask = jnp.eye(BLOCK, dtype=bool)
    return jnp.where(diagonal_mask[None, :, :], diag_values[:, :, None], off_diagonal)


def block_scale(rng, dims, pieces, low, top_value):
    def one(axis_at, shards_of):
        draws = jax.random.uniform(jax.random.fold_in(jax.random.fold_in(rng, 6), axis_at), (shards_of,), jnp.float32, low / len(pieces), top_value / len(pieces))
        return jnp.repeat(jnp.exp(draws), dims[axis_at] // shards_of).reshape((-1,) + (1,) * (len(dims) - axis_at - 1))

    gain = one(*pieces[0])
    for cut in pieces[1:]:
        gain = gain * one(*cut)
    return gain


def gaussian(key, dims, deviation, most, shards=(), kind=jnp.bfloat16):
    gain = block_scale(key, dims, shards, -0.22, 0.18) if shards else 1.0
    values = jax.random.normal(key, dims, jnp.float32) * deviation * gain
    return jnp.minimum(jnp.maximum(values, -most), most).astype(kind)


def setup_inputs(seed: int = 0) -> dict:
    streams_of = jax.random.split(jax.random.key(seed), 5)
    return {
        "sep_block": draw_sep_block(jax.random.fold_in(streams_of[4], 71), 0),
        "own_couple": gaussian(streams_of[1], (PARTS_SIZE, BLOCK, BLOCK), (BLOCK * 100 // 169) ** -0.5, 0.1875, ((0, 8), (1, 4))),
        "prev_couple": gaussian(streams_of[2], (PARTS_SIZE, BLOCK, BLOCK), (BLOCK * 100 // 169) ** -0.5, 0.1875, ((0, 8), (1, 4))),
        "inner_diag": jnp.clip(jnp.exp(math.log(4.0) - 2.0794415 * jax.random.uniform(streams_of[3], (PARTS_SIZE, BLOCK), jnp.float32) ** block_scale(streams_of[3], (PARTS_SIZE, BLOCK), ((0, 8),), -0.2, 0.2)), 0.5, 4.0),
    }


def scaled_by(matrix, factors):
    return (matrix.astype(jnp.float32) * factors.astype(jnp.float32)[None, :]).astype(jnp.bfloat16)


def outer_form(left_side, right_side):
    return jnp.dot(left_side, right_side.T, preferred_element_type=jnp.float32)


def local_step(partition_item):
    separator, own_rows, prev_rows, pivot_diag = partition_item
    reciprocal = 1.0 / pivot_diag
    own_scaled = scaled_by(own_rows, reciprocal)
    prev_scaled = scaled_by(prev_rows, reciprocal)
    own_form = outer_form(own_scaled, own_rows)
    prev_form = outer_form(prev_scaled, prev_rows)
    coupling = (-outer_form(prev_scaled, own_rows)).astype(jnp.bfloat16)
    return separator - own_form, prev_form, coupling


def reduce_level(schur, link, distance):
    partitions = schur.shape[0]
    pivot_count = partitions // (2 * distance)
    pivots = (jnp.arange(pivot_count) * (2 * distance) + distance - 1).astype(jnp.int32)

    def eliminate(pivot):
        schur_block = lax.dynamic_index_in_dim(schur, pivot, 0, keepdims=False)
        first_link = lax.dynamic_index_in_dim(link, pivot, 0, keepdims=False)
        later = (pivot + distance).astype(jnp.int32)
        later_link = lax.dynamic_index_in_dim(link, later, 0, keepdims=False)
        pivot_scale = (1.0 / jnp.maximum(jnp.diagonal(schur_block), 1.0)).astype(jnp.bfloat16)
        first_scaled = scaled_by(first_link, pivot_scale)
        second_scaled = scaled_by(later_link.T, pivot_scale)
        left_form = jnp.dot(first_scaled, first_link.T, preferred_element_type=jnp.float32)
        right_form = jnp.dot(second_scaled, later_link, preferred_element_type=jnp.float32)
        fill_link = (-jnp.dot(first_scaled, later_link, preferred_element_type=jnp.float32)).astype(jnp.bfloat16)
        return left_form, right_form, fill_link

    left_forms, right_forms, fill_links = lax.map(eliminate, pivots)
    receivers = (pivots + distance).astype(jnp.int32)
    left_after = jnp.concatenate([left_forms[1:], jnp.zeros_like(left_forms[:1])], axis=0)
    updated = (schur[receivers] - left_after) - right_forms
    schur = schur.at[receivers].set(updated)
    link = link.at[receivers].set(fill_links)
    return schur, link


def reference(sep_block, own_couple, prev_couple, inner_diag):
    partial_schur, prev_forms, link = lax.map(local_step, (sep_block, own_couple, prev_couple, inner_diag))
    link = link.at[0].set(jnp.zeros_like(link[0]))
    incoming = jnp.concatenate([prev_forms[1:], jnp.zeros_like(prev_forms[:1])], axis=0)
    schur = partial_schur - incoming
    schur, link = reduce_level(schur, link, 1)
    schur, link = reduce_level(schur, link, 2)
    return schur, link
```

```python
import jax
import jax.numpy as jnp
from jax import lax
from jax.sharding import PartitionSpec as P

BF16 = jnp.bfloat16
F32 = jnp.float32


def scaled_by(matrix, factors):
    return (matrix.astype(F32) * factors.astype(F32)[None, :]).astype(BF16)


def row_scaled_by(matrix, factors):
    return (matrix.astype(F32) * factors.astype(F32)[:, None]).astype(BF16)


def dot_nt(left, right):
    return lax.dot_general(left, right, (((1,), (1,)), ((), ())), preferred_element_type=F32)


def dot_nn(left, right):
    return lax.dot_general(left, right, (((1,), (0,)), ((), ())), preferred_element_type=F32)


def dot_tn(left, right):
    return lax.dot_general(left, right, (((0,), (0,)), ((), ())), preferred_element_type=F32)


def line_gather(blocks, axis):
    size = lax.axis_size(axis)
    place = lax.axis_index(axis)
    ahead, back = list(blocks), list(blocks)
    from_before, from_after = {}, {}
    for step in range(1, size):
        up = [(j, j + 1) for j in range(step - 1, size - 1)]
        down = [(j, j - 1) for j in range(1, size - step + 1)]
        for which in range(len(blocks)):
            ahead[which] = lax.ppermute(ahead[which], axis, up)
            back[which] = lax.ppermute(back[which], axis, down)
        from_before[step] = list(ahead)
        from_after[step] = list(back)
    gathered = []
    for which, block in enumerate(blocks):
        rows = block.shape[0]
        whole = jnp.zeros((size * rows,) + block.shape[1:], block.dtype)
        whole = lax.dynamic_update_slice_in_dim(whole, block, place * rows, 0)
        for step in range(1, size):
            piece = jnp.where(
                place >= step, from_before[step][which], from_after[size - step][which]
            )
            at = (place + size - step) % size
            whole = lax.dynamic_update_slice_in_dim(whole, piece, at * rows, 0)
        gathered.append(whole)
    return gathered


def on_device(sep_block, own_couple, prev_couple, inner_diag):
    separator = sep_block[0]
    own_rows = own_couple[0]
    prev_rows = prev_couple[0]
    reciprocal = 1.0 / inner_diag[0]
    rows, order = own_rows.shape
    row_start = lax.axis_index("space") * rows
    partition = lax.axis_index("tm")
    parts = lax.axis_size("tm")

    def level_route(distance, sign):
        pivots = range(distance - 1, parts, 2 * distance)
        route = [(p, p + sign * distance) for p in pivots]
        return [(a, b) for a, b in route if 0 <= b < parts]

    own_full, prev_full = line_gather([own_rows, prev_rows], "space")

    own_scaled = scaled_by(own_rows, reciprocal)
    prev_scaled = scaled_by(prev_rows, reciprocal)
    own_diag = jnp.sum(own_scaled.astype(F32) * own_rows.astype(F32), axis=1)
    prev_diag = jnp.sum(prev_scaled.astype(F32) * prev_rows.astype(F32), axis=1)
    row_ids = lax.broadcasted_iota(jnp.int32, separator.shape, 0) + row_start
    col_ids = lax.broadcasted_iota(jnp.int32, separator.shape, 1)
    sep_diag = jnp.sum(jnp.where(row_ids == col_ids, separator, 0.0), axis=1)
    earlier = [(p, p - 1) for p in range(1, parts)]
    diag_rows = sep_diag - own_diag - lax.ppermute(prev_diag, "tm", earlier)
    (diag,) = line_gather([diag_rows], "space")

    link = (-dot_nt(scaled_by(prev_full, reciprocal), own_full)).astype(BF16)
    link = jnp.where(partition == 0, jnp.zeros_like(link), link)
    link_rows = lax.dynamic_slice_in_dim(link, row_start, rows, 0)

    own_form = dot_nt(own_scaled, own_full)
    prev_form = dot_nt(prev_scaled, prev_full)

    scale = (1.0 / jnp.maximum(diag, 1.0)).astype(BF16)
    pivot_link, pivot_scale = lax.ppermute((link, scale), "tm", level_route(1, 1))
    next_link = (-dot_nn(scaled_by(pivot_link, pivot_scale), link)).astype(BF16)
    left_form = dot_nt(scaled_by(link_rows, scale), link)
    left_diag = jnp.sum(scaled_by(link, scale).astype(F32) * link.astype(F32), axis=1)
    link_cols = lax.dynamic_slice_in_dim(link, row_start, rows, 1)
    right_form = dot_tn(row_scaled_by(link_cols, pivot_scale), link)
    right_diag = jnp.sum(row_scaled_by(link, pivot_scale).astype(F32) * link.astype(F32), axis=0)
    is_pivot = partition % 2 == 0
    is_receiver = partition % 2 == 1
    to_earlier = jnp.where(is_pivot, prev_form + left_form, prev_form).astype(BF16)
    from_later = lax.ppermute(to_earlier, "tm", earlier)
    schur = separator - own_form - from_later.astype(F32)
    schur = jnp.where(is_receiver, schur - right_form, schur)
    diag = diag - lax.ppermute(left_diag, "tm", level_route(1, -1)) - right_diag
    next_rows = lax.dynamic_slice_in_dim(next_link, row_start, rows, 0)
    out_link = jnp.where(is_receiver, next_rows, link_rows)

    scale = (1.0 / jnp.maximum(diag, 1.0)).astype(BF16)
    pivot_rows, pivot_scale = lax.ppermute((next_rows, scale), "tm", level_route(2, 1))
    left_form = dot_nt(scaled_by(next_rows, scale), next_link).astype(BF16)
    from_later = lax.ppermute(left_form, "tm", level_route(2, -1))
    next_cols = lax.dynamic_slice_in_dim(next_link, row_start, rows, 1)
    right_form = dot_tn(row_scaled_by(next_cols, pivot_scale), next_link)
    last_rows = (-dot_nn(scaled_by(pivot_rows, pivot_scale), next_link)).astype(BF16)
    is_receiver = partition % 4 == 3
    schur = jnp.where(is_receiver, schur - from_later.astype(F32) - right_form, schur)
    out_link = jnp.where(is_receiver, last_rows, out_link)
    return (schur[None], out_link[None])


def solution(mesh):
    placed = (P("tm", "space", None), P("tm", "space", None), P("tm", "space", None), P("tm", None))
    return jax.shard_map(
        on_device,
        mesh=mesh,
        in_specs=placed,
        out_specs=(P("tm", "space", None), P("tm", "space", None)),
        check_vma=False,
    )
```

```python
import jax
import jax.numpy as jnp
from jax import lax
from jax.sharding import PartitionSpec as P

BF16 = jnp.bfloat16
F32 = jnp.float32


def scaled_by(matrix, factors):
    return (matrix.astype(F32) * factors.astype(F32)[None, :]).astype(BF16)


def row_scaled_by(matrix, factors):
    return (matrix.astype(F32) * factors.astype(F32)[:, None]).astype(BF16)


def dot_nt(left, right):
    return lax.dot_general(left, right, (((1,), (1,)), ((), ())), preferred_element_type=F32)


def dot_nn(left, right):
    return lax.dot_general(left, right, (((1,), (0,)), ((), ())), preferred_element_type=F32)


def dot_tn(left, right):
    return lax.dot_general(left, right, (((0,), (0,)), ((), ())), preferred_element_type=F32)


def on_device(sep_block, own_couple, prev_couple, inner_diag):
    separator = sep_block[0]
    own_rows = own_couple[0]
    prev_rows = prev_couple[0]
    reciprocal = 1.0 / inner_diag[0]
    rows, order = own_rows.shape
    place = lax.axis_index("space")
    size = lax.axis_size("space")
    middle = size // 2
    half = middle * rows
    early = order - rows
    on_right = place >= middle
    partition = lax.axis_index("tm")
    parts = lax.axis_size("tm")

    inward = [(j, j + 1) for j in range(middle - 1)]
    inward += [(j, j - 1) for j in range(middle + 1, size)]
    across = [(middle - 1, middle), (middle, middle - 1)]

    def pulled_in(block):
        mine = [block]
        for _ in range(middle - 1):
            mine.append(lax.ppermute(mine[-1], "space", inward))
        theirs = [lax.ppermute(piece, "space", across) for piece in mine]
        return mine, theirs

    def pushed_out(block, parity, period):
        shape = block.shape[:-2] + (rows, block.shape[-1])
        result = jnp.zeros(shape, block.dtype)
        for away in range(1, middle):
            route = []
            for p in range(parity, parts, period):
                route.append((p * size + middle - 1, p * size + middle - 1 - away))
                route.append((p * size + middle, p * size + middle + away))
            piece = block[..., half - (away + 1) * rows : half - away * rows, :]
            result = result + lax.ppermute(piece, ("tm", "space"), route)
        return result

    def between(block, route):
        return lax.ppermute(block, "tm", [(a, b) for a, b in route if 0 <= b < parts])

    even = range(0, parts, 2)
    odd = range(1, parts, 2)
    pivots = range(1, parts, 4)

    own_mine, own_theirs = pulled_in(own_rows)
    prev_mine, prev_theirs = pulled_in(prev_rows)
    own_early = jnp.concatenate(own_mine[::-1] + own_theirs[:-1])
    prev_early = jnp.concatenate(prev_mine[::-1] + prev_theirs[:-1])
    own_late, prev_late = own_theirs[-1], prev_theirs[-1]

    own_sum = jnp.sum(scaled_by(own_rows, reciprocal).astype(F32) * own_rows.astype(F32), axis=1)
    prev_sum = jnp.sum(scaled_by(prev_rows, reciprocal).astype(F32) * prev_rows.astype(F32), axis=1)
    row_ids = lax.broadcasted_iota(jnp.int32, separator.shape, 0) + place * rows
    col_ids = lax.broadcasted_iota(jnp.int32, separator.shape, 1)
    sep_diag = jnp.sum(jnp.where(row_ids == col_ids, separator, 0.0), axis=1)
    diag_rows = sep_diag - own_sum - between(prev_sum, [(p, p - 1) for p in range(parts)])
    diag_mine, diag_theirs = pulled_in(diag_rows)
    diag = jnp.concatenate(diag_mine[::-1] + diag_theirs)
    scale = (1.0 / jnp.maximum(diag, 1.0)).astype(BF16)
    pivot_scale = between(scale, [(p, p + 1) for p in even])

    is_even = partition % 2 == 0
    is_first = partition == 0

    own_scaled = scaled_by(jnp.concatenate([own_early, own_late]), reciprocal)
    prev_scaled = scaled_by(prev_early[:half], reciprocal)
    own_form_early = dot_nt(own_scaled[:half], own_early)
    prev_form_early = dot_nt(prev_scaled, prev_early)
    link_top = (-dot_nt(prev_early, own_scaled)).astype(BF16)
    link_top = jnp.where(is_first, jnp.zeros_like(link_top), link_top)
    first_top = scaled_by(link_top, scale)
    pivot_top = between(first_top, [(p, p + 1) for p in even])

    from_odd_early = between(prev_form_early.astype(BF16), [(p, p - 1) for p in odd])
    left_early = dot_nt(first_top[:half], link_top)
    from_even_early = between((prev_form_early + left_early).astype(BF16), [(p, p - 1) for p in even])
    even_form_early = own_form_early + from_odd_early.astype(F32)
    even_out_early = pushed_out(even_form_early.astype(BF16), 0, 2)
    even_link_early = pushed_out(link_top[:half, :early], 0, 2)
    next_top_part = dot_nn(pivot_top[:, :early], link_top)

    link_last = (-dot_nt(prev_late, own_scaled)).astype(BF16)
    link_last = jnp.where(is_first, jnp.zeros_like(link_last), link_last)
    first_last = scaled_by(link_last, scale)
    pivot_last = between(first_last, [(p, p + 1) for p in even])
    left_diag = jnp.concatenate(
        [
            jnp.sum(first_top.astype(F32) * link_top.astype(F32), axis=1),
            jnp.sum(first_last.astype(F32) * link_last.astype(F32), axis=1),
        ]
    )
    later_diag = between(left_diag, [(p, p - 1) for p in even])
    own_form_late = dot_nt(own_scaled[:half], own_late)
    prev_form_late = dot_nt(prev_scaled, prev_late)
    left_late = dot_nt(first_top[:half], link_last)
    to_earlier = jnp.where(is_even, prev_form_late + left_late, prev_form_late).astype(BF16)
    later_late = between(to_earlier, [(p, p - 1) for p in range(parts)])
    even_form_late = own_form_late + later_late.astype(F32)
    even_late = jnp.stack([even_form_late.astype(BF16), link_top[:half, early:]])
    even_out_late = pushed_out(even_late, 0, 2)

    next_top = (-(next_top_part + dot_nn(pivot_top[:, early:], link_last))).astype(BF16)
    next_last = (-(dot_nn(pivot_last[:, :early], link_top) + dot_nn(pivot_last[:, early:], link_last))).astype(BF16)
    second_top = row_scaled_by(link_top[:, :half], pivot_scale[:early])
    second_last = row_scaled_by(link_last[:, :half], pivot_scale[early:])
    right_form = dot_tn(second_top, link_top) + dot_tn(second_last, link_last)
    right_diag = jnp.sum(row_scaled_by(link_top, pivot_scale[:early]).astype(F32) * link_top.astype(F32), axis=0)
    right_diag += jnp.sum(row_scaled_by(link_last, pivot_scale[early:]).astype(F32) * link_last.astype(F32), axis=0)
    odd_form = jnp.concatenate([own_form_early + from_even_early.astype(F32), own_form_late + later_late.astype(F32)], axis=1)
    odd_form = odd_form + right_form
    diag = diag - later_diag - right_diag
    odd_out = pushed_out(jnp.stack([odd_form.astype(BF16), next_top[:half]]), 1, 4)

    scale = (1.0 / jnp.maximum(diag, 1.0)).astype(BF16)
    pivot_rows = between(next_top[:half], [(p, p + 2) for p in pivots if p != 1])
    pivot_scale = between(scale, [(p, p + 2) for p in pivots])
    first_scaled = scaled_by(next_top[:half], scale)
    left_form = jnp.concatenate([dot_nt(first_scaled, next_top), dot_nt(first_scaled, next_last)], axis=1)
    from_later = between(left_form.astype(BF16), [(p, p - 2) for p in pivots])
    pivot_scaled = scaled_by(pivot_rows, pivot_scale)
    last_link = (-(dot_nn(pivot_scaled[:, :early], next_top) + dot_nn(pivot_scaled[:, early:], next_last))).astype(BF16)
    second_top = row_scaled_by(next_top[:, :half], pivot_scale[:early])
    second_last = row_scaled_by(next_last[:, :half], pivot_scale[early:])
    last_form = odd_form + from_later.astype(F32) + dot_tn(second_top, next_top) + dot_tn(second_last, next_last)
    last_out = pushed_out(jnp.stack([last_form.astype(BF16), last_link]), 3, 4)

    is_middle = jnp.logical_or(place == middle - 1, place == middle)
    is_last = partition % 4 == 3
    home = half - rows
    even_form = jnp.concatenate([even_form_early, even_form_late], axis=1)[home:]
    form = jnp.where(is_even, even_form, jnp.where(is_last, last_form[home:], odd_form[home:]))
    link = jnp.where(is_even, link_top[home:half], jnp.where(is_last, last_link[home:], next_top[home:half]))
    form_in = jnp.concatenate([even_out_early, even_out_late[0]], axis=1) + odd_out[0] + last_out[0]
    link_in = jnp.concatenate([even_link_early, even_out_late[1]], axis=1) + odd_out[1] + last_out[1]
    form = jnp.where(is_middle, form, form_in.astype(F32))
    link = jnp.where(is_middle, link, link_in)

    def in_order(block):
        pieces = [block[:, j * rows : (j + 1) * rows] for j in range(size)]
        return jnp.where(on_right, jnp.concatenate(pieces[::-1], axis=1), block)

    return ((separator - in_order(form))[None], in_order(link)[None])


def solution(mesh):
    placed = (P("tm", "space", None), P("tm", "space", None), P("tm", "space", None), P("tm", None))
    return jax.shard_map(
        on_device,
        mesh=mesh,
        in_specs=placed,
        out_specs=(P("tm", "space", None), P("tm", "space", None)),
        check_vma=False,
    )
```

```python
import functools

import jax
import jax.numpy as jnp
from jax import lax
from jax.experimental import pallas as pl
from jax.experimental.pallas import tpu as pltpu
from jax.sharding import PartitionSpec as P

BF16 = jnp.bfloat16
F32 = jnp.float32
EXTRA = 16
VMEM_LIMIT = 56 * 1024 * 1024

ANY = pl.BlockSpec(memory_space=pl.ANY)


def scaled_by(matrix, factors):
    return (matrix.astype(F32) * factors.astype(F32)[None, :]).astype(BF16)


def row_scaled_by(matrix, factors):
    return (matrix.astype(F32) * factors.astype(F32)[:, None]).astype(BF16)


def dot_nt(left, right):
    return lax.dot_general(left, right, (((1,), (1,)), ((), ())), preferred_element_type=F32)


def dot_nn(left, right):
    return lax.dot_general(left, right, (((1,), (0,)), ((), ())), preferred_element_type=F32)


def dot_tn(left, right):
    return lax.dot_general(left, right, (((0,), (0,)), ((), ())), preferred_element_type=F32)


def after(block, *others):
    def body(*refs):
        del refs

    return pl.pallas_call(
        body,
        out_shape=jax.ShapeDtypeStruct(block.shape, block.dtype),
        in_specs=[ANY] * (1 + len(others)),
        out_specs=ANY,
        input_output_aliases={0: 0},
    )(block, *others)


def last_rows_kernel(
    flags, p_last, a_scaled, p_half, first_half, scale, *refs
):
    link, first, update, diag = refs[-4:]
    step = pl.program_id(0)
    width = a_scaled.shape[0]
    at = pl.multiple_of(step * width, width)
    columns = pl.ds(at, width)
    part = -dot_nt(p_last[...], a_scaled[...])
    part = jnp.where(flags[1] == 1, jnp.zeros_like(part), part).astype(BF16)
    link[:, columns] = part
    first[:, columns] = (part.astype(F32) * scale[0:1, columns].astype(F32)).astype(BF16)

    @pl.when(step == pl.num_programs(0) - 1)
    def _():
        whole = link[...]
        forms = dot_nt(p_half[...], p_last[...])
        keep = jnp.where(flags[0] == 1, 1.0, 0.0)
        left = dot_nt(first_half[...], whole)
        update[...] = (forms + left * keep).astype(BF16)
        diag[...] = dot_nt(scale[...], whole * whole)


def last_rows(flags, p_last, a_scaled, p_half, first_half, scale8, *wait_for):
    rows, order = p_last.shape
    half = p_half.shape[0]
    width = 512 if order % 512 == 0 else 256
    whole = lambda shape: pl.BlockSpec(shape, lambda j, f: (0, 0))
    return pl.pallas_call(
        last_rows_kernel,
        out_shape=[
            jax.ShapeDtypeStruct((rows, order), BF16),
            jax.ShapeDtypeStruct((rows, order), BF16),
            jax.ShapeDtypeStruct((half, rows), BF16),
            jax.ShapeDtypeStruct((8, rows), F32),
        ],
        grid_spec=pltpu.PrefetchScalarGridSpec(
            num_scalar_prefetch=1,
            grid=(order // width,),
            in_specs=[
                whole((rows, order)),
                pl.BlockSpec((width, order), lambda j, f: (j, 0)),
                whole((half, order)),
                whole((half, order)),
                whole((8, order)),
            ]
            + [ANY] * len(wait_for),
            out_specs=[whole((rows, order)), whole((rows, order)), whole((half, rows)), whole((8, rows))],
        ),
        compiler_params=pltpu.CompilerParams(vmem_limit_bytes=VMEM_LIMIT),
        cost_estimate=pl.CostEstimate(
            flops=2 * rows * order * (order + 2 * half), bytes_accessed=2 * order * (order + 4 * rows + 2 * half), transcendentals=0
        ),
    )(flags, p_last, a_scaled, p_half, first_half, scale8, *wait_for)


def next_link_kernel(count, pivot, scale, top, bottom, *refs):
    new, diag, whole, sems = refs[-4:]
    split = top.shape[0]

    @pl.when(pl.program_id(0) == 0)
    def _():
        copies = [
            pltpu.make_async_copy(top, whole.at[pl.ds(0, split)], sems.at[0]),
            pltpu.make_async_copy(bottom, whole.at[pl.ds(split, bottom.shape[0])], sems.at[1]),
        ]
        for copy in copies:
            copy.start()
        for copy in copies:
            copy.wait()
        if count:
            link = whole[...]
            diag[...] = dot_nn(scale[...], link * link)
        else:
            diag[...] = jnp.zeros_like(diag)

    new[...] = (-dot_nn(pivot[...], whole[...])).astype(BF16)


def next_link(count, pivot, scale8, top, bottom, *wait_for):
    rows, order = pivot.shape
    block = bottom.shape[0]
    return pl.pallas_call(
        functools.partial(next_link_kernel, count),
        out_shape=[
            jax.ShapeDtypeStruct((rows, order), BF16),
            jax.ShapeDtypeStruct((8, order), F32),
        ],
        grid=(rows // block,),
        in_specs=[
            pl.BlockSpec((block, order), lambda i: (i, 0)),
            pl.BlockSpec((8, order), lambda i: (0, 0)),
            ANY,
            ANY,
        ]
        + [ANY] * len(wait_for),
        out_specs=[
            pl.BlockSpec((block, order), lambda i: (i, 0)),
            pl.BlockSpec((8, order), lambda i: (0, 0)),
        ],
        scratch_shapes=[pltpu.VMEM((order, order), BF16), pltpu.SemaphoreType.DMA((2,))],
        compiler_params=pltpu.CompilerParams(vmem_limit_bytes=VMEM_LIMIT),
        cost_estimate=pl.CostEstimate(
            flops=2 * rows * order * order, bytes_accessed=2 * order * (order + 2 * rows), transcendentals=0
        ),
    )(pivot, scale8, top, bottom, *wait_for)


def on_device(sep_block, own_couple, prev_couple, inner_diag):
    separator = sep_block[0]
    own_rows = own_couple[0]
    prev_rows = prev_couple[0]
    reciprocal = 1.0 / inner_diag[0]
    rows, order = own_rows.shape
    place = lax.axis_index("space")
    size = lax.axis_size("space")
    middle = size // 2
    half = middle * rows
    early = order - rows
    home = half - rows
    on_right = place >= middle
    partition = lax.axis_index("tm")
    parts = lax.axis_size("tm")

    inward = [(j, j + 1) for j in range(middle - 1)]
    inward += [(j, j - 1) for j in range(middle + 1, size)]
    across = [(middle - 1, middle), (middle, middle - 1)]

    def gathered(block):
        mine = [block]
        for _ in range(middle - 1):
            mine.append(lax.ppermute(mine[-1], "space", inward))
        return mine

    def crossed(block):
        return lax.ppermute(block, "space", across)

    def pushed_out(block, parity, period):
        result = jnp.zeros((rows, block.shape[-1]), block.dtype)
        for away in range(1, middle):
            route = []
            for p in range(parity, parts, period):
                route.append((p * size + middle - 1, p * size + middle - 1 - away))
                route.append((p * size + middle, p * size + middle + away))
            piece = block[home - away * rows : half - away * rows]
            result = result + lax.ppermute(piece, ("tm", "space"), route)
        return result

    def between(block, route):
        return lax.ppermute(block, "tm", [(a, b) for a, b in route if 0 <= b < parts])

    even = range(0, parts, 2)
    odd = range(1, parts, 2)
    pivots = range(1, parts, 4)
    is_even = partition % 2 == 0
    is_first = partition == 0
    is_last = partition % 4 == 3
    flags = jnp.stack([is_even, is_first]).astype(jnp.int32)

    prev_mine = gathered(prev_rows)
    prev_theirs = [crossed(block) for block in prev_mine[:-1]]

    own_sum = jnp.sum(scaled_by(own_rows, reciprocal).astype(F32) * own_rows.astype(F32), axis=1)
    prev_sum = jnp.sum(scaled_by(prev_rows, reciprocal).astype(F32) * prev_rows.astype(F32), axis=1)
    row_ids = lax.broadcasted_iota(jnp.int32, separator.shape, 0) + place * rows
    col_ids = lax.broadcasted_iota(jnp.int32, separator.shape, 1)
    sep_diag = jnp.sum(jnp.where(row_ids == col_ids, separator, 0.0), axis=1)
    diag_rows = sep_diag - own_sum - between(prev_sum, [(p, p - 1) for p in range(parts)])
    high = lax.reduce_precision(diag_rows, 8, 7)
    words = jnp.stack([high, diag_rows - high]).astype(BF16)
    own_long = jnp.concatenate([own_rows, jnp.pad(words, ((0, EXTRA - 2), (0, order - rows)))])
    own_mine = gathered(own_long)
    own_theirs = [crossed(block) for block in own_mine]
    prev_mine[-1] = after(prev_mine[-1], own_mine[-1])
    prev_late = crossed(prev_mine[-1])

    own_all = jnp.concatenate([block[:rows] for block in own_mine[::-1] + own_theirs])
    own_early = jnp.concatenate([block[:rows] for block in own_mine[::-1] + own_theirs[:-1]])
    prev_early = jnp.concatenate(prev_mine[::-1] + prev_theirs)
    diag = jnp.concatenate(
        [
            block[rows, :rows].astype(F32) + block[rows + 1, :rows].astype(F32)
            for block in own_mine[::-1] + own_theirs
        ]
    )
    scale = (1.0 / jnp.maximum(diag, 1.0)).astype(BF16)
    scale8 = jnp.broadcast_to(scale[None, :], (8, order))
    pivot_scale = between(scale, [(p, p + 1) for p in even])
    pivot_scale8 = jnp.broadcast_to(pivot_scale[None, :], (8, order))

    prev_scaled = scaled_by(prev_early[:half], reciprocal)
    prev_form_early = dot_nt(prev_scaled, prev_early)
    from_odd_early = between(prev_form_early.astype(BF16), [(p, p - 1) for p in odd])
    own_half = scaled_by(own_early[:half], reciprocal)
    own_form_early = dot_nt(own_half, own_early)
    even_form_early = own_form_early + from_odd_early.astype(F32)
    even_out_early = pushed_out(even_form_early.astype(BF16), 0, 2)

    own_scaled = scaled_by(own_all, reciprocal)
    link_top = (-dot_nt(prev_early, own_scaled)).astype(BF16)
    link_top = jnp.where(is_first, jnp.zeros_like(link_top), link_top)
    even_link = pushed_out(link_top, 0, 2)
    first_top = scaled_by(link_top, scale)
    pivot_top = between(first_top, [(p, p + 1) for p in even])
    left_diag_top = between(dot_nt(scale8, link_top * link_top), [(p, p - 1) for p in even])
    left_early = dot_nt(first_top[:half], link_top)
    from_even_early = between((prev_form_early + left_early).astype(BF16), [(p, p - 1) for p in even])
    own_form_late = dot_nt(own_half, own_all[early:])

    link_last, first_last, to_earlier, left_diag_last = last_rows(
        flags, prev_late, own_scaled, prev_scaled, first_top[:half], scale8,
        pivot_top, left_diag_top, even_out_early,
    )
    pivot_last = between(first_last, [(p, p + 1) for p in even])
    later_late = between(to_earlier, [(p, p - 1) for p in range(parts)])
    later_diag_last = between(left_diag_last, [(p, p - 1) for p in even])

    next_top, right_diag = next_link(True, pivot_top, pivot_scale8, link_top, link_last, even_link)
    senders = [(p, p + 2) for p in pivots if p != 1]
    pivot_rows = [between(next_top[j * rows : (j + 1) * rows], senders) for j in range(middle)]
    next_last, _ = next_link(
        False, pivot_last, pivot_scale8, link_top, link_last, from_even_early, later_diag_last
    )
    odd_link = pushed_out(next_top, 1, 4)
    later_diag = jnp.concatenate([left_diag_top[0], later_diag_last[0]])
    diag = diag - later_diag - right_diag[0]

    scale = (1.0 / jnp.maximum(diag, 1.0)).astype(BF16)
    pivot_scale2 = between(scale, [(p, p + 2) for p in pivots])
    next_whole = jnp.concatenate([next_top, next_last])
    left_form = dot_nt(scaled_by(next_top[:half], scale), next_whole).astype(BF16)
    left_out = pushed_out(left_form, 1, 4)
    left_out = between(left_out, [(p, p - 2) for p in pivots])
    left_home = between(left_form[home:], [(p, p - 2) for p in pivots])

    link_whole = jnp.concatenate([link_top, link_last])
    right_form = dot_tn(row_scaled_by(link_whole[:, :half], pivot_scale), link_whole)
    later = jnp.concatenate([from_even_early, later_late], axis=1).astype(F32)
    own_form = jnp.concatenate([own_form_early, own_form_late], axis=1)
    odd_form = own_form + later + right_form
    odd_out = pushed_out(odd_form.astype(BF16), 1, 4)

    last_form = odd_form + dot_tn(row_scaled_by(next_whole[:, :half], pivot_scale2), next_whole)
    last_out = pushed_out(last_form.astype(BF16), 3, 4)
    last_link = [
        (-dot_nn(scaled_by(block, pivot_scale2), next_whole)).astype(BF16) for block in pivot_rows
    ]
    last_link_out = jnp.zeros_like(last_link[0])
    for away in range(1, middle):
        route = []
        for p in range(3, parts, 4):
            route.append((p * size + middle - 1, p * size + middle - 1 - away))
            route.append((p * size + middle, p * size + middle + away))
        last_link_out += lax.ppermute(last_link[middle - 1 - away], ("tm", "space"), route)

    even_late = own_form_late + later_late.astype(F32)
    even_out_late = pushed_out(even_late.astype(BF16), 0, 2)
    is_middle = jnp.logical_or(place == middle - 1, place == middle)
    even_form = jnp.concatenate([even_form_early, even_late], axis=1)[home:]
    last_home = last_form[home:] + left_home.astype(F32)
    form = jnp.where(is_even, even_form, jnp.where(is_last, last_home, odd_form[home:]))
    link = jnp.where(is_even, link_top[home:half], jnp.where(is_last, last_link[-1], next_top[home:half]))
    form_in = jnp.concatenate([even_out_early, even_out_late], axis=1) + odd_out + last_out
    form_in = form_in.astype(F32) + left_out.astype(F32)
    link_in = even_link + odd_link + last_link_out
    form = jnp.where(is_middle, form, form_in)
    link = jnp.where(is_middle, link, link_in)

    def in_order(block):
        pieces = [block[:, j * rows : (j + 1) * rows] for j in range(size)]
        return jnp.where(on_right, jnp.concatenate(pieces[::-1], axis=1), block)

    return ((separator - in_order(form))[None], in_order(link)[None])


def solution(mesh):
    placed = (P("tm", "space", None), P("tm", "space", None), P("tm", "space", None), P("tm", None))
    return jax.shard_map(
        on_device,
        mesh=mesh,
        in_specs=placed,
        out_specs=(P("tm", "space", None), P("tm", "space", None)),
        check_vma=False,
    )
```

```python
import jax
import jax.numpy as jnp
from jax import lax
from jax.sharding import PartitionSpec as P

BF16 = jnp.bfloat16
F32 = jnp.float32
EXTRA = 16


def scaled_by(matrix, factors):
    return (matrix.astype(F32) * factors.astype(F32)[None, :]).astype(BF16)


def row_scaled_by(matrix, factors):
    return (matrix.astype(F32) * factors.astype(F32)[:, None]).astype(BF16)


def dot_nt(left, right):
    return lax.dot_general(left, right, (((1,), (1,)), ((), ())), preferred_element_type=F32)


def dot_nn(left, right):
    return lax.dot_general(left, right, (((1,), (0,)), ((), ())), preferred_element_type=F32)


def dot_tn(left, right):
    return lax.dot_general(left, right, (((0,), (0,)), ((), ())), preferred_element_type=F32)


def rows_of(scale):
    return jnp.broadcast_to(scale[None, :], (8, scale.shape[0]))


def on_device(sep_block, own_couple, prev_couple, inner_diag):
    separator = sep_block[0]
    own_rows = own_couple[0]
    prev_rows = prev_couple[0]
    reciprocal = 1.0 / inner_diag[0]
    rows, order = own_rows.shape
    place = lax.axis_index("space")
    size = lax.axis_size("space")
    row_start = place * rows
    partition = lax.axis_index("tm")
    parts = lax.axis_size("tm")

    def between(block, route):
        return lax.ppermute(block, "tm", [(a, b) for a, b in route if 0 <= b < parts])

    even = range(0, parts, 2)
    pivots = range(1, parts, 4)
    everyone = range(parts)

    def one_step(ahead, back, step):
        up = [(j, j + 1) for j in range(step - 1, size - 1)]
        down = [(j, j - 1) for j in range(1, size - step + 1)]
        return lax.ppermute(ahead, "space", up), lax.ppermute(back, "space", down)

    def block_at(arrived, spot):
        block = arrived[0][0]
        for step in range(1, size):
            if spot + step < size:
                block = jnp.where(place == spot + step, arrived[step][0], block)
            if spot - step >= 0:
                block = jnp.where(place == spot - step, arrived[step][1], block)
        return block

    own_arrived = [(own_rows, own_rows)]
    own_arrived.append(one_step(own_rows, own_rows, 1))

    own_scaled = scaled_by(own_rows, reciprocal)
    prev_scaled = scaled_by(prev_rows, reciprocal)
    own_sum = jnp.sum(own_scaled.astype(F32) * own_rows.astype(F32), axis=1)
    prev_sum = jnp.sum(prev_scaled.astype(F32) * prev_rows.astype(F32), axis=1)
    row_ids = lax.broadcasted_iota(jnp.int32, separator.shape, 0) + row_start
    col_ids = lax.broadcasted_iota(jnp.int32, separator.shape, 1)
    sep_diag = jnp.sum(jnp.where(row_ids == col_ids, separator, 0.0), axis=1)
    diag_rows = sep_diag - own_sum - between(prev_sum, [(p, p - 1) for p in everyone])
    high = lax.reduce_precision(diag_rows, 8, 7)
    words = jnp.stack([high, diag_rows - high]).astype(BF16)
    prev_long = jnp.concatenate([prev_rows, jnp.pad(words, ((0, EXTRA - 2), (0, order - rows)))])
    prev_arrived = [(prev_long, prev_long)]
    prev_arrived.append(one_step(prev_long, prev_long, 1))
    for step in range(2, size):
        own_arrived.append(one_step(*own_arrived[-1], step))
        prev_arrived.append(one_step(*prev_arrived[-1], step))

    own_full = jnp.concatenate([block_at(own_arrived, spot) for spot in range(size)])

    left_side = place < size // 2
    late = jnp.where(left_side, size - 1, 0)
    late_start = late * rows
    before = [list(pair) for pair in prev_arrived[:-1]]
    before.append([jnp.zeros_like(prev_long)] * 2)
    prev_blocks = [block_at(before, spot) for spot in range(size)]
    prev_first = jnp.concatenate([block[:rows] for block in prev_blocks])
    prev_late = jnp.where(left_side, block_at(prev_arrived, size - 1), block_at(prev_arrived, 0))

    def diag_of(block):
        return block[rows, :rows].astype(F32) + block[rows + 1, :rows].astype(F32)

    diag = jnp.concatenate([diag_of(block) for block in prev_blocks])
    diag = lax.dynamic_update_slice_in_dim(diag, diag_of(prev_late), late_start, 0)
    prev_late = prev_late[:rows]

    is_first = partition == 0
    own_form = dot_nt(own_scaled, own_full)
    prev_form = dot_nt(prev_scaled, prev_first)
    link = (-dot_nt(scaled_by(prev_first, reciprocal), own_full)).astype(BF16)
    link = jnp.where(is_first, jnp.zeros_like(link), link)
    pivot_link = between(link, [(p, p + 1) for p in even])

    link_late = (-dot_nt(scaled_by(prev_late, reciprocal), own_full)).astype(BF16)
    link_late = jnp.where(is_first, jnp.zeros_like(link_late), link_late)
    pivot_late = between(link_late, [(p, p + 1) for p in even])
    link = lax.dynamic_update_slice_in_dim(link, link_late, late_start, 0)
    pivot_link = lax.dynamic_update_slice_in_dim(pivot_link, pivot_late, late_start, 0)
    prev_form = lax.dynamic_update_slice_in_dim(
        prev_form, dot_nt(prev_scaled, prev_late), late_start, 1
    )

    is_pivot = partition % 2 == 0
    is_receiver = partition % 2 == 1
    scale = (1.0 / jnp.maximum(diag, 1.0)).astype(BF16)
    pivot_scale = between(scale, [(p, p + 1) for p in even])
    left_diag = between(dot_nt(rows_of(scale), link * link)[0], [(p, p - 1) for p in even])
    next_link = (-dot_nn(scaled_by(pivot_link, pivot_scale), link)).astype(BF16)
    next_rows = lax.dynamic_slice_in_dim(next_link, row_start, rows, 0)
    pivot_rows = between(next_rows, [(p, p + 2) for p in pivots if p != 1])

    right_diag = dot_nn(rows_of(pivot_scale), link * link)[0]
    next_diag = diag - left_diag - right_diag
    next_scale = (1.0 / jnp.maximum(next_diag, 1.0)).astype(BF16)
    next_pivot_scale = between(next_scale, [(p, p + 2) for p in pivots])
    left_next = dot_nt(scaled_by(next_rows, next_scale), next_link).astype(BF16)
    from_pivot = between(left_next, [(p, p - 2) for p in pivots])

    link_rows = lax.dynamic_slice_in_dim(link, row_start, rows, 0)
    left_form = dot_nt(scaled_by(link_rows, scale), link)
    to_earlier = jnp.where(is_pivot, prev_form + left_form, prev_form).astype(BF16)
    from_later = between(to_earlier, [(p, p - 1) for p in everyone])
    link_cols = lax.dynamic_slice_in_dim(link, row_start, rows, 1)
    right_form = dot_tn(row_scaled_by(link_cols, pivot_scale), link)
    schur = separator - own_form - from_later.astype(F32)
    schur = jnp.where(is_receiver, schur - right_form, schur)

    is_last = partition % 4 == 3
    next_cols = lax.dynamic_slice_in_dim(next_link, row_start, rows, 1)
    right_next = dot_tn(row_scaled_by(next_cols, next_pivot_scale), next_link)
    last_rows = (-dot_nn(scaled_by(pivot_rows, next_pivot_scale), next_link)).astype(BF16)
    schur = jnp.where(is_last, schur - from_pivot.astype(F32) - right_next, schur)
    out_link = jnp.where(is_last, last_rows, jnp.where(is_receiver, next_rows, link_rows))
    return (schur[None], out_link[None])


def solution(mesh):
    placed = (P("tm", "space", None), P("tm", "space", None), P("tm", "space", None), P("tm", None))
    return jax.shard_map(
        on_device,
        mesh=mesh,
        in_specs=placed,
        out_specs=(P("tm", "space", None), P("tm", "space", None)),
        check_vma=False,
    )
```

```python
import jax
import jax.numpy as jnp
from jax import lax
from jax.experimental import pallas as pl
from jax.experimental.pallas import tpu as pltpu
from jax.sharding import PartitionSpec as P

BF16 = jnp.bfloat16
F32 = jnp.float32

ANY = pl.BlockSpec(memory_space=pl.ANY)


def after(block, *others):
    def body(*refs):
        del refs

    return pl.pallas_call(
        body,
        out_shape=jax.ShapeDtypeStruct(block.shape, block.dtype),
        in_specs=[ANY] * (1 + len(others)),
        out_specs=ANY,
        input_output_aliases={0: 0},
    )(block, *others)


def early_forms_kernel(
    flags, prev_whole, prev_rows, own_rows, own, prev, separator, scale, scale_here, pivot_scale,
    link, first, partial, form, left_diag, right_diag,
):
    part = jnp.where(flags[0] == 1, 0.0, -dot_nt(prev_whole[...], own[...])).astype(BF16)
    link[...] = part
    first[...] = (part.astype(F32) * scale_here[0:1].astype(F32)).astype(BF16)
    partial[...] = separator[...] - dot_nt(own_rows[...], own[...])
    form[...] = dot_nt(prev_rows[...], prev[...])
    square = part * part
    right_diag[...] = dot_nn(pivot_scale[...], square)

    @pl.when(pl.program_id(0) == 0)
    def _():
        left_diag[...] = jnp.zeros_like(left_diag)

    left_diag[...] += dot_nt(scale_here[...], square)


def early_forms(flags, prev_whole, prev_rows, own_rows, own, prev, separator, scale, pivot_scale):
    rows, order = own_rows.shape
    width = 256
    whole = lambda shape: pl.BlockSpec(shape, lambda j, f: (0, 0))
    down = lambda count: pl.BlockSpec((width, count), lambda j, f: (j, 0))
    along = lambda count: pl.BlockSpec((count, width), lambda j, f: (0, j))
    return pl.pallas_call(
        early_forms_kernel,
        out_shape=[
            jax.ShapeDtypeStruct((order, order), BF16),
            jax.ShapeDtypeStruct((order, order), BF16),
            jax.ShapeDtypeStruct((rows, order), F32),
            jax.ShapeDtypeStruct((rows, order), F32),
            jax.ShapeDtypeStruct((8, order), F32),
            jax.ShapeDtypeStruct((8, order), F32),
        ],
        grid_spec=pltpu.PrefetchScalarGridSpec(
            num_scalar_prefetch=1,
            grid=(order // width,),
            in_specs=[
                whole((order, order)),
                whole((rows, order)),
                whole((rows, order)),
                down(order),
                down(order),
                along(rows),
                whole((8, order)),
                along(8),
                whole((8, order)),
            ],
            out_specs=[
                along(order),
                along(order),
                along(rows),
                along(rows),
                whole((8, order)),
                along(8),
            ],
        ),
        compiler_params=pltpu.CompilerParams(vmem_limit_bytes=32 * 1024 * 1024),
        cost_estimate=pl.CostEstimate(flops=0, bytes_accessed=0, transcendentals=0),
    )(flags, prev_whole, prev_rows, own_rows, own, prev, separator, scale, scale, pivot_scale)


def scaled_by(matrix, factors):
    return (matrix.astype(F32) * factors.astype(F32)[None, :]).astype(BF16)


def row_scaled_by(matrix, factors):
    return (matrix.astype(F32) * factors.astype(F32)[:, None]).astype(BF16)


def dot_nt(left, right):
    return lax.dot_general(left, right, (((1,), (1,)), ((), ())), preferred_element_type=F32)


def dot_nn(left, right):
    return lax.dot_general(left, right, (((1,), (0,)), ((), ())), preferred_element_type=F32)


def dot_tn(left, right):
    return lax.dot_general(left, right, (((0,), (0,)), ((), ())), preferred_element_type=F32)


def rows_of(scale):
    return jnp.broadcast_to(scale[None, :], (8, scale.shape[0]))


def on_device(sep_block, own_couple, prev_couple, inner_diag):
    separator = sep_block[0]
    own_rows = own_couple[0]
    prev_rows = prev_couple[0]
    reciprocal = 1.0 / inner_diag[0]
    rows, order = own_rows.shape
    place = lax.axis_index("space")
    size = lax.axis_size("space")
    row_start = place * rows
    partition = lax.axis_index("tm")
    parts = lax.axis_size("tm")

    def between(block, route):
        return lax.ppermute(block, "tm", [(a, b) for a, b in route if 0 <= b < parts])

    even = range(0, parts, 2)
    pivots = range(1, parts, 4)
    everyone = range(parts)

    def one_step(ahead, back, step):
        up = [(j, j + 1) for j in range(step - 1, size - 1)]
        down = [(j, j - 1) for j in range(1, size - step + 1)]
        return lax.ppermute(ahead, "space", up), lax.ppermute(back, "space", down)

    def block_at(arrived, spot):
        block = arrived[0][0]
        for step in range(1, size):
            if spot + step < size:
                block = jnp.where(place == spot + step, arrived[step][0], block)
            if spot - step >= 0:
                block = jnp.where(place == spot - step, arrived[step][1], block)
        return block

    own_arrived = [(own_rows, own_rows)]
    prev_arrived = [(prev_rows, prev_rows)]
    for step in range(1, size):
        own_arrived.append(one_step(*own_arrived[-1], step))
        prev_arrived.append(one_step(*prev_arrived[-1], step))

    own_scaled = scaled_by(own_rows, reciprocal)
    prev_scaled = scaled_by(prev_rows, reciprocal)
    own_sum = jnp.sum(own_scaled.astype(F32) * own_rows.astype(F32), axis=1)
    prev_sum = jnp.sum(prev_scaled.astype(F32) * prev_rows.astype(F32), axis=1)
    row_ids = lax.broadcasted_iota(jnp.int32, separator.shape, 0) + row_start
    col_ids = lax.broadcasted_iota(jnp.int32, separator.shape, 1)
    sep_diag = jnp.sum(jnp.where(row_ids == col_ids, separator, 0.0), axis=1)
    diag_rows = sep_diag - own_sum - between(prev_sum, [(p, p - 1) for p in everyone])
    diag = jnp.zeros((order,), F32)
    diag = lax.dynamic_update_slice_in_dim(diag, diag_rows, row_start, 0)
    for shift in range(1, size):
        ring = [(j, (j + shift) % size) for j in range(size)]
        piece = lax.ppermute(diag_rows, "space", ring)
        at = (place + size - shift) % size
        diag = lax.dynamic_update_slice_in_dim(diag, piece, at * rows, 0)
    scale = (1.0 / jnp.maximum(diag, 1.0)).astype(BF16)
    pivot_scale = between(scale, [(p, p + 1) for p in even])

    left_side = place < size // 2
    late_start = jnp.where(left_side, size - 1, 0) * rows
    is_end = jnp.logical_or(place == 0, place == size - 1)
    own_full = jnp.concatenate([block_at(own_arrived, spot) for spot in range(size)])
    before = prev_arrived[:-1] + [(jnp.zeros_like(prev_rows),) * 2]
    prev_blocks = [block_at(before, spot) for spot in range(size)]
    prev_first = jnp.concatenate(prev_blocks)
    prev_far = jnp.where(left_side, prev_blocks[-1], prev_blocks[0])
    prev_first, prev_far = lax.optimization_barrier((prev_first, prev_far))

    is_first = partition == 0
    is_pivot = partition % 2 == 0
    is_receiver = partition % 2 == 1
    flags = jnp.stack([is_first, is_end, left_side]).astype(jnp.int32)
    link, first, partial, prev_form, left_diag, right_diag = early_forms(
        flags, scaled_by(prev_first, reciprocal), prev_scaled, own_scaled, own_full, prev_first,
        separator, rows_of(scale), rows_of(pivot_scale),
    )

    flags = after(flags, link)
    end_block = jnp.where(flags[2] == 1, prev_arrived[-1][1], prev_arrived[-1][0])
    prev_late = jnp.where(flags[1] == 1, end_block, prev_far)
    link_late = (-dot_nt(scaled_by(prev_late, reciprocal), own_full)).astype(BF16)
    link_late = jnp.where(is_first, jnp.zeros_like(link_late), link_late)
    link = lax.dynamic_update_slice_in_dim(link, link_late, late_start, 0)
    first_late = scaled_by(link_late, scale)
    first = lax.dynamic_update_slice_in_dim(first, first_late, late_start, 0)
    pivot_first = between(first, [(p, p + 1) for p in even])
    late_square = link_late * link_late
    left_diag = lax.dynamic_update_slice_in_dim(
        left_diag[0], dot_nt(rows_of(scale), late_square)[0], late_start, 0
    )
    left_diag = between(left_diag, [(p, p - 1) for p in even])
    late_scale = lax.dynamic_slice_in_dim(pivot_scale, late_start, rows, 0)
    late_scale = jnp.where(is_end, late_scale, jnp.zeros_like(late_scale))
    right_diag = right_diag[0] + dot_nn(rows_of(late_scale), late_square)[0]
    prev_form = lax.dynamic_update_slice_in_dim(
        prev_form, dot_nt(prev_scaled, prev_late), late_start, 1
    )

    first_rows = lax.dynamic_slice_in_dim(first, row_start, rows, 0)
    left_form = dot_nt(first_rows, link)
    to_earlier = jnp.where(is_pivot, prev_form + left_form, prev_form).astype(BF16)
    from_later = between(to_earlier, [(p, p - 1) for p in everyone])
    next_link = (-dot_nn(pivot_first, link)).astype(BF16)
    next_rows = lax.dynamic_slice_in_dim(next_link, row_start, rows, 0)
    pivot_rows = between(next_rows, [(p, p + 2) for p in pivots if p != 1])

    next_diag = diag - left_diag - right_diag
    next_scale = (1.0 / jnp.maximum(next_diag, 1.0)).astype(BF16)
    next_pivot_scale = between(next_scale, [(p, p + 2) for p in pivots])
    left_next = dot_nt(scaled_by(next_rows, next_scale), next_link).astype(BF16)
    from_pivot = between(left_next, [(p, p - 2) for p in pivots])

    link_cols = lax.dynamic_slice_in_dim(link, row_start, rows, 1)
    right_form = dot_tn(row_scaled_by(link_cols, pivot_scale), link)

    is_last = partition % 4 == 3
    next_cols = lax.dynamic_slice_in_dim(next_link, row_start, rows, 1)
    right_next = dot_tn(row_scaled_by(next_cols, next_pivot_scale), next_link)
    last_rows = (-dot_nn(scaled_by(pivot_rows, next_pivot_scale), next_link)).astype(BF16)
    link_rows = lax.dynamic_slice_in_dim(link, row_start, rows, 0)
    out_link = jnp.where(is_last, last_rows, jnp.where(is_receiver, next_rows, link_rows))
    updates = jnp.where(is_last, right_form + right_next, jnp.where(is_receiver, right_form, 0.0))
    updates = lax.optimization_barrier(updates)
    schur = partial - updates - from_later.astype(F32) - from_pivot.astype(F32)
    return (schur[None], out_link[None])


def solution(mesh):
    placed = (P("tm", "space", None), P("tm", "space", None), P("tm", "space", None), P("tm", None))
    return jax.shard_map(
        on_device,
        mesh=mesh,
        in_specs=placed,
        out_specs=(P("tm", "space", None), P("tm", "space", None)),
        check_vma=False,
    )
```

```python
import functools

import jax
import jax.numpy as jnp
from jax import lax
from jax.experimental import pallas as pl
from jax.experimental.pallas import tpu as pltpu
from jax.sharding import PartitionSpec as P

BF16 = jnp.bfloat16
F32 = jnp.float32
EXTRA = 16
WIDTH = 256

ANY = pl.BlockSpec(memory_space=pl.ANY)
SHAPE = jax.ShapeDtypeStruct
FREE = pl.CostEstimate(flops=0, bytes_accessed=0, transcendentals=0)


def after(block, *others):
    def body(*refs):
        del refs

    return pl.pallas_call(
        body,
        out_shape=SHAPE(block.shape, block.dtype),
        in_specs=[ANY] * (1 + len(others)),
        out_specs=ANY,
        input_output_aliases={0: 0},
    )(block, *others)


def scaled_by(matrix, factors):
    return (matrix.astype(F32) * factors.astype(F32)[None, :]).astype(BF16)


def row_scaled_by(matrix, factors):
    return (matrix.astype(F32) * factors.astype(F32)[:, None]).astype(BF16)


def dot_nt(left, right):
    return lax.dot_general(left, right, (((1,), (1,)), ((), ())), preferred_element_type=F32)


def dot_nn(left, right):
    return lax.dot_general(left, right, (((1,), (0,)), ((), ())), preferred_element_type=F32)


def dot_tn(left, right):
    return lax.dot_general(left, right, (((0,), (0,)), ((), ())), preferred_element_type=F32)


def rows_of(scale):
    return jnp.broadcast_to(scale[None, :], (8, scale.shape[0]))


def whole_spec(shape):
    return pl.BlockSpec(shape, lambda j, f: (0,) * len(shape))


def along_spec(count):
    return pl.BlockSpec((count, WIDTH), lambda j, f: (0, j))


def down_spec(count):
    return pl.BlockSpec((WIDTH, count), lambda j, f: (j, 0))


def early_kernel(
    size, flags, prev_whole, prev_rows, own_rows, prev, separator, scale, scale_here, pivot_scale, *refs
):
    sources = refs[: 2 * size - 1]
    (link, first, partial, update, left_diag, right_diag, own_out, own, form, sems) = refs[2 * size - 1 :]
    rows = separator.shape[0]
    step = pl.program_id(0)
    here = pl.ds(pl.multiple_of(step * WIDTH, WIDTH), WIDTH)
    place = flags[2]

    def copies():
        for spot in range(size):
            for by, source in enumerate(sources):
                distance = (by + 1) // 2 if by % 2 else -(by // 2)
                target = own.at[pl.ds(spot * rows, rows)]
                copy = pltpu.make_async_copy(source.at[pl.ds(0, rows)], target, sems.at[spot])
                yield place - spot == distance, copy

    @pl.when(step == 0)
    def _():
        for chosen, copy in copies():
            pl.when(chosen)(copy.start)
        for chosen, copy in copies():
            pl.when(chosen)(copy.wait)
        pltpu.make_async_copy(own, own_out, sems.at[size]).start()
        left_diag[...] = jnp.zeros_like(left_diag)
        form[...] = jnp.zeros_like(form)

    block = own[here, :]
    part = jnp.where(flags[0] == 1, 0.0, -dot_nt(prev_whole[...], block)).astype(BF16)
    link[...] = part
    scaled = part * scale_here[0:1]
    first[...] = scaled
    partial[...] = separator[...] - dot_nt(own_rows[...], block)
    square = part * part
    right_diag[...] = dot_nn(pivot_scale[...], square)
    left_diag[...] += dot_nt(scale_here[...], square)

    @pl.when(flags[1] == 1)
    def _():
        mine = first[pl.ds(pl.multiple_of(place * rows, rows), rows), :]
        form[...] += dot_nt(mine, part)

    form[:, here] += dot_nt(prev_rows[...], prev[...])

    @pl.when(step == pl.num_programs(0) - 1)
    def _():
        update[...] = form[...].astype(BF16)
        pltpu.make_async_copy(own, own_out, sems.at[size]).wait()


def early_forms(flags, prev_whole, prev_rows, own_rows, prev, separator, scale, pivot_scale, sources):
    rows, order = own_rows.shape
    size = order // rows
    return pl.pallas_call(
        functools.partial(early_kernel, size),
        out_shape=[
            SHAPE((order, order), BF16),
            SHAPE((order, order), BF16),
            SHAPE((rows, order), F32),
            SHAPE((rows, order), BF16),
            SHAPE((8, order), F32),
            SHAPE((8, order), F32),
            SHAPE((order, order), BF16),
        ],
        grid_spec=pltpu.PrefetchScalarGridSpec(
            num_scalar_prefetch=1,
            grid=(order // WIDTH,),
            in_specs=[
                whole_spec((order, order)),
                whole_spec((rows, order)),
                whole_spec((rows, order)),
                down_spec(order),
                along_spec(rows),
                whole_spec((8, order)),
                along_spec(8),
                whole_spec((8, order)),
            ]
            + [ANY] * len(sources),
            out_specs=[
                along_spec(order),
                along_spec(order),
                along_spec(rows),
                whole_spec((rows, order)),
                whole_spec((8, order)),
                along_spec(8),
                ANY,
            ],
            scratch_shapes=[
                pltpu.VMEM((order, order), BF16),
                pltpu.VMEM((rows, order), F32),
                pltpu.SemaphoreType.DMA((size + 1,)),
            ],
        ),
        compiler_params=pltpu.CompilerParams(vmem_limit_bytes=40 * 1024 * 1024),
        cost_estimate=FREE,
    )(flags, prev_whole, prev_rows, own_rows, prev, separator, scale, scale, pivot_scale, *sources)


def late_kernel(
    size, flags, reciprocal, prev_rows, own, scale, late_scale, from_below, from_above, far, link_in, first_in,
    link, first, corner, left_diag, right_diag, raw, scaled, late, late_first, mine, sems,
):
    del link_in, first_in
    rows = raw.shape[0]
    place = flags[2]
    step = pl.program_id(0)
    here = pl.ds(pl.multiple_of(step * WIDTH, WIDTH), WIDTH)
    low = place < size // 2
    late_start = pl.multiple_of(jnp.where(low, (size - 1) * rows, 0), rows)
    late_rows = pl.ds(late_start, rows)
    my_rows = pl.ds(pl.multiple_of(place * rows, rows), rows)

    @pl.when(step == 0)
    def _():
        fetch = pltpu.make_async_copy(first.at[my_rows], mine, sems.at[1])
        fetch.start()
        for chosen, source in (
            (place == 0, from_above),
            (place == size - 1, from_below),
            (jnp.logical_and(place != 0, place != size - 1), far),
        ):
            copy = pltpu.make_async_copy(source, raw, sems.at[0])
            pl.when(chosen)(copy.start)
            pl.when(chosen)(copy.wait)
        fetch.wait()
        scaled[...] = (raw[...].astype(F32) * reciprocal[0:1]).astype(BF16)

    part = jnp.where(flags[0] == 1, 0.0, -dot_nt(scaled[...], own[...])).astype(BF16)
    late[:, here] = part
    late_first[:, here] = part * scale[0:1, here]

    @pl.when(step == pl.num_programs(0) - 1)
    def _():
        copies = [
            pltpu.make_async_copy(late, link.at[late_rows], sems.at[0]),
            pltpu.make_async_copy(late_first, first.at[late_rows], sems.at[1]),
        ]
        for copy in copies:
            copy.start()
        whole = late[...]
        square = whole * whole
        keep = jnp.where(flags[1] == 1, 1.0, 0.0)
        corner[...] = (dot_nt(prev_rows[...], raw[...]) + keep * dot_nt(mine[...], whole)).astype(BF16)
        left_diag[...] = dot_nt(scale[...], square)
        right_diag[...] = dot_nn(late_scale[...], square)
        for copy in copies:
            copy.wait()


def late_forms(flags, reciprocal, prev_rows, own, scale, late_scale, from_below, from_above, far, link, first):
    rows, order = prev_rows.shape
    size = order // rows
    return pl.pallas_call(
        functools.partial(late_kernel, size),
        out_shape=[
            SHAPE((order, order), BF16),
            SHAPE((order, order), BF16),
            SHAPE((rows, rows), BF16),
            SHAPE((8, rows), F32),
            SHAPE((8, order), F32),
        ],
        grid_spec=pltpu.PrefetchScalarGridSpec(
            num_scalar_prefetch=1,
            grid=(order // WIDTH,),
            in_specs=[
                whole_spec((8, order)),
                whole_spec((rows, order)),
                down_spec(order),
                whole_spec((8, order)),
                whole_spec((8, rows)),
                ANY,
                ANY,
                ANY,
                ANY,
                ANY,
            ],
            out_specs=[
                ANY,
                ANY,
                whole_spec((rows, rows)),
                whole_spec((8, rows)),
                whole_spec((8, order)),
            ],
            scratch_shapes=[
                pltpu.VMEM((rows, order), BF16),
                pltpu.VMEM((rows, order), BF16),
                pltpu.VMEM((rows, order), BF16),
                pltpu.VMEM((rows, order), BF16),
                pltpu.VMEM((rows, order), BF16),
                pltpu.SemaphoreType.DMA((2,)),
            ],
        ),
        input_output_aliases={9: 0, 10: 1},
        compiler_params=pltpu.CompilerParams(vmem_limit_bytes=24 * 1024 * 1024),
    )(flags, reciprocal, prev_rows, own, scale, late_scale, from_below, from_above, far, link, first)


def on_device(sep_block, own_couple, prev_couple, inner_diag):
    separator = sep_block[0]
    own_rows = own_couple[0]
    prev_rows = prev_couple[0]
    reciprocal = 1.0 / inner_diag[0]
    rows, order = own_rows.shape
    place = lax.axis_index("space")
    size = lax.axis_size("space")
    row_start = place * rows
    partition = lax.axis_index("tm")
    parts = lax.axis_size("tm")

    def between(block, route):
        return lax.ppermute(block, "tm", [(a, b) for a, b in route if 0 <= b < parts])

    even = range(0, parts, 2)
    pivots = range(1, parts, 4)
    everyone = range(parts)

    def one_step(ahead, back, step):
        up = [(j, j + 1) for j in range(step - 1, size - 1)]
        down = [(j, j - 1) for j in range(1, size - step + 1)]
        return lax.ppermute(ahead, "space", up), lax.ppermute(back, "space", down)

    def block_at(arrived, spot):
        block = arrived[0][0]
        for step in range(1, len(arrived)):
            if spot + step < size:
                block = jnp.where(place == spot + step, arrived[step][0], block)
            if spot - step >= 0:
                block = jnp.where(place == spot - step, arrived[step][1], block)
        return block

    own_arrived = [(own_rows, own_rows)]
    own_arrived.append(one_step(own_rows, own_rows, 1))

    own_scaled = scaled_by(own_rows, reciprocal)
    prev_scaled = scaled_by(prev_rows, reciprocal)
    own_sum = jnp.sum(own_scaled.astype(F32) * own_rows.astype(F32), axis=1)
    prev_sum = jnp.sum(prev_scaled.astype(F32) * prev_rows.astype(F32), axis=1)
    row_ids = lax.broadcasted_iota(jnp.int32, separator.shape, 0) + row_start
    col_ids = lax.broadcasted_iota(jnp.int32, separator.shape, 1)
    sep_diag = jnp.sum(jnp.where(row_ids == col_ids, separator, 0.0), axis=1)
    diag_rows = sep_diag - own_sum - between(prev_sum, [(p, p - 1) for p in everyone])
    high = lax.reduce_precision(diag_rows, 8, 7)
    words = jnp.stack([high, diag_rows - high]).astype(BF16)
    words = jnp.pad(words, ((0, EXTRA - 2), (0, order - rows)))
    words_arrived = [(words, words)]
    words_arrived.append(one_step(words, words, 1))
    prev_rows = after(prev_rows, *words_arrived[1])
    prev_arrived = [(prev_rows, prev_rows)]
    prev_arrived.append(one_step(prev_rows, prev_rows, 1))
    longer = [jnp.concatenate(pair) for pair in zip(own_arrived[1], words_arrived[1])]
    for step in range(2, size):
        longer = one_step(*longer, step)
        own_arrived.append(longer)
        words_arrived.append(tuple(block[rows:] for block in longer))
        prev_arrived.append(one_step(*prev_arrived[-1], step))

    words = [block_at(words_arrived, spot) for spot in range(size)]
    diag = jnp.concatenate([word[0, :rows].astype(F32) + word[1, :rows].astype(F32) for word in words])
    scale = (1.0 / jnp.maximum(diag, 1.0)).astype(BF16)
    pivot_scale = between(scale, [(p, p + 1) for p in even])

    left_side = place < size // 2
    late_start = jnp.where(left_side, size - 1, 0) * rows
    is_end = jnp.logical_or(place == 0, place == size - 1)
    prev_blocks = [block_at(prev_arrived[:-1], spot) for spot in range(size)]
    zero = jnp.zeros_like(prev_rows)
    prev_blocks[0] = jnp.where(place == size - 1, zero, prev_blocks[0])
    prev_blocks[-1] = jnp.where(place == 0, zero, prev_blocks[-1])
    prev_first = jnp.concatenate(prev_blocks)
    prev_far = jnp.where(left_side, prev_blocks[-1], prev_blocks[0])

    is_first = partition == 0
    is_pivot = partition % 2 == 0
    is_receiver = partition % 2 == 1
    flags = jnp.stack([is_first.astype(jnp.int32), is_pivot.astype(jnp.int32), place])
    sources = [own_rows]
    for up, down in own_arrived[1:]:
        sources += [up, down]
    link, first, partial, update, left_diag, right_diag, own_full = early_forms(
        flags, scaled_by(prev_first, reciprocal), prev_scaled, own_scaled, prev_first,
        separator, rows_of(scale), rows_of(pivot_scale), sources,
    )

    late_scale = lax.dynamic_slice_in_dim(pivot_scale, late_start, rows, 0)
    late_scale = jnp.where(is_end, late_scale, jnp.zeros_like(late_scale))
    link, first, corner, left_late, right_late = late_forms(
        flags, rows_of(reciprocal), prev_scaled, own_full, rows_of(scale), rows_of(late_scale),
        prev_arrived[-1][0], prev_arrived[-1][1], prev_far, link, first,
    )
    pivot_first = between(first, [(p, p + 1) for p in even])
    left_diag = lax.dynamic_update_slice_in_dim(left_diag[0], left_late[0], late_start, 0)
    left_diag = between(left_diag, [(p, p - 1) for p in even])
    right_diag = right_diag[0] + right_late[0]
    to_earlier = lax.dynamic_update_slice_in_dim(update, corner, late_start, 1)
    from_later = between(to_earlier, [(p, p - 1) for p in everyone])

    next_link = (-dot_nn(pivot_first, link)).astype(BF16)
    next_rows = lax.dynamic_slice_in_dim(next_link, row_start, rows, 0)
    pivot_rows = between(next_rows, [(p, p + 2) for p in pivots if p != 1])

    next_diag = diag - left_diag - right_diag
    next_scale = (1.0 / jnp.maximum(next_diag, 1.0)).astype(BF16)
    next_pivot_scale = between(next_scale, [(p, p + 2) for p in pivots])
    left_next = dot_nt(scaled_by(next_rows, next_scale), next_link).astype(BF16)
    from_pivot = between(left_next, [(p, p - 2) for p in pivots])

    link_cols = lax.dynamic_slice_in_dim(link, row_start, rows, 1)
    right_form = dot_tn(row_scaled_by(link_cols, pivot_scale), link)

    is_last = partition % 4 == 3
    next_cols = lax.dynamic_slice_in_dim(next_link, row_start, rows, 1)
    right_next = dot_tn(row_scaled_by(next_cols, next_pivot_scale), next_link)
    last_rows = (-dot_nn(scaled_by(pivot_rows, next_pivot_scale), next_link)).astype(BF16)
    link_rows = lax.dynamic_slice_in_dim(link, row_start, rows, 0)
    out_link = jnp.where(is_last, last_rows, jnp.where(is_receiver, next_rows, link_rows))
    updates = jnp.where(is_last, right_form + right_next, jnp.where(is_receiver, right_form, 0.0))
    updates = lax.optimization_barrier(updates)
    schur = partial - updates - from_later.astype(F32) - from_pivot.astype(F32)
    return (schur[None], out_link[None])


def solution(mesh):
    placed = (P("tm", "space", None), P("tm", "space", None), P("tm", "space", None), P("tm", None))
    return jax.shard_map(
        on_device,
        mesh=mesh,
        in_specs=placed,
        out_specs=(P("tm", "space", None), P("tm", "space", None)),
        check_vma=False,
    )
```

```python
import functools

import jax
import jax.numpy as jnp
from jax import lax
from jax.experimental import pallas as pl
from jax.experimental.pallas import tpu as pltpu
from jax.sharding import PartitionSpec as P

BF16 = jnp.bfloat16
F32 = jnp.float32
EXTRA = 16
WIDTH = 256

ANY = pl.BlockSpec(memory_space=pl.ANY)
SHAPE = jax.ShapeDtypeStruct
FREE = pl.CostEstimate(flops=0, bytes_accessed=0, transcendentals=0)


def after(block, *others):
    def body(*refs):
        del refs

    return pl.pallas_call(
        body,
        out_shape=SHAPE(block.shape, block.dtype),
        in_specs=[ANY] * (1 + len(others)),
        out_specs=ANY,
        input_output_aliases={0: 0},
    )(block, *others)


def scaled_by(matrix, factors):
    return (matrix.astype(F32) * factors.astype(F32)[None, :]).astype(BF16)


def row_scaled_by(matrix, factors):
    return (matrix.astype(F32) * factors.astype(F32)[:, None]).astype(BF16)


def dot_nt(left, right):
    return lax.dot_general(left, right, (((1,), (1,)), ((), ())), preferred_element_type=F32)


def dot_nn(left, right):
    return lax.dot_general(left, right, (((1,), (0,)), ((), ())), preferred_element_type=F32)


def dot_tn(left, right):
    return lax.dot_general(left, right, (((0,), (0,)), ((), ())), preferred_element_type=F32)


def rows_of(scale):
    return jnp.broadcast_to(scale[None, :], (8, scale.shape[0]))


def whole_spec(shape):
    return pl.BlockSpec(shape, lambda j, f: (0,) * len(shape))


def along_spec(count):
    return pl.BlockSpec((count, WIDTH), lambda j, f: (0, j))


def down_spec(count):
    return pl.BlockSpec((WIDTH, count), lambda j, f: (j, 0))


def opening_kernel(flags, own, prev, separator, reciprocal, long):
    rows, order = own.shape
    row_ids = lax.broadcasted_iota(jnp.int32, (rows, order), 0) + flags[1] * rows
    col_ids = lax.broadcasted_iota(jnp.int32, (rows, order), 1)
    on_diagonal = jnp.where(row_ids == col_ids, separator[...], 0.0)
    ones = jnp.ones((8, order), BF16)

    def split(value):
        high = value.astype(BF16)
        return high, (value - high.astype(F32)).astype(BF16)

    def form_diagonal(block):
        wide = block.astype(F32)
        high, low = split((wide * reciprocal[0:1]).astype(BF16).astype(F32) * wide)
        return (dot_nt(ones, high) + dot_nt(ones, low))[0:1]

    def placed(words, count):
        ids = lax.broadcasted_iota(jnp.int32, (EXTRA, count), 0)
        total = jnp.zeros((EXTRA, count), F32)
        for at, word in words.items():
            total = jnp.where(ids == at, word.astype(F32), total)
        return total.astype(BF16)

    long[0:rows, :] = prev[...]
    high, low = split(jnp.sum(on_diagonal, axis=0, keepdims=True))
    long[rows:, :] = placed({0: high, 1: low}, order)
    own_high, own_low = split(form_diagonal(own[...]))
    prev_high, prev_low = split(form_diagonal(prev[...]))
    local = placed({2: own_high, 3: own_low, 4: prev_high, 5: prev_low}, rows)
    long[rows:, 0:rows] = long[rows:, 0:rows] + local


def opening(flags, own, prev, separator, reciprocal):
    rows, order = own.shape
    return pl.pallas_call(
        opening_kernel,
        out_shape=SHAPE((rows + EXTRA, order), BF16),
        in_specs=[pl.BlockSpec(memory_space=pltpu.SMEM)] + [pl.BlockSpec(memory_space=pltpu.VMEM)] * 4,
        out_specs=pl.BlockSpec(memory_space=pltpu.VMEM),
        compiler_params=pltpu.CompilerParams(vmem_limit_bytes=32 * 1024 * 1024),
        cost_estimate=FREE,
    )(flags, own, prev, separator, reciprocal)


def early_kernel(size, flags, prev_whole, prev_rows, own_rows, separator, *refs):
    sources = refs[: 2 * size - 1]
    link, partial, form, own_out, own, sems = refs[2 * size - 1 :]
    rows = separator.shape[0]
    step = pl.program_id(0)
    here = pl.ds(pl.multiple_of(step * WIDTH, WIDTH), WIDTH)

    def copies():
        for spot in range(size):
            for by, source in enumerate(sources):
                distance = (by + 1) // 2 if by % 2 else -(by // 2)
                target = own.at[pl.ds(spot * rows, rows)]
                copy = pltpu.make_async_copy(source, target, sems.at[spot])
                yield flags[1] - spot == distance, copy

    @pl.when(step == 0)
    def _():
        for chosen, copy in copies():
            pl.when(chosen)(copy.start)
        for chosen, copy in copies():
            pl.when(chosen)(copy.wait)
        pltpu.make_async_copy(own, own_out, sems.at[size]).start()

    block = own[here, :]
    link[...] = jnp.where(flags[0] == 1, 0.0, -dot_nt(prev_whole[...], block)).astype(BF16)
    partial[...] = separator[...] - dot_nt(own_rows[...], block)
    form[...] = dot_nt(prev_rows[...], prev_whole[here, :])

    @pl.when(step == pl.num_programs(0) - 1)
    def _():
        pltpu.make_async_copy(own, own_out, sems.at[size]).wait()


def early_forms(flags, prev_whole, prev_rows, own_rows, separator, sources):
    rows, order = own_rows.shape
    size = order // rows
    return pl.pallas_call(
        functools.partial(early_kernel, size),
        out_shape=[
            SHAPE((order, order), BF16),
            SHAPE((rows, order), F32),
            SHAPE((rows, order), F32),
            SHAPE((order, order), BF16),
        ],
        grid_spec=pltpu.PrefetchScalarGridSpec(
            num_scalar_prefetch=1,
            grid=(order // WIDTH,),
            in_specs=[
                whole_spec((order, order)),
                whole_spec((rows, order)),
                whole_spec((rows, order)),
                along_spec(rows),
            ]
            + [ANY] * len(sources),
            out_specs=[along_spec(order), along_spec(rows), along_spec(rows), ANY],
            scratch_shapes=[pltpu.VMEM((order, order), BF16), pltpu.SemaphoreType.DMA((size + 1,))],
        ),
        compiler_params=pltpu.CompilerParams(vmem_limit_bytes=32 * 1024 * 1024),
        cost_estimate=FREE,
    )(flags, prev_whole, prev_rows, own_rows, separator, *sources)


def late_kernel(
    size, flags, reciprocal, prev_rows, own, from_below, from_above, far, link, corner, raw, scaled, sem
):
    place = flags[1]
    rows = raw.shape[0]
    step = pl.program_id(0)
    width = own.shape[0]
    here = pl.ds(pl.multiple_of(step * width, width), width)

    @pl.when(step == 0)
    def _():
        for chosen, source in (
            (place == 0, from_above.at[pl.ds(0, rows)]),
            (place == size - 1, from_below.at[pl.ds(0, rows)]),
            (jnp.logical_and(place != 0, place != size - 1), far),
        ):
            copy = pltpu.make_async_copy(source, raw, sem)
            pl.when(chosen)(copy.start)
            pl.when(chosen)(copy.wait)
        scaled[...] = (raw[...].astype(F32) * reciprocal[0:1]).astype(BF16)
        corner[...] = dot_nt(prev_rows[...], scaled[...])

    link[:, here] = jnp.where(flags[0] == 1, 0.0, -dot_nt(scaled[...], own[...])).astype(BF16)


def late_forms(flags, reciprocal, prev_rows, own, from_below, from_above, far):
    rows, order = prev_rows.shape
    size = order // rows
    width = 512
    return pl.pallas_call(
        functools.partial(late_kernel, size),
        out_shape=[SHAPE((rows, order), BF16), SHAPE((rows, rows), F32)],
        grid_spec=pltpu.PrefetchScalarGridSpec(
            num_scalar_prefetch=1,
            grid=(order // width,),
            in_specs=[
                whole_spec((8, order)),
                whole_spec((rows, order)),
                pl.BlockSpec((width, order), lambda j, f: (j, 0)),
                ANY,
                ANY,
                ANY,
            ],
            out_specs=[whole_spec((rows, order)), whole_spec((rows, rows))],
            scratch_shapes=[
                pltpu.VMEM((rows, order), BF16),
                pltpu.VMEM((rows, order), BF16),
                pltpu.SemaphoreType.DMA,
            ],
        ),
        compiler_params=pltpu.CompilerParams(vmem_limit_bytes=20 * 1024 * 1024),
    )(flags, reciprocal, prev_rows, own, from_below, from_above, far)


def on_device(sep_block, own_couple, prev_couple, inner_diag):
    separator = sep_block[0]
    own_rows = own_couple[0]
    prev_rows = prev_couple[0]
    reciprocal = 1.0 / inner_diag[0]
    rows, order = own_rows.shape
    place = lax.axis_index("space")
    size = lax.axis_size("space")
    row_start = place * rows
    partition = lax.axis_index("tm")
    parts = lax.axis_size("tm")

    def between(block, route):
        return lax.ppermute(block, "tm", [(a, b) for a, b in route if 0 <= b < parts])

    even = range(0, parts, 2)
    pivots = range(1, parts, 4)
    everyone = range(parts)

    def one_step(ahead, back, step):
        up = [(j, j + 1) for j in range(step - 1, size - 1)]
        down = [(j, j - 1) for j in range(1, size - step + 1)]
        return lax.ppermute(ahead, "space", up), lax.ppermute(back, "space", down)

    def block_at(arrived, spot):
        block = arrived[0][0]
        for step in range(1, len(arrived)):
            if spot + step < size:
                block = jnp.where(place == spot + step, arrived[step][0], block)
            if spot - step >= 0:
                block = jnp.where(place == spot - step, arrived[step][1], block)
        return block

    own_arrived = [(own_rows, own_rows)]
    own_arrived.append(one_step(own_rows, own_rows, 1))

    is_first = partition == 0
    flags = jnp.stack([is_first.astype(jnp.int32), place])
    prev_long = opening(flags, own_rows, prev_rows, separator, rows_of(reciprocal))
    long_arrived = [(prev_long, prev_long)]
    long_arrived.append(one_step(prev_long, prev_long, 1))
    for step in range(2, size):
        own_arrived.append(one_step(*own_arrived[-1], step))
        long_arrived.append(one_step(*long_arrived[-1], step))

    left_side = place < size // 2
    late_start = jnp.where(left_side, size - 1, 0) * rows
    is_end = jnp.logical_or(place == 0, place == size - 1)
    prev_arrived = [tuple(block[:rows] for block in pair) for pair in long_arrived[:-1]]
    words_arrived = [tuple(block[rows:] for block in pair) for pair in long_arrived[:-1]]
    prev_blocks = [block_at(prev_arrived, spot) for spot in range(size)]
    zero = jnp.zeros_like(prev_rows)
    prev_blocks[0] = jnp.where(place == size - 1, zero, prev_blocks[0])
    prev_blocks[-1] = jnp.where(place == 0, zero, prev_blocks[-1])
    prev_first = jnp.concatenate(prev_blocks)
    prev_far = jnp.where(left_side, prev_blocks[-1], prev_blocks[0])
    words = [block_at(words_arrived, spot) for spot in range(size)]
    none = jnp.zeros_like(words[0])
    words[0] = jnp.where(place == size - 1, none, words[0])
    words[-1] = jnp.where(place == 0, none, words[-1])

    def pair_sum(block, at):
        return block[at].astype(F32) + block[at + 1].astype(F32)

    sep_diag = sum(pair_sum(block, 0) for block in words)
    own_diag = jnp.concatenate([pair_sum(block, 2)[:rows] for block in words])
    prev_diag = jnp.concatenate([pair_sum(block, 4)[:rows] for block in words])
    prev_first, prev_far, sep_diag, own_diag, prev_diag = lax.optimization_barrier(
        (prev_first, prev_far, sep_diag, own_diag, prev_diag)
    )

    is_pivot = partition % 2 == 0
    is_receiver = partition % 2 == 1
    own_scaled = scaled_by(own_rows, reciprocal)
    sources = [own_rows]
    for up, down in own_arrived[1:]:
        sources += [up, down]
    link, partial, prev_form, own_full = early_forms(
        flags, scaled_by(prev_first, reciprocal), prev_rows, own_scaled, separator, sources
    )

    from_below, from_above = long_arrived[-1]
    late, corner = late_forms(
        flags, rows_of(reciprocal), prev_rows, own_full, from_below, from_above, prev_far
    )
    link = lax.dynamic_update_slice_in_dim(link, late, late_start, 0)
    pivot_link = between(link, [(p, p + 1) for p in even])
    end_words = jnp.where(left_side, from_above[rows:], from_below[rows:])
    end_words = jnp.where(is_end, end_words, jnp.zeros_like(end_words))
    sep_diag = sep_diag + pair_sum(end_words, 0)
    own_diag = own_diag + lax.dynamic_update_slice_in_dim(
        jnp.zeros_like(own_diag), pair_sum(end_words, 2)[:rows], late_start, 0
    )
    prev_diag = prev_diag + lax.dynamic_update_slice_in_dim(
        jnp.zeros_like(prev_diag), pair_sum(end_words, 4)[:rows], late_start, 0
    )
    diag = sep_diag - own_diag - between(prev_diag, [(p, p - 1) for p in everyone])
    scale = (1.0 / jnp.maximum(diag, 1.0)).astype(BF16)
    pivot_scale = between(scale, [(p, p + 1) for p in even])

    link_rows = lax.dynamic_slice_in_dim(link, row_start, rows, 0)
    left_form = dot_nt(scaled_by(link_rows, scale), link)
    prev_form = lax.dynamic_update_slice_in_dim(prev_form, corner, late_start, 1)
    to_earlier = jnp.where(is_pivot, prev_form + left_form, prev_form).astype(BF16)
    from_even = between(to_earlier, [(p, p - 1) for p in even])
    from_odd = between(to_earlier, [(p, p - 1) for p in range(1, parts, 2)])
    left_diag = between(dot_nt(rows_of(scale), link * link)[0], [(p, p - 1) for p in even])
    right_diag = dot_nn(rows_of(pivot_scale), link * link)[0]

    pivot_rows = lax.dynamic_slice_in_dim(pivot_link, row_start, rows, 0)
    next_rows = (-dot_nn(scaled_by(pivot_rows, pivot_scale), link)).astype(BF16)
    pivot_rows = between(next_rows, [(p, p + 2) for p in pivots if p != 1])
    next_link = (-dot_nn(scaled_by(pivot_link, after(pivot_scale, next_rows)), link)).astype(BF16)

    next_diag = diag - left_diag - right_diag
    next_scale = (1.0 / jnp.maximum(next_diag, 1.0)).astype(BF16)
    next_pivot_scale = between(next_scale, [(p, p + 2) for p in pivots])
    left_next = dot_nt(scaled_by(next_rows, next_scale), next_link).astype(BF16)
    from_pivot = between(left_next, [(p, p - 2) for p in pivots])

    link_cols = lax.dynamic_slice_in_dim(link, row_start, rows, 1)
    right_form = dot_tn(row_scaled_by(link_cols, pivot_scale), link)

    is_last = partition % 4 == 3
    next_cols = lax.dynamic_slice_in_dim(next_link, row_start, rows, 1)
    right_next = dot_tn(row_scaled_by(next_cols, next_pivot_scale), next_link)
    last_rows = (-dot_nn(scaled_by(pivot_rows, next_pivot_scale), next_link)).astype(BF16)
    out_link = jnp.where(is_last, last_rows, jnp.where(is_receiver, next_rows, link_rows))
    updates = jnp.where(is_last, right_form + right_next, jnp.where(is_receiver, right_form, 0.0))
    updates = lax.optimization_barrier(updates)
    schur = partial - updates - (from_even + from_odd).astype(F32) - from_pivot.astype(F32)
    return (schur[None], out_link[None])


def solution(mesh):
    placed = (P("tm", "space", None), P("tm", "space", None), P("tm", "space", None), P("tm", None))
    return jax.shard_map(
        on_device,
        mesh=mesh,
        in_specs=placed,
        out_specs=(P("tm", "space", None), P("tm", "space", None)),
        check_vma=False,
    )
```

```python
import functools

import jax
import jax.numpy as jnp
from jax import lax
from jax.experimental import pallas as pl
from jax.experimental.pallas import tpu as pltpu
from jax.sharding import PartitionSpec as P

BF16 = jnp.bfloat16
F32 = jnp.float32
EXTRA = 16
WIDTH = 256

ANY = pl.BlockSpec(memory_space=pl.ANY)
SHAPE = jax.ShapeDtypeStruct
FREE = pl.CostEstimate(flops=0, bytes_accessed=0, transcendentals=0)


def after(block, *others):
    def body(*refs):
        del refs

    return pl.pallas_call(
        body,
        out_shape=SHAPE(block.shape, block.dtype),
        in_specs=[ANY] * (1 + len(others)),
        out_specs=ANY,
        input_output_aliases={0: 0},
    )(block, *others)


def scaled_by(matrix, factors):
    return (matrix.astype(F32) * factors.astype(F32)[None, :]).astype(BF16)


def row_scaled_by(matrix, factors):
    return (matrix.astype(F32) * factors.astype(F32)[:, None]).astype(BF16)


def dot_nt(left, right):
    return lax.dot_general(left, right, (((1,), (1,)), ((), ())), preferred_element_type=F32)


def dot_nn(left, right):
    return lax.dot_general(left, right, (((1,), (0,)), ((), ())), preferred_element_type=F32)


def dot_tn(left, right):
    return lax.dot_general(left, right, (((0,), (0,)), ((), ())), preferred_element_type=F32)


def rows_of(scale):
    return jnp.broadcast_to(scale[None, :], (8, scale.shape[0]))


def whole_spec(shape):
    return pl.BlockSpec(shape, lambda j, f: (0,) * len(shape))


def along_spec(count):
    return pl.BlockSpec((count, WIDTH), lambda j, f: (0, j))


def down_spec(count):
    return pl.BlockSpec((WIDTH, count), lambda j, f: (j, 0))


def opening_kernel(flags, own, prev, separator, reciprocal, long):
    rows, order = own.shape
    row_ids = lax.broadcasted_iota(jnp.int32, (rows, order), 0) + flags[1] * rows
    col_ids = lax.broadcasted_iota(jnp.int32, (rows, order), 1)
    on_diagonal = jnp.where(row_ids == col_ids, separator[...], 0.0)
    ones = jnp.ones((8, order), BF16)

    def split(value):
        high = value.astype(BF16)
        return high, (value - high.astype(F32)).astype(BF16)

    def form_diagonal(block):
        wide = block.astype(F32)
        high, low = split((wide * reciprocal[0:1]).astype(BF16).astype(F32) * wide)
        return (dot_nt(ones, high) + dot_nt(ones, low))[0:1]

    def placed(words, count):
        ids = lax.broadcasted_iota(jnp.int32, (EXTRA, count), 0)
        total = jnp.zeros((EXTRA, count), F32)
        for at, word in words.items():
            total = jnp.where(ids == at, word.astype(F32), total)
        return total.astype(BF16)

    long[0:rows, :] = prev[...]
    high, low = split(jnp.sum(on_diagonal, axis=0, keepdims=True))
    long[rows:, :] = placed({0: high, 1: low}, order)
    own_high, own_low = split(form_diagonal(own[...]))
    prev_high, prev_low = split(form_diagonal(prev[...]))
    local = placed({2: own_high, 3: own_low, 4: prev_high, 5: prev_low}, rows)
    long[rows:, 0:rows] = long[rows:, 0:rows] + local


def opening(flags, own, prev, separator, reciprocal):
    rows, order = own.shape
    return pl.pallas_call(
        opening_kernel,
        out_shape=SHAPE((rows + EXTRA, order), BF16),
        grid_spec=pltpu.PrefetchScalarGridSpec(
            num_scalar_prefetch=1,
            grid=(1,),
            in_specs=[whole_spec((rows, order))] * 3 + [whole_spec((8, order))],
            out_specs=whole_spec((rows + EXTRA, order)),
        ),
        compiler_params=pltpu.CompilerParams(vmem_limit_bytes=32 * 1024 * 1024),
        cost_estimate=FREE,
    )(flags, own, prev, separator, reciprocal)


def early_kernel(size, flags, prev_whole, prev_rows, own_rows, separator, *refs):
    sources = refs[: 2 * size - 1]
    link, partial, form, own_out, own, sems = refs[2 * size - 1 :]
    rows = separator.shape[0]
    step = pl.program_id(0)
    here = pl.ds(pl.multiple_of(step * WIDTH, WIDTH), WIDTH)

    def copies():
        for spot in range(size):
            for by, source in enumerate(sources):
                distance = (by + 1) // 2 if by % 2 else -(by // 2)
                target = own.at[pl.ds(spot * rows, rows)]
                copy = pltpu.make_async_copy(source, target, sems.at[spot])
                yield flags[1] - spot == distance, copy

    @pl.when(step == 0)
    def _():
        for chosen, copy in copies():
            pl.when(chosen)(copy.start)
        for chosen, copy in copies():
            pl.when(chosen)(copy.wait)

    block = own[here, :]
    own_out[...] = block
    link[...] = jnp.where(flags[0] == 1, 0.0, -dot_nt(prev_whole[...], block)).astype(BF16)
    partial[...] = separator[...] - dot_nt(own_rows[...], block)
    form[...] = dot_nt(prev_rows[...], prev_whole[here, :])


def early_forms(flags, prev_whole, prev_rows, own_rows, separator, sources):
    rows, order = own_rows.shape
    size = order // rows
    return pl.pallas_call(
        functools.partial(early_kernel, size),
        out_shape=[
            SHAPE((order, order), BF16),
            SHAPE((rows, order), F32),
            SHAPE((rows, order), F32),
            SHAPE((order, order), BF16),
        ],
        grid_spec=pltpu.PrefetchScalarGridSpec(
            num_scalar_prefetch=1,
            grid=(order // WIDTH,),
            in_specs=[
                whole_spec((order, order)),
                whole_spec((rows, order)),
                whole_spec((rows, order)),
                along_spec(rows),
            ]
            + [ANY] * len(sources),
            out_specs=[along_spec(order), along_spec(rows), along_spec(rows), down_spec(order)],
            scratch_shapes=[pltpu.VMEM((order, order), BF16), pltpu.SemaphoreType.DMA((size,))],
        ),
        compiler_params=pltpu.CompilerParams(vmem_limit_bytes=32 * 1024 * 1024),
        cost_estimate=FREE,
    )(flags, prev_whole, prev_rows, own_rows, separator, *sources)


def late_kernel(
    size, flags, reciprocal, prev_rows, own, from_below, from_above, far, link, corner, raw, scaled, sem
):
    place = flags[1]
    rows = raw.shape[0]
    step = pl.program_id(0)
    width = own.shape[0]
    here = pl.ds(pl.multiple_of(step * width, width), width)

    @pl.when(step == 0)
    def _():
        for chosen, source in (
            (place == 0, from_above.at[pl.ds(0, rows)]),
            (place == size - 1, from_below.at[pl.ds(0, rows)]),
            (jnp.logical_and(place != 0, place != size - 1), far),
        ):
            copy = pltpu.make_async_copy(source, raw, sem)
            pl.when(chosen)(copy.start)
            pl.when(chosen)(copy.wait)
        scaled[...] = (raw[...].astype(F32) * reciprocal[0:1]).astype(BF16)
        corner[...] = dot_nt(prev_rows[...], scaled[...])

    link[:, here] = jnp.where(flags[0] == 1, 0.0, -dot_nt(scaled[...], own[...])).astype(BF16)


def late_forms(flags, reciprocal, prev_rows, own, from_below, from_above, far):
    rows, order = prev_rows.shape
    size = order // rows
    width = 512
    return pl.pallas_call(
        functools.partial(late_kernel, size),
        out_shape=[SHAPE((rows, order), BF16), SHAPE((rows, rows), F32)],
        grid_spec=pltpu.PrefetchScalarGridSpec(
            num_scalar_prefetch=1,
            grid=(order // width,),
            in_specs=[
                whole_spec((8, order)),
                whole_spec((rows, order)),
                pl.BlockSpec((width, order), lambda j, f: (j, 0)),
                ANY,
                ANY,
                ANY,
            ],
            out_specs=[whole_spec((rows, order)), whole_spec((rows, rows))],
            scratch_shapes=[
                pltpu.VMEM((rows, order), BF16),
                pltpu.VMEM((rows, order), BF16),
                pltpu.SemaphoreType.DMA,
            ],
        ),
        compiler_params=pltpu.CompilerParams(vmem_limit_bytes=20 * 1024 * 1024),
    )(flags, reciprocal, prev_rows, own, from_below, from_above, far)


def level_kernel(flags, link, mine, scale, pivot_scale, form, update, left_diag, right_diag):
    part = link[...]
    scaled = mine[...] * scale[0:1]
    keep = jnp.where(flags[2] == 1, 1.0, 0.0)
    update[...] = (form[...] + keep * dot_nt(scaled, part)).astype(BF16)
    square = part * part
    left_diag[...] = dot_nt(scale[...], square)

    @pl.when(pl.program_id(0) == 0)
    def _():
        right_diag[...] = jnp.zeros_like(right_diag)

    right_diag[...] += dot_nn(pivot_scale[...], square)


def level_forms(flags, link, scale, pivot_scale, form):
    rows, order = form.shape
    width = 512
    along = lambda count: pl.BlockSpec((count, width), lambda j, f: (0, j))
    return pl.pallas_call(
        level_kernel,
        out_shape=[SHAPE((rows, order), BF16), SHAPE((8, order), F32), SHAPE((8, order), F32)],
        grid_spec=pltpu.PrefetchScalarGridSpec(
            num_scalar_prefetch=1,
            grid=(order // width,),
            in_specs=[
                pl.BlockSpec((width, order), lambda j, f: (j, 0)),
                pl.BlockSpec((rows, order), lambda j, f: (f[1], 0)),
                whole_spec((8, order)),
                along(8),
                along(rows),
            ],
            out_specs=[along(rows), along(8), whole_spec((8, order))],
        ),
        compiler_params=pltpu.CompilerParams(vmem_limit_bytes=24 * 1024 * 1024),
    )(flags, link, link, scale, pivot_scale, form)


def on_device(sep_block, own_couple, prev_couple, inner_diag):
    separator = sep_block[0]
    own_rows = own_couple[0]
    prev_rows = prev_couple[0]
    reciprocal = 1.0 / inner_diag[0]
    rows, order = own_rows.shape
    place = lax.axis_index("space")
    size = lax.axis_size("space")
    row_start = place * rows
    partition = lax.axis_index("tm")
    parts = lax.axis_size("tm")

    def between(block, route):
        return lax.ppermute(block, "tm", [(a, b) for a, b in route if 0 <= b < parts])

    even = range(0, parts, 2)
    pivots = range(1, parts, 4)
    everyone = range(parts)

    def one_step(ahead, back, step):
        up = [(j, j + 1) for j in range(step - 1, size - 1)]
        down = [(j, j - 1) for j in range(1, size - step + 1)]
        return lax.ppermute(ahead, "space", up), lax.ppermute(back, "space", down)

    def block_at(arrived, spot):
        block = arrived[0][0]
        for step in range(1, len(arrived)):
            if spot + step < size:
                block = jnp.where(place == spot + step, arrived[step][0], block)
            if spot - step >= 0:
                block = jnp.where(place == spot - step, arrived[step][1], block)
        return block

    own_arrived = [(own_rows, own_rows)]
    own_arrived.append(one_step(own_rows, own_rows, 1))

    is_first = partition == 0
    is_pivot = partition % 2 == 0
    is_receiver = partition % 2 == 1
    is_last = partition % 4 == 3
    flags = jnp.stack([is_first.astype(jnp.int32), place, is_pivot.astype(jnp.int32)])
    prev_long = opening(flags, own_rows, prev_rows, separator, rows_of(reciprocal))
    long_arrived = [(prev_long, prev_long)]
    long_arrived.append(one_step(prev_long, prev_long, 1))
    for step in range(2, size):
        own_arrived.append(one_step(*own_arrived[-1], step))
        long_arrived.append(one_step(*long_arrived[-1], step))

    left_side = place < size // 2
    late_start = jnp.where(left_side, size - 1, 0) * rows
    is_end = jnp.logical_or(place == 0, place == size - 1)
    prev_arrived = [tuple(block[:rows] for block in pair) for pair in long_arrived[:-1]]
    words_arrived = [tuple(block[rows:] for block in pair) for pair in long_arrived[:-1]]
    prev_blocks = [block_at(prev_arrived, spot) for spot in range(size)]
    zero = jnp.zeros_like(prev_rows)
    prev_blocks[0] = jnp.where(place == size - 1, zero, prev_blocks[0])
    prev_blocks[-1] = jnp.where(place == 0, zero, prev_blocks[-1])
    prev_first = jnp.concatenate(prev_blocks)
    prev_far = jnp.where(left_side, prev_blocks[-1], prev_blocks[0])
    words = [block_at(words_arrived, spot) for spot in range(size)]
    none = jnp.zeros_like(words[0])
    words[0] = jnp.where(place == size - 1, none, words[0])
    words[-1] = jnp.where(place == 0, none, words[-1])

    def pair_sum(block, at):
        return block[at].astype(F32) + block[at + 1].astype(F32)

    sep_diag = sum(pair_sum(block, 0) for block in words)
    own_diag = jnp.concatenate([pair_sum(block, 2)[:rows] for block in words])
    prev_diag = jnp.concatenate([pair_sum(block, 4)[:rows] for block in words])
    prev_first, prev_far, sep_diag, own_diag, prev_diag = lax.optimization_barrier(
        (prev_first, prev_far, sep_diag, own_diag, prev_diag)
    )

    own_scaled = scaled_by(own_rows, reciprocal)
    sources = [own_rows]
    for up, down in own_arrived[1:]:
        sources += [up, down]
    link, partial, prev_form, own_full = early_forms(
        flags, scaled_by(prev_first, reciprocal), prev_rows, own_scaled, separator, sources
    )

    from_below, from_above = long_arrived[-1]
    flags = after(flags, link)
    late, corner = late_forms(
        flags, rows_of(reciprocal), prev_rows, own_full, from_below, from_above, prev_far
    )
    end_words = jnp.where(flags[1] == 0, from_above[rows:], from_below[rows:])
    end_words = jnp.where(is_end, end_words, jnp.zeros_like(end_words))

    def with_end(diag, at):
        piece = pair_sum(end_words, at)[:rows]
        return lax.dynamic_update_slice_in_dim(
            diag, piece + lax.dynamic_slice_in_dim(diag, late_start, rows, 0), late_start, 0
        )

    part_diag = sep_diag + pair_sum(end_words, 0) - with_end(own_diag, 2)
    prev_diag = with_end(prev_diag, 4)
    diag = part_diag - between(prev_diag, [(p, p - 1) for p in everyone])
    pivot_diag = between(part_diag, [(p, p + 1) for p in even]) - prev_diag
    scale = (1.0 / jnp.maximum(diag, 1.0)).astype(BF16)
    pivot_scale = (1.0 / jnp.maximum(pivot_diag, 1.0)).astype(BF16)

    late_at = after(jnp.full((8, 128), late_start, jnp.int32), scale, pivot_scale)[0, 0]
    link = lax.dynamic_update_slice_in_dim(link, late, late_at, 0)
    pivot_link = between(link, [(p, p + 1) for p in even])

    prev_form = lax.dynamic_update_slice_in_dim(prev_form, corner, late_start, 1)
    update, left_diag, right_diag = level_forms(flags, link, rows_of(scale), rows_of(pivot_scale), prev_form)
    left_diag = between(left_diag[0], [(p, p - 1) for p in even])
    from_even = between(
        update, [(p, p - 1) for p in range(2, parts, 4)] + [(p, p - 4) for p in range(4, parts, 4)]
    )
    from_odd = between(update, [(p, p - 1) for p in range(1, parts, 2)])
    next_diag = diag - left_diag - right_diag[0]
    next_scale = (1.0 / jnp.maximum(next_diag, 1.0)).astype(BF16)
    pivot_rows = lax.dynamic_slice_in_dim(pivot_link, row_start, rows, 0)
    pivot_rows = lax.optimization_barrier(scaled_by(pivot_rows, pivot_scale))
    next_rows = (-dot_nn(pivot_rows, link)).astype(BF16)
    pivot_rows = between(next_rows, [(p, p + 2) for p in pivots if p != 1])

    left_next = scaled_by(dot_nt(scaled_by(next_rows, next_scale), link), pivot_scale)
    left_next = (-dot_nt(left_next, pivot_link)).astype(BF16)
    from_pivot = between(left_next, [(p, p - 2) for p in pivots])

    next_pivot_scale = between(after(next_scale, left_next), [(p, p + 2) for p in pivots])
    go_on = after(jnp.ones((8, 128), jnp.int32), left_next)[0, 0] == 1
    passed_on = jnp.where(go_on, from_even, jnp.zeros_like(from_even))
    from_far = between(passed_on, [(p - 4, p - 1) for p in range(4, parts, 4)])
    pivot_scale = after(pivot_scale, left_next)
    link_cols = lax.dynamic_slice_in_dim(link, row_start, rows, 1).T
    right = lax.optimization_barrier(scaled_by(link_cols, pivot_scale))
    next_cols = (-dot_nt(right, pivot_link)).astype(BF16)
    both = jnp.concatenate([next_cols, pivot_rows])
    both = lax.optimization_barrier(scaled_by(both, next_pivot_scale))
    both = dot_nn(both, pivot_link) * pivot_scale.astype(F32)[None, :]
    right = jnp.where(is_last, right.astype(F32) - both[:rows], right.astype(F32))
    both = lax.optimization_barrier(jnp.concatenate([right, both[rows:]]).astype(BF16))
    both = lax.optimization_barrier(dot_nn(both, link))
    link_rows = lax.dynamic_slice_in_dim(link, row_start, rows, 0)
    out_link = jnp.where(is_last, both[rows:].astype(BF16), jnp.where(is_receiver, next_rows, link_rows))
    from_even = jnp.where(is_receiver, from_even + from_far, jnp.zeros_like(from_even))
    from_later = (from_even + from_odd).astype(F32) + from_pivot.astype(F32)
    schur = partial - jnp.where(is_receiver, both[:rows], 0.0) - from_later
    return (schur[None], out_link[None])


def solution(mesh):
    placed = (P("tm", "space", None), P("tm", "space", None), P("tm", "space", None), P("tm", None))
    return jax.shard_map(
        on_device,
        mesh=mesh,
        in_specs=placed,
        out_specs=(P("tm", "space", None), P("tm", "space", None)),
        check_vma=False,
    )
```

```python
import functools

import jax
import jax.numpy as jnp
from jax import lax
from jax.experimental import pallas as pl
from jax.experimental.pallas import tpu as pltpu
from jax.sharding import PartitionSpec as P

BF16 = jnp.bfloat16
F32 = jnp.float32
EXTRA = 16
WIDTH = 256

ANY = pl.BlockSpec(memory_space=pl.ANY)
SHAPE = jax.ShapeDtypeStruct
FREE = pl.CostEstimate(flops=0, bytes_accessed=0, transcendentals=0)


def after(block, *others):
    def body(*refs):
        del refs

    return pl.pallas_call(
        body,
        out_shape=SHAPE(block.shape, block.dtype),
        in_specs=[ANY] * (1 + len(others)),
        out_specs=ANY,
        input_output_aliases={0: 0},
    )(block, *others)


def scaled_by(matrix, factors):
    return (matrix.astype(F32) * factors.astype(F32)[None, :]).astype(BF16)


def row_scaled_by(matrix, factors):
    return (matrix.astype(F32) * factors.astype(F32)[:, None]).astype(BF16)


def dot_nt(left, right):
    return lax.dot_general(left, right, (((1,), (1,)), ((), ())), preferred_element_type=F32)


def dot_nn(left, right):
    return lax.dot_general(left, right, (((1,), (0,)), ((), ())), preferred_element_type=F32)


def dot_tn(left, right):
    return lax.dot_general(left, right, (((0,), (0,)), ((), ())), preferred_element_type=F32)


def rows_of(scale):
    return jnp.broadcast_to(scale[None, :], (8, scale.shape[0]))


def whole_spec(shape):
    return pl.BlockSpec(shape, lambda j, f: (0,) * len(shape))


def along_spec(count):
    return pl.BlockSpec((count, WIDTH), lambda j, f: (0, j))


def down_spec(count):
    return pl.BlockSpec((WIDTH, count), lambda j, f: (j, 0))


def opening_kernel(flags, own, prev, separator, reciprocal, long):
    rows, order = own.shape
    row_ids = lax.broadcasted_iota(jnp.int32, (rows, order), 0) + flags[1] * rows
    col_ids = lax.broadcasted_iota(jnp.int32, (rows, order), 1)
    on_diagonal = jnp.where(row_ids == col_ids, separator[...], 0.0)
    ones = jnp.ones((8, order), BF16)

    def split(value):
        high = value.astype(BF16)
        return high, (value - high.astype(F32)).astype(BF16)

    def form_diagonal(block):
        wide = block.astype(F32)
        high, low = split((wide * reciprocal[0:1]).astype(BF16).astype(F32) * wide)
        return (dot_nt(ones, high) + dot_nt(ones, low))[0:1]

    def placed(words, count):
        ids = lax.broadcasted_iota(jnp.int32, (EXTRA, count), 0)
        total = jnp.zeros((EXTRA, count), F32)
        for at, word in words.items():
            total = jnp.where(ids == at, word.astype(F32), total)
        return total.astype(BF16)

    long[0:rows, :] = prev[...]
    high, low = split(jnp.sum(on_diagonal, axis=0, keepdims=True))
    long[rows:, :] = placed({0: high, 1: low}, order)
    own_high, own_low = split(form_diagonal(own[...]))
    prev_high, prev_low = split(form_diagonal(prev[...]))
    local = placed({2: own_high, 3: own_low, 4: prev_high, 5: prev_low}, rows)
    long[rows:, 0:rows] = long[rows:, 0:rows] + local


def opening(flags, own, prev, separator, reciprocal):
    rows, order = own.shape
    return pl.pallas_call(
        opening_kernel,
        out_shape=SHAPE((rows + EXTRA, order), BF16),
        grid_spec=pltpu.PrefetchScalarGridSpec(
            num_scalar_prefetch=1,
            grid=(1,),
            in_specs=[whole_spec((rows, order))] * 3 + [whole_spec((8, order))],
            out_specs=whole_spec((rows + EXTRA, order)),
        ),
        compiler_params=pltpu.CompilerParams(vmem_limit_bytes=32 * 1024 * 1024),
        cost_estimate=FREE,
    )(flags, own, prev, separator, reciprocal)


def early_kernel(size, flags, prev_whole, prev_rows, own_rows, separator, plain_rows, *refs):
    sources = refs[: 2 * size - 1]
    link, partial, form, own_out, across, mine, own, sems = refs[2 * size - 1 :]
    rows = separator.shape[0]
    step = pl.program_id(0)
    here = pl.ds(pl.multiple_of(step * WIDTH, WIDTH), WIDTH)

    def copies():
        for spot in range(size):
            for by, source in enumerate(sources):
                distance = (by + 1) // 2 if by % 2 else -(by // 2)
                target = own.at[pl.ds(spot * rows, rows)]
                copy = pltpu.make_async_copy(source.at[pl.ds(0, rows)], target, sems.at[spot])
                yield flags[1] - spot == distance, copy

    @pl.when(step == 0)
    def _():
        for chosen, copy in copies():
            pl.when(chosen)(copy.start)
        for chosen, copy in copies():
            pl.when(chosen)(copy.wait)

    block = own[here, :]
    own_out[...] = block
    link[...] = jnp.where(flags[0] == 1, 0.0, -dot_nt(prev_whole[...], block)).astype(BF16)
    mine[...] = link[pl.ds(pl.multiple_of(flags[1] * rows, rows), rows), :]
    partial[...] = separator[...] - dot_nt(own_rows[...], block)
    prev_block = prev_whole[here, :]
    form[...] = dot_nt(prev_rows[...], prev_block)
    across[...] = jnp.where(flags[0] == 1, 0.0, -dot_nt(plain_rows[...], prev_block)).astype(BF16)


def early_forms(flags, prev_whole, prev_rows, own_rows, separator, plain_rows, sources):
    rows, order = own_rows.shape
    size = order // rows
    return pl.pallas_call(
        functools.partial(early_kernel, size),
        out_shape=[
            SHAPE((order, order), BF16),
            SHAPE((rows, order), F32),
            SHAPE((rows, order), F32),
            SHAPE((order, order), BF16),
            SHAPE((rows, order), BF16),
            SHAPE((rows, order), BF16),
        ],
        grid_spec=pltpu.PrefetchScalarGridSpec(
            num_scalar_prefetch=1,
            grid=(order // WIDTH,),
            in_specs=[
                whole_spec((order, order)),
                whole_spec((rows, order)),
                whole_spec((rows, order)),
                along_spec(rows),
                whole_spec((rows, order)),
            ]
            + [ANY] * len(sources),
            out_specs=[along_spec(order), along_spec(rows), along_spec(rows), down_spec(order), along_spec(rows), along_spec(rows)],
            scratch_shapes=[pltpu.VMEM((order, order), BF16), pltpu.SemaphoreType.DMA((size,))],
        ),
        compiler_params=pltpu.CompilerParams(vmem_limit_bytes=32 * 1024 * 1024),
        cost_estimate=FREE,
    )(flags, prev_whole, prev_rows, own_rows, separator, plain_rows, *sources)


def late_kernel(
    size, flags, reciprocal, prev_rows, plain_rows, mine, own, scale, late_scale, from_below, from_above, far,
    ready, link, corner, across, left_diag, right_diag, raw, scaled, sem,
):
    del ready
    place = flags[1]
    step = pl.program_id(0)
    width = own.shape[0]
    here = pl.ds(pl.multiple_of(step * width, width), width)

    @pl.when(step == 0)
    def _():
        for chosen, source in (
            (place == 0, from_above),
            (place == size - 1, from_below),
            (jnp.logical_and(place != 0, place != size - 1), far),
        ):
            copy = pltpu.make_async_copy(source, raw, sem)
            pl.when(chosen)(copy.start)
            pl.when(chosen)(copy.wait)
        scaled[...] = (raw[...].astype(F32) * reciprocal[0:1]).astype(BF16)
        across[...] = jnp.where(flags[0] == 1, 0.0, -dot_nt(plain_rows[...], scaled[...])).astype(BF16)

    link[:, here] = jnp.where(flags[0] == 1, 0.0, -dot_nt(scaled[...], own[...])).astype(BF16)

    @pl.when(step == pl.num_programs(0) - 1)
    def _():
        late = link[...]
        square = late * late
        keep = jnp.where(flags[2] == 1, 1.0, 0.0)
        ours = mine[...] * scale[0:1]
        corner[...] = (dot_nt(prev_rows[...], scaled[...]) + keep * dot_nt(ours, late)).astype(BF16)
        left_diag[...] = dot_nt(scale[...], square)
        right_diag[...] = dot_nn(late_scale[...], square)


def late_forms(
    flags, reciprocal, prev_rows, plain_rows, mine, own, scale, late_scale, from_below, from_above, far, ready
):
    rows, order = prev_rows.shape
    size = order // rows
    width = 512
    return pl.pallas_call(
        functools.partial(late_kernel, size),
        out_shape=[
            SHAPE((rows, order), BF16),
            SHAPE((rows, rows), BF16),
            SHAPE((rows, rows), BF16),
            SHAPE((8, rows), F32),
            SHAPE((8, order), F32),
        ],
        grid_spec=pltpu.PrefetchScalarGridSpec(
            num_scalar_prefetch=1,
            grid=(order // width,),
            in_specs=[
                whole_spec((8, order)),
                whole_spec((rows, order)),
                whole_spec((rows, order)),
                whole_spec((rows, order)),
                pl.BlockSpec((width, order), lambda j, f: (j, 0)),
                whole_spec((8, order)),
                whole_spec((8, rows)),
                ANY,
                ANY,
                ANY,
                ANY,
            ],
            out_specs=[
                whole_spec((rows, order)),
                whole_spec((rows, rows)),
                whole_spec((rows, rows)),
                whole_spec((8, rows)),
                whole_spec((8, order)),
            ],
            scratch_shapes=[
                pltpu.VMEM((rows, order), BF16),
                pltpu.VMEM((rows, order), BF16),
                pltpu.SemaphoreType.DMA,
            ],
        ),
        compiler_params=pltpu.CompilerParams(vmem_limit_bytes=24 * 1024 * 1024),
    )(
        flags, reciprocal, prev_rows, plain_rows, mine, own, scale, late_scale, from_below, from_above, far,
        ready,
    )


def level_kernel(flags, link, mine, scale, pivot_scale, form, update, left_diag, right_diag):
    part = link[...]
    scaled = mine[...] * scale[0:1]
    keep = jnp.where(flags[2] == 1, 1.0, 0.0)
    update[...] = (form[...] + keep * dot_nt(scaled, part)).astype(BF16)
    square = part * part
    left_diag[...] = dot_nt(scale[...], square)

    @pl.when(pl.program_id(0) == 0)
    def _():
        right_diag[...] = jnp.zeros_like(right_diag)

    right_diag[...] += dot_nn(pivot_scale[...], square)


def level_forms(flags, link, mine, scale, pivot_scale, form):
    rows, order = form.shape
    width = 512
    along = lambda count: pl.BlockSpec((count, width), lambda j, f: (0, j))
    return pl.pallas_call(
        level_kernel,
        out_shape=[SHAPE((rows, order), BF16), SHAPE((8, order), F32), SHAPE((8, order), F32)],
        grid_spec=pltpu.PrefetchScalarGridSpec(
            num_scalar_prefetch=1,
            grid=(order // width,),
            in_specs=[
                pl.BlockSpec((width, order), lambda j, f: (j, 0)),
                whole_spec((rows, order)),
                whole_spec((8, order)),
                along(8),
                along(rows),
            ],
            out_specs=[along(rows), along(8), whole_spec((8, order))],
        ),
        compiler_params=pltpu.CompilerParams(vmem_limit_bytes=24 * 1024 * 1024),
        cost_estimate=FREE,
    )(flags, link, mine, scale, pivot_scale, form)


def on_device(sep_block, own_couple, prev_couple, inner_diag):
    separator = sep_block[0]
    own_rows = own_couple[0]
    prev_rows = prev_couple[0]
    reciprocal = 1.0 / inner_diag[0]
    rows, order = own_rows.shape
    place = lax.axis_index("space")
    size = lax.axis_size("space")
    row_start = place * rows
    partition = lax.axis_index("tm")
    parts = lax.axis_size("tm")

    def between(block, route):
        return lax.ppermute(block, "tm", [(a, b) for a, b in route if 0 <= b < parts])

    even = range(0, parts, 2)
    pivots = range(1, parts, 4)
    everyone = range(parts)

    def one_step(ahead, back, step):
        up = [(j, j + 1) for j in range(step - 1, size - 1)]
        down = [(j, j - 1) for j in range(1, size - step + 1)]
        return lax.ppermute(ahead, "space", up), lax.ppermute(back, "space", down)

    def block_at(arrived, spot):
        block = arrived[0][0]
        for step in range(1, len(arrived)):
            if spot + step < size:
                block = jnp.where(place == spot + step, arrived[step][0], block)
            if spot - step >= 0:
                block = jnp.where(place == spot - step, arrived[step][1], block)
        return block

    own_arrived = [(own_rows, own_rows)]
    own_arrived.append(one_step(own_rows, own_rows, 1))

    is_first = partition == 0
    is_pivot = partition % 2 == 0
    is_receiver = partition % 2 == 1
    is_last = partition % 4 == 3
    flags = jnp.stack([is_first.astype(jnp.int32), place, is_pivot.astype(jnp.int32)])
    prev_long = opening(flags, own_rows, prev_rows, separator, rows_of(reciprocal))
    words = prev_long[rows:]
    prev_long = one_step(prev_long, prev_long, 1)
    prev_arrived = [(prev_rows, prev_rows), tuple(block[:rows] for block in prev_long)]
    words_arrived = [(words, words), tuple(block[rows:] for block in prev_long)]
    own_long = [jnp.concatenate(pair) for pair in zip(own_arrived[1], words_arrived[1])]
    for step in range(2, size):
        prev_arrived.append(one_step(*prev_arrived[-1], step))
        own_long = one_step(*own_long, step)
        own_arrived.append(own_long)
        words_arrived.append(tuple(block[rows:] for block in own_long))

    left_side = place < size // 2
    late_start = jnp.where(left_side, size - 1, 0) * rows
    is_end = jnp.logical_or(place == 0, place == size - 1)
    prev_blocks = [block_at(prev_arrived[:-1], spot) for spot in range(size)]
    zero = jnp.zeros_like(prev_rows)
    prev_blocks[0] = jnp.where(place == size - 1, zero, prev_blocks[0])
    prev_blocks[-1] = jnp.where(place == 0, zero, prev_blocks[-1])
    prev_first = jnp.concatenate(prev_blocks)
    prev_far = jnp.where(left_side, prev_blocks[-1], prev_blocks[0])
    prev_first, prev_far = lax.optimization_barrier((prev_first, prev_far))
    words = [block_at(words_arrived, spot) for spot in range(size)]

    def pair_sum(block, at):
        return block[at].astype(F32) + block[at + 1].astype(F32)

    part_diag = sum(pair_sum(block, 0) for block in words)
    part_diag = part_diag - jnp.concatenate([pair_sum(block, 2)[:rows] for block in words])
    prev_diag = jnp.concatenate([pair_sum(block, 4)[:rows] for block in words])
    diag = part_diag - between(prev_diag, [(p, p - 1) for p in everyone])
    pivot_diag = between(part_diag, [(p, p + 1) for p in even]) - prev_diag
    scale = (1.0 / jnp.maximum(diag, 1.0)).astype(BF16)
    pivot_scale = (1.0 / jnp.maximum(pivot_diag, 1.0)).astype(BF16)

    own_scaled = scaled_by(own_rows, reciprocal)
    sources = [own_rows]
    for up, down in own_arrived[1:]:
        sources += [up, down]
    link, partial, prev_form, own_full, across, mine = early_forms(
        flags, scaled_by(prev_first, reciprocal), prev_rows, own_scaled, separator, own_rows, sources
    )
    scale8, pivot_scale8 = rows_of(scale), rows_of(pivot_scale)
    update, left_diag, right_diag = level_forms(flags, link, mine, scale8, pivot_scale8, prev_form)

    from_below, from_above = prev_arrived[-1]
    late_scale = lax.dynamic_slice_in_dim(pivot_scale, late_start, rows, 0)
    late_scale = jnp.where(is_end, late_scale, jnp.zeros_like(late_scale))
    late, corner, across_late, left_late, right_late = late_forms(
        flags, rows_of(reciprocal), prev_rows, own_rows, mine, own_full, scale8, rows_of(late_scale),
        from_below, from_above, prev_far, right_diag,
    )
    link = lax.dynamic_update_slice_in_dim(link, late, late_start, 0)
    pivot_link = between(link, [(p, p + 1) for p in even])
    update = lax.dynamic_update_slice_in_dim(update, corner, late_start, 1)
    left_diag = lax.dynamic_update_slice_in_dim(left_diag[0], left_late[0], late_start, 0)
    right_diag = right_diag[0] + right_late[0]

    left_diag = between(left_diag, [(p, p - 1) for p in even])
    from_even = between(
        update, [(p, p - 1) for p in range(2, parts, 4)] + [(p, p - 4) for p in range(4, parts, 4)]
    )
    from_odd = between(update, [(p, p - 1) for p in range(1, parts, 2)])
    next_diag = diag - left_diag - right_diag
    next_scale = (1.0 / jnp.maximum(next_diag, 1.0)).astype(BF16)
    pivot_rows = lax.dynamic_slice_in_dim(pivot_link, row_start, rows, 0)
    pivot_rows = lax.optimization_barrier(scaled_by(pivot_rows, pivot_scale))
    next_rows = (-dot_nn(pivot_rows, link)).astype(BF16)
    pivot_rows = between(next_rows, [(p, p + 2) for p in pivots if p != 1])

    left_next = scaled_by(dot_nt(scaled_by(next_rows, next_scale), link), pivot_scale)
    left_next = lax.optimization_barrier(left_next)
    left_next = (-dot_nt(left_next, pivot_link)).astype(BF16)
    from_pivot = between(left_next, [(p, p - 2) for p in pivots])

    next_pivot_scale = between(after(next_scale, left_next), [(p, p + 2) for p in pivots])
    go_on = after(jnp.ones((8, 128), jnp.int32), left_next)[0, 0] == 1
    passed_on = jnp.where(go_on, from_even, jnp.zeros_like(from_even))
    from_far = between(passed_on, [(p - 4, p - 1) for p in range(4, parts, 4)])
    pivot_scale = after(pivot_scale, left_next, pivot_rows)
    across = lax.dynamic_update_slice_in_dim(across, across_late, late_start, 1)
    right = lax.optimization_barrier(scaled_by(across, pivot_scale))
    next_cols = (-dot_nt(right, pivot_link)).astype(BF16)
    both = jnp.concatenate([next_cols, pivot_rows])
    both = lax.optimization_barrier(scaled_by(both, next_pivot_scale))
    both = dot_nn(both, pivot_link) * pivot_scale.astype(F32)[None, :]
    right = jnp.where(is_last, right.astype(F32) - both[:rows], right.astype(F32))
    both = lax.optimization_barrier(jnp.concatenate([right, both[rows:]]).astype(BF16))
    both = lax.optimization_barrier(dot_nn(both, link))
    link_rows = lax.dynamic_slice_in_dim(link, row_start, rows, 0)
    out_link = jnp.where(is_last, both[rows:].astype(BF16), jnp.where(is_receiver, next_rows, link_rows))
    from_even = jnp.where(is_receiver, from_even + from_far, jnp.zeros_like(from_even))
    from_later = (from_even + from_odd).astype(F32) + from_pivot.astype(F32)
    schur = partial - jnp.where(is_receiver, both[:rows], 0.0) - from_later
    return (schur[None], out_link[None])


def solution(mesh):
    placed = (P("tm", "space", None), P("tm", "space", None), P("tm", "space", None), P("tm", None))
    return jax.shard_map(
        on_device,
        mesh=mesh,
        in_specs=placed,
        out_specs=(P("tm", "space", None), P("tm", "space", None)),
        check_vma=False,
    )
```

```python
import functools

import jax
import jax.numpy as jnp
from jax import lax
from jax.experimental import pallas as pl
from jax.experimental.pallas import tpu as pltpu
from jax.sharding import PartitionSpec as P

BF16 = jnp.bfloat16
F32 = jnp.float32
EXTRA = 16
WIDTH = 256

ANY = pl.BlockSpec(memory_space=pl.ANY)
SHAPE = jax.ShapeDtypeStruct
FREE = pl.CostEstimate(flops=0, bytes_accessed=0, transcendentals=0)


def after(block, *others):
    def body(*refs):
        del refs

    return pl.pallas_call(
        body,
        out_shape=SHAPE(block.shape, block.dtype),
        in_specs=[ANY] * (1 + len(others)),
        out_specs=ANY,
        input_output_aliases={0: 0},
    )(block, *others)


def scaled_by(matrix, factors):
    return (matrix.astype(F32) * factors.astype(F32)[None, :]).astype(BF16)


def row_scaled_by(matrix, factors):
    return (matrix.astype(F32) * factors.astype(F32)[:, None]).astype(BF16)


def dot_nt(left, right):
    return lax.dot_general(left, right, (((1,), (1,)), ((), ())), preferred_element_type=F32)


def dot_nn(left, right):
    return lax.dot_general(left, right, (((1,), (0,)), ((), ())), preferred_element_type=F32)


def dot_tn(left, right):
    return lax.dot_general(left, right, (((0,), (0,)), ((), ())), preferred_element_type=F32)


def rows_of(scale):
    return jnp.broadcast_to(scale[None, :], (8, scale.shape[0]))


def whole_spec(shape):
    return pl.BlockSpec(shape, lambda j, f: (0,) * len(shape), pipeline_mode=pl.Buffered(1))


def along_spec(count):
    return pl.BlockSpec((count, WIDTH), lambda j, f: (0, j))


def down_spec(count):
    return pl.BlockSpec((WIDTH, count), lambda j, f: (j, 0))


def opening_kernel(flags, own, prev, separator, reciprocal, long):
    rows, order = own.shape
    row_ids = lax.broadcasted_iota(jnp.int32, (rows, order), 0) + flags[1] * rows
    col_ids = lax.broadcasted_iota(jnp.int32, (rows, order), 1)
    on_diagonal = jnp.where(row_ids == col_ids, separator[...], 0.0)
    ones = jnp.ones((8, order), BF16)

    def split(value):
        high = value.astype(BF16)
        return high, (value - high.astype(F32)).astype(BF16)

    def form_diagonal(block):
        wide = block.astype(F32)
        high, low = split((wide * reciprocal[0:1]).astype(BF16).astype(F32) * wide)
        return (dot_nt(ones, high) + dot_nt(ones, low))[0:1]

    def placed(words, count):
        ids = lax.broadcasted_iota(jnp.int32, (EXTRA, count), 0)
        total = jnp.zeros((EXTRA, count), F32)
        for at, word in words.items():
            total = jnp.where(ids == at, word.astype(F32), total)
        return total.astype(BF16)

    long[0:rows, :] = own[...]
    high, low = split(jnp.sum(on_diagonal, axis=0, keepdims=True))
    long[rows:, :] = placed({0: high, 1: low}, order)
    own_high, own_low = split(form_diagonal(own[...]))
    prev_high, prev_low = split(form_diagonal(prev[...]))
    local = placed({2: own_high, 3: own_low, 4: prev_high, 5: prev_low}, rows)
    long[rows:, 0:rows] = long[rows:, 0:rows] + local


def opening(flags, own, prev, separator, reciprocal):
    rows, order = own.shape
    return pl.pallas_call(
        opening_kernel,
        out_shape=SHAPE((rows + EXTRA, order), BF16),
        grid_spec=pltpu.PrefetchScalarGridSpec(
            num_scalar_prefetch=1,
            grid=(1,),
            in_specs=[whole_spec((rows, order))] * 3 + [whole_spec((8, order))],
            out_specs=whole_spec((rows + EXTRA, order)),
        ),
        compiler_params=pltpu.CompilerParams(vmem_limit_bytes=32 * 1024 * 1024),
        cost_estimate=FREE,
    )(flags, own, prev, separator, reciprocal)


def early_kernel(size, flags, prev_whole, prev_rows, own_rows, separator, *refs):
    sources = refs[: 2 * size - 1]
    link, partial, form, own_out, mine, own, sems = refs[2 * size - 1 :]
    rows = separator.shape[0]
    step = pl.program_id(0)
    here = pl.ds(pl.multiple_of(step * WIDTH, WIDTH), WIDTH)

    def copies():
        for spot in range(size):
            for by, source in enumerate(sources):
                distance = (by + 1) // 2 if by % 2 else -(by // 2)
                target = own.at[pl.ds(spot * rows, rows)]
                copy = pltpu.make_async_copy(source.at[pl.ds(0, rows)], target, sems.at[spot])
                yield flags[1] - spot == distance, copy

    @pl.when(step == 0)
    def _():
        for chosen, copy in copies():
            pl.when(chosen)(copy.start)
        for chosen, copy in copies():
            pl.when(chosen)(copy.wait)

    block = own[here, :]
    own_out[...] = block
    link[...] = jnp.where(flags[0] == 1, 0.0, -dot_nt(prev_whole[...], block)).astype(BF16)
    mine[...] = link[pl.ds(pl.multiple_of(flags[1] * rows, rows), rows), :]
    partial[...] = separator[...] - dot_nt(own_rows[...], block)
    form[...] = dot_nt(prev_rows[...], prev_whole[here, :])


def early_forms(flags, prev_whole, prev_rows, own_rows, separator, sources):
    rows, order = own_rows.shape
    size = order // rows
    return pl.pallas_call(
        functools.partial(early_kernel, size),
        out_shape=[
            SHAPE((order, order), BF16),
            SHAPE((rows, order), F32),
            SHAPE((rows, order), F32),
            SHAPE((order, order), BF16),
            SHAPE((rows, order), BF16),
        ],
        grid_spec=pltpu.PrefetchScalarGridSpec(
            num_scalar_prefetch=1,
            grid=(order // WIDTH,),
            in_specs=[
                whole_spec((order, order)),
                whole_spec((rows, order)),
                whole_spec((rows, order)),
                along_spec(rows),
            ]
            + [ANY] * len(sources),
            out_specs=[along_spec(order), along_spec(rows), along_spec(rows), down_spec(order), along_spec(rows)],
            scratch_shapes=[pltpu.VMEM((order, order), BF16), pltpu.SemaphoreType.DMA((size,))],
        ),
        compiler_params=pltpu.CompilerParams(vmem_limit_bytes=26 * 1024 * 1024),
        cost_estimate=FREE,
    )(flags, prev_whole, prev_rows, own_rows, separator, *sources)


def late_kernel(
    size, flags, reciprocal, prev_rows, plain_rows, mine, own, scale, late_scale, from_below, from_above, far,
    ready, link, corner, across, left_diag, right_diag, raw, scaled, sem,
):
    del ready
    place = flags[1]
    step = pl.program_id(0)
    width = own.shape[0]
    here = pl.ds(pl.multiple_of(step * width, width), width)

    @pl.when(step == 0)
    def _():
        for chosen, source in (
            (place == 0, from_above),
            (place == size - 1, from_below),
            (jnp.logical_and(place != 0, place != size - 1), far),
        ):
            copy = pltpu.make_async_copy(source, raw, sem)
            pl.when(chosen)(copy.start)
            pl.when(chosen)(copy.wait)
        scaled[...] = (raw[...].astype(F32) * reciprocal[0:1]).astype(BF16)
        across[...] = jnp.where(flags[0] == 1, 0.0, -dot_nt(plain_rows[...], scaled[...])).astype(BF16)

    link[:, here] = jnp.where(flags[0] == 1, 0.0, -dot_nt(scaled[...], own[...])).astype(BF16)

    @pl.when(step == pl.num_programs(0) - 1)
    def _():
        late = link[...]
        square = late * late
        keep = jnp.where(flags[2] == 1, 1.0, 0.0)
        ours = mine[...] * scale[0:1]
        corner[...] = (dot_nt(prev_rows[...], scaled[...]) + keep * dot_nt(ours, late)).astype(BF16)
        left_diag[...] = dot_nt(scale[...], square)
        right_diag[...] = dot_nn(late_scale[...], square)


def late_forms(
    flags, reciprocal, prev_rows, plain_rows, mine, own, scale, late_scale, from_below, from_above, far, ready
):
    rows, order = prev_rows.shape
    size = order // rows
    width = 512
    return pl.pallas_call(
        functools.partial(late_kernel, size),
        out_shape=[
            SHAPE((rows, order), BF16),
            SHAPE((rows, rows), BF16),
            SHAPE((rows, rows), BF16),
            SHAPE((8, rows), F32),
            SHAPE((8, order), F32),
        ],
        grid_spec=pltpu.PrefetchScalarGridSpec(
            num_scalar_prefetch=1,
            grid=(order // width,),
            in_specs=[
                whole_spec((8, order)),
                whole_spec((rows, order)),
                whole_spec((rows, order)),
                whole_spec((rows, order)),
                pl.BlockSpec((width, order), lambda j, f: (j, 0)),
                whole_spec((8, order)),
                whole_spec((8, rows)),
                ANY,
                ANY,
                ANY,
                ANY,
            ],
            out_specs=[
                whole_spec((rows, order)),
                whole_spec((rows, rows)),
                whole_spec((rows, rows)),
                whole_spec((8, rows)),
                whole_spec((8, order)),
            ],
            scratch_shapes=[
                pltpu.VMEM((rows, order), BF16),
                pltpu.VMEM((rows, order), BF16),
                pltpu.SemaphoreType.DMA,
            ],
        ),
        compiler_params=pltpu.CompilerParams(vmem_limit_bytes=18 * 1024 * 1024),
    )(
        flags, reciprocal, prev_rows, plain_rows, mine, own, scale, late_scale, from_below, from_above, far,
        ready,
    )


def level_kernel(flags, link, mine, scale, pivot_scale, form, update, left_diag, right_diag):
    part = link[...]
    scaled = mine[...] * scale[0:1]
    keep = jnp.where(flags[2] == 1, 1.0, 0.0)
    update[...] = (form[...] + keep * dot_nt(scaled, part)).astype(BF16)
    square = part * part
    left_diag[...] = dot_nt(scale[...], square)

    @pl.when(pl.program_id(0) == 0)
    def _():
        right_diag[...] = jnp.zeros_like(right_diag)

    right_diag[...] += dot_nn(pivot_scale[...], square)


def level_forms(flags, link, mine, scale, pivot_scale, form):
    rows, order = form.shape
    width = 512
    along = lambda count: pl.BlockSpec((count, width), lambda j, f: (0, j))
    return pl.pallas_call(
        level_kernel,
        out_shape=[SHAPE((rows, order), BF16), SHAPE((8, order), F32), SHAPE((8, order), F32)],
        grid_spec=pltpu.PrefetchScalarGridSpec(
            num_scalar_prefetch=1,
            grid=(order // width,),
            in_specs=[
                pl.BlockSpec((width, order), lambda j, f: (j, 0)),
                whole_spec((rows, order)),
                whole_spec((8, order)),
                along(8),
                along(rows),
            ],
            out_specs=[along(rows), along(8), whole_spec((8, order))],
        ),
        compiler_params=pltpu.CompilerParams(vmem_limit_bytes=18 * 1024 * 1024),
        cost_estimate=FREE,
    )(flags, link, mine, scale, pivot_scale, form)


def on_device(sep_block, own_couple, prev_couple, inner_diag):
    separator = sep_block[0]
    own_rows = own_couple[0]
    prev_rows = prev_couple[0]
    reciprocal = 1.0 / inner_diag[0]
    rows, order = own_rows.shape
    place = lax.axis_index("space")
    size = lax.axis_size("space")
    row_start = place * rows
    partition = lax.axis_index("tm")
    parts = lax.axis_size("tm")

    def between(block, route):
        return lax.ppermute(block, "tm", [(a, b) for a, b in route if 0 <= b < parts])

    even = range(0, parts, 2)
    pivots = range(1, parts, 4)
    everyone = range(parts)

    def one_step(ahead, back, step):
        up = [(j, j + 1) for j in range(step - 1, size - 1)]
        down = [(j, j - 1) for j in range(1, size - step + 1)]
        return lax.ppermute(ahead, "space", up), lax.ppermute(back, "space", down)

    def block_at(arrived, spot):
        block = arrived[0][0]
        for step in range(1, len(arrived)):
            if spot + step < size:
                block = jnp.where(place == spot + step, arrived[step][0], block)
            if spot - step >= 0:
                block = jnp.where(place == spot - step, arrived[step][1], block)
        return block

    is_first = partition == 0
    is_pivot = partition % 2 == 0
    is_receiver = partition % 2 == 1
    is_last = partition % 4 == 3
    flags = jnp.stack([is_first.astype(jnp.int32), place, is_pivot.astype(jnp.int32)])
    own_long = opening(flags, own_rows, prev_rows, separator, rows_of(reciprocal))
    own_arrived = [(own_long, own_long)]
    prev_arrived = [(prev_rows, prev_rows)]
    for step in range(1, size):
        own_arrived.append(one_step(*own_arrived[-1], step))
        prev_arrived.append(one_step(*prev_arrived[-1], step))
    words_arrived = [tuple(block[rows:] for block in pair) for pair in own_arrived]

    left_side = place < size // 2
    late_start = jnp.where(left_side, size - 1, 0) * rows
    is_end = jnp.logical_or(place == 0, place == size - 1)
    prev_blocks = [block_at(prev_arrived[:-1], spot) for spot in range(size)]
    zero = jnp.zeros_like(prev_rows)
    prev_blocks[0] = jnp.where(place == size - 1, zero, prev_blocks[0])
    prev_blocks[-1] = jnp.where(place == 0, zero, prev_blocks[-1])
    prev_first = jnp.concatenate(prev_blocks)
    prev_far = jnp.where(left_side, prev_blocks[-1], prev_blocks[0])
    prev_first, prev_far = lax.optimization_barrier((prev_first, prev_far))
    words = [block_at(words_arrived, spot) for spot in range(size)]

    def pair_sum(block, at):
        return block[at].astype(F32) + block[at + 1].astype(F32)

    part_diag = sum(pair_sum(block, 0) for block in words)
    part_diag = part_diag - jnp.concatenate([pair_sum(block, 2)[:rows] for block in words])
    prev_diag = jnp.concatenate([pair_sum(block, 4)[:rows] for block in words])
    part_diag, prev_diag = lax.optimization_barrier((part_diag, prev_diag))
    diag = part_diag - between(prev_diag, [(p, p - 1) for p in everyone])
    pivot_diag = between(part_diag, [(p, p + 1) for p in even]) - prev_diag
    scale = (1.0 / jnp.maximum(diag, 1.0)).astype(BF16)
    pivot_scale = (1.0 / jnp.maximum(pivot_diag, 1.0)).astype(BF16)

    own_scaled = scaled_by(own_rows, reciprocal)
    sources = [own_long]
    for up, down in own_arrived[1:]:
        sources += [up, down]
    prev_first = scaled_by(prev_first, reciprocal)
    link, partial, prev_form, own_full, mine = early_forms(
        flags, prev_first, prev_rows, own_scaled, separator, sources
    )
    scale8, pivot_scale8 = rows_of(scale), rows_of(pivot_scale)
    update, left_diag, right_diag = level_forms(flags, link, mine, scale8, pivot_scale8, prev_form)

    from_below, from_above = prev_arrived[-1]
    late_scale = lax.dynamic_slice_in_dim(pivot_scale, late_start, rows, 0)
    late_scale = jnp.where(is_end, late_scale, jnp.zeros_like(late_scale))
    late, corner, across_late, left_late, right_late = late_forms(
        flags, rows_of(reciprocal), prev_rows, own_rows, mine, own_full, scale8, rows_of(late_scale),
        from_below, from_above, prev_far, right_diag,
    )
    link = lax.dynamic_update_slice_in_dim(link, late, late_start, 0)
    pivot_link = between(link, [(p, p + 1) for p in even])
    update = lax.dynamic_update_slice_in_dim(update, corner, late_start, 1)
    left_diag = lax.dynamic_update_slice_in_dim(left_diag[0], left_late[0], late_start, 0)
    right_diag = right_diag[0] + right_late[0]

    left_diag = between(left_diag, [(p, p - 1) for p in even])
    from_even = between(
        update, [(p, p - 1) for p in range(2, parts, 4)] + [(p, p - 4) for p in range(4, parts, 4)]
    )
    next_diag = diag - left_diag - right_diag
    next_scale = (1.0 / jnp.maximum(next_diag, 1.0)).astype(BF16)
    pivot_rows = lax.dynamic_slice_in_dim(pivot_link, row_start, rows, 0)
    pivot_rows = lax.optimization_barrier(scaled_by(pivot_rows, pivot_scale))
    next_rows = (-dot_nn(pivot_rows, link)).astype(BF16)
    pivot_rows = between(next_rows, [(p, p + 2) for p in pivots if p != 1])

    left_next = scaled_by(dot_nt(scaled_by(next_rows, next_scale), link), pivot_scale)
    left_next = lax.optimization_barrier(left_next)
    left_next = (-dot_nt(left_next, pivot_link)).astype(BF16)
    from_pivot = between(left_next, [(p, p - 2) for p in pivots])

    next_pivot_scale = between(after(next_scale, left_next), [(p, p + 2) for p in pivots])
    go_on = after(jnp.ones((8, 128), jnp.int32), left_next)[0, 0] == 1
    passed_on = jnp.where(go_on, from_even, jnp.zeros_like(from_even))
    own_update = jnp.where(go_on, update, jnp.zeros_like(update))
    from_odd = between(own_update, [(p, p - 1) for p in range(1, parts, 2)])
    from_far = between(passed_on, [(p - 4, p - 1) for p in range(4, parts, 4)])
    pivot_scale = after(pivot_scale, left_next, pivot_rows)
    across = jnp.where(go_on, own_rows, jnp.zeros_like(own_rows))
    across = (-dot_nt(across, prev_first)).astype(BF16)
    across = jnp.where(is_first, jnp.zeros_like(across), across)
    across = lax.dynamic_update_slice_in_dim(across, across_late, late_start, 1)
    right = lax.optimization_barrier(scaled_by(across, pivot_scale))
    next_cols = (-dot_nt(right, pivot_link)).astype(BF16)
    both = jnp.concatenate([next_cols, pivot_rows])
    both = lax.optimization_barrier(scaled_by(both, next_pivot_scale))
    both = dot_nn(both, pivot_link) * pivot_scale.astype(F32)[None, :]
    right = jnp.where(is_last, right.astype(F32) - both[:rows], right.astype(F32))
    both = lax.optimization_barrier(jnp.concatenate([right, both[rows:]]).astype(BF16))
    both = lax.optimization_barrier(dot_nn(both, link))
    link_rows = lax.dynamic_slice_in_dim(link, row_start, rows, 0)
    out_link = jnp.where(is_last, both[rows:].astype(BF16), jnp.where(is_receiver, next_rows, link_rows))
    from_even = jnp.where(is_receiver, from_even + from_far, jnp.zeros_like(from_even))
    from_later = (from_even + from_odd).astype(F32) + from_pivot.astype(F32)
    schur = partial - jnp.where(is_receiver, both[:rows], 0.0) - from_later
    return (schur[None], out_link[None])


def solution(mesh):
    placed = (P("tm", "space", None), P("tm", "space", None), P("tm", "space", None), P("tm", None))
    return jax.shard_map(
        on_device,
        mesh=mesh,
        in_specs=placed,
        out_specs=(P("tm", "space", None), P("tm", "space", None)),
        check_vma=False,
    )
```

```python
import functools

import jax
import jax.numpy as jnp
from jax import lax
from jax.experimental import pallas as pl
from jax.experimental.pallas import tpu as pltpu
from jax.sharding import PartitionSpec as P

BF16 = jnp.bfloat16
F32 = jnp.float32
EXTRA = 16
WIDTH = 256

ANY = pl.BlockSpec(memory_space=pl.ANY)
SHAPE = jax.ShapeDtypeStruct
FREE = pl.CostEstimate(flops=0, bytes_accessed=0, transcendentals=0)


def after(block, *others):
    def body(*refs):
        del refs

    return pl.pallas_call(
        body,
        out_shape=SHAPE(block.shape, block.dtype),
        in_specs=[ANY] * (1 + len(others)),
        out_specs=ANY,
        input_output_aliases={0: 0},
    )(block, *others)


def scaled_by(matrix, factors):
    return (matrix.astype(F32) * factors.astype(F32)[None, :]).astype(BF16)


def row_scaled_by(matrix, factors):
    return (matrix.astype(F32) * factors.astype(F32)[:, None]).astype(BF16)


def dot_nt(left, right):
    return lax.dot_general(left, right, (((1,), (1,)), ((), ())), preferred_element_type=F32)


def dot_nn(left, right):
    return lax.dot_general(left, right, (((1,), (0,)), ((), ())), preferred_element_type=F32)


def dot_tn(left, right):
    return lax.dot_general(left, right, (((0,), (0,)), ((), ())), preferred_element_type=F32)


def rows_of(scale):
    return jnp.broadcast_to(scale[None, :], (8, scale.shape[0]))


def whole_spec(shape):
    return pl.BlockSpec(shape, lambda j, f: (0,) * len(shape), pipeline_mode=pl.Buffered(1))


def along_spec(count):
    return pl.BlockSpec((count, WIDTH), lambda j, f: (0, j))


def down_spec(count):
    return pl.BlockSpec((WIDTH, count), lambda j, f: (j, 0))


def opening_kernel(flags, own, prev, separator, reciprocal, long):
    rows, order = own.shape
    row_ids = lax.broadcasted_iota(jnp.int32, (rows, order), 0) + flags[1] * rows
    col_ids = lax.broadcasted_iota(jnp.int32, (rows, order), 1)
    on_diagonal = jnp.where(row_ids == col_ids, separator[...], 0.0)
    ones = jnp.ones((8, order), BF16)

    def split(value):
        high = value.astype(BF16)
        return high, (value - high.astype(F32)).astype(BF16)

    def form_diagonal(block):
        wide = block.astype(F32)
        high, low = split((wide * reciprocal[0:1]).astype(BF16).astype(F32) * wide)
        return (dot_nt(ones, high) + dot_nt(ones, low))[0:1]

    def placed(words, count):
        ids = lax.broadcasted_iota(jnp.int32, (EXTRA, count), 0)
        total = jnp.zeros((EXTRA, count), F32)
        for at, word in words.items():
            total = jnp.where(ids == at, word.astype(F32), total)
        return total.astype(BF16)

    long[0:rows, :] = own[...]
    high, low = split(jnp.sum(on_diagonal, axis=0, keepdims=True))
    long[rows:, :] = placed({0: high, 1: low}, order)
    own_high, own_low = split(form_diagonal(own[...]))
    prev_high, prev_low = split(form_diagonal(prev[...]))
    local = placed({2: own_high, 3: own_low, 4: prev_high, 5: prev_low}, rows)
    long[rows:, 0:rows] = long[rows:, 0:rows] + local


def opening(flags, own, prev, separator, reciprocal):
    rows, order = own.shape
    return pl.pallas_call(
        opening_kernel,
        out_shape=SHAPE((rows + EXTRA, order), BF16),
        grid_spec=pltpu.PrefetchScalarGridSpec(
            num_scalar_prefetch=1,
            grid=(1,),
            in_specs=[whole_spec((rows, order))] * 3 + [whole_spec((8, order))],
            out_specs=whole_spec((rows + EXTRA, order)),
        ),
        compiler_params=pltpu.CompilerParams(vmem_limit_bytes=32 * 1024 * 1024),
        cost_estimate=FREE,
    )(flags, own, prev, separator, reciprocal)


def early_kernel(size, flags, prev_whole, prev_rows, own_rows, separator, *refs):
    sources = refs[: 2 * size - 1]
    link, partial, form, own_out, mine, own, sems = refs[2 * size - 1 :]
    rows = separator.shape[0]
    step = pl.program_id(0)
    here = pl.ds(pl.multiple_of(step * WIDTH, WIDTH), WIDTH)

    def copies():
        for spot in range(size):
            for by, source in enumerate(sources):
                distance = (by + 1) // 2 if by % 2 else -(by // 2)
                target = own.at[pl.ds(spot * rows, rows)]
                copy = pltpu.make_async_copy(source.at[pl.ds(0, rows)], target, sems.at[spot])
                yield flags[1] - spot == distance, copy

    @pl.when(step == 0)
    def _():
        for chosen, copy in copies():
            pl.when(chosen)(copy.start)
        for chosen, copy in copies():
            pl.when(chosen)(copy.wait)

    block = own[here, :]
    own_out[...] = block
    link[...] = jnp.where(flags[0] == 1, 0.0, -dot_nt(prev_whole[...], block)).astype(BF16)
    mine[...] = link[pl.ds(pl.multiple_of(flags[1] * rows, rows), rows), :]
    partial[...] = separator[...] - dot_nt(own_rows[...], block)
    form[...] = dot_nt(prev_rows[...], prev_whole[here, :])


def early_forms(flags, prev_whole, prev_rows, own_rows, separator, sources):
    rows, order = own_rows.shape
    size = order // rows
    return pl.pallas_call(
        functools.partial(early_kernel, size),
        out_shape=[
            SHAPE((order, order), BF16),
            SHAPE((rows, order), F32),
            SHAPE((rows, order), F32),
            SHAPE((order, order), BF16),
            SHAPE((rows, order), BF16),
        ],
        grid_spec=pltpu.PrefetchScalarGridSpec(
            num_scalar_prefetch=1,
            grid=(order // WIDTH,),
            in_specs=[
                whole_spec((order, order)),
                whole_spec((rows, order)),
                whole_spec((rows, order)),
                along_spec(rows),
            ]
            + [ANY] * len(sources),
            out_specs=[along_spec(order), along_spec(rows), along_spec(rows), down_spec(order), along_spec(rows)],
            scratch_shapes=[pltpu.VMEM((order, order), BF16), pltpu.SemaphoreType.DMA((size,))],
        ),
        compiler_params=pltpu.CompilerParams(vmem_limit_bytes=26 * 1024 * 1024),
        cost_estimate=FREE,
    )(flags, prev_whole, prev_rows, own_rows, separator, *sources)


def late_kernel(
    size, flags, reciprocal, prev_rows, mine, own, scale, late_scale, from_below, from_above, far,
    ready, link, corner, scaled, left_diag, right_diag, raw, sem,
):
    del ready
    place = flags[1]
    step = pl.program_id(0)
    width = own.shape[0]
    here = pl.ds(pl.multiple_of(step * width, width), width)

    @pl.when(step == 0)
    def _():
        for chosen, source in (
            (place == 0, from_above),
            (place == size - 1, from_below),
            (jnp.logical_and(place != 0, place != size - 1), far),
        ):
            copy = pltpu.make_async_copy(source, raw, sem)
            pl.when(chosen)(copy.start)
            pl.when(chosen)(copy.wait)
        scaled[...] = (raw[...].astype(F32) * reciprocal[0:1]).astype(BF16)

    link[:, here] = jnp.where(flags[0] == 1, 0.0, -dot_nt(scaled[...], own[...])).astype(BF16)

    @pl.when(step == pl.num_programs(0) - 1)
    def _():
        late = link[...]
        square = late * late
        keep = jnp.where(flags[2] == 1, 1.0, 0.0)
        ours = mine[...] * scale[0:1]
        corner[...] = (dot_nt(prev_rows[...], scaled[...]) + keep * dot_nt(ours, late)).astype(BF16)
        left_diag[...] = dot_nt(scale[...], square)
        right_diag[...] = dot_nn(late_scale[...], square)


def late_forms(
    flags, reciprocal, prev_rows, mine, own, scale, late_scale, from_below, from_above, far, ready
):
    rows, order = prev_rows.shape
    size = order // rows
    width = 512
    return pl.pallas_call(
        functools.partial(late_kernel, size),
        out_shape=[
            SHAPE((rows, order), BF16),
            SHAPE((rows, rows), BF16),
            SHAPE((rows, order), BF16),
            SHAPE((8, rows), F32),
            SHAPE((8, order), F32),
        ],
        grid_spec=pltpu.PrefetchScalarGridSpec(
            num_scalar_prefetch=1,
            grid=(order // width,),
            in_specs=[
                whole_spec((8, order)),
                whole_spec((rows, order)),
                whole_spec((rows, order)),
                pl.BlockSpec((width, order), lambda j, f: (j, 0)),
                whole_spec((8, order)),
                whole_spec((8, rows)),
                ANY,
                ANY,
                ANY,
                ANY,
            ],
            out_specs=[
                whole_spec((rows, order)),
                whole_spec((rows, rows)),
                whole_spec((rows, order)),
                whole_spec((8, rows)),
                whole_spec((8, order)),
            ],
            scratch_shapes=[pltpu.VMEM((rows, order), BF16), pltpu.SemaphoreType.DMA],
        ),
        compiler_params=pltpu.CompilerParams(vmem_limit_bytes=18 * 1024 * 1024),
    )(
        flags, reciprocal, prev_rows, mine, own, scale, late_scale, from_below, from_above, far, ready
    )


def level_kernel(flags, link, mine, scale, pivot_scale, form, update, left_diag, right_diag):
    part = link[...]
    scaled = mine[...] * scale[0:1]
    keep = jnp.where(flags[2] == 1, 1.0, 0.0)
    update[...] = (form[...] + keep * dot_nt(scaled, part)).astype(BF16)
    square = part * part
    left_diag[...] = dot_nt(scale[...], square)

    @pl.when(pl.program_id(0) == 0)
    def _():
        right_diag[...] = jnp.zeros_like(right_diag)

    right_diag[...] += dot_nn(pivot_scale[...], square)


def level_forms(flags, link, mine, scale, pivot_scale, form):
    rows, order = form.shape
    width = 512
    along = lambda count: pl.BlockSpec((count, width), lambda j, f: (0, j))
    return pl.pallas_call(
        level_kernel,
        out_shape=[SHAPE((rows, order), BF16), SHAPE((8, order), F32), SHAPE((8, order), F32)],
        grid_spec=pltpu.PrefetchScalarGridSpec(
            num_scalar_prefetch=1,
            grid=(order // width,),
            in_specs=[
                pl.BlockSpec((width, order), lambda j, f: (j, 0)),
                whole_spec((rows, order)),
                whole_spec((8, order)),
                along(8),
                along(rows),
            ],
            out_specs=[along(rows), along(8), whole_spec((8, order))],
        ),
        compiler_params=pltpu.CompilerParams(vmem_limit_bytes=18 * 1024 * 1024),
        cost_estimate=FREE,
    )(flags, link, mine, scale, pivot_scale, form)


def fetched(early, late, whole, sems, at):
    rows, order = late.shape
    size = order // rows
    place = at[0]
    low = place < size // 2
    spans = [pl.ds(spot * rows, rows) for spot in range(size)]
    copies = []
    for spot, span in enumerate(spans):
        plain = pltpu.make_async_copy(early.at[span], whole.at[span], sems.at[spot])
        if spot not in (0, size - 1):
            copies.append((True, plain))
            continue
        is_late = low if spot else jnp.logical_not(low)
        copies.append((jnp.logical_not(is_late), plain))
        copies.append((is_late, pltpu.make_async_copy(late, whole.at[span], sems.at[spot])))
    for chosen, copy in copies:
        pl.when(chosen)(copy.start) if chosen is not True else copy.start()

    def wait():
        for chosen, copy in copies:
            pl.when(chosen)(copy.wait) if chosen is not True else copy.wait()

    return wait


def times(block, factors):
    return (block.astype(F32) * factors[0:1].astype(F32)).astype(BF16)


def next_rows_kernel(flags, pivot_rows, pivot_scale, early, late, *refs):
    result, link, sems = refs[-3:]
    wait = fetched(early, late, link, sems, [flags[1]])
    scaled = times(pivot_rows[...], pivot_scale)
    wait()
    result[...] = (-dot_nn(scaled, link[...])).astype(BF16)


def level_2_kernel(flags, rows, scale, pivot_scale, early, late, pivot_early, pivot_late, result, link, pivot, sems):
    wait_link = fetched(early, late, link, sems.at[0], [flags[1]])
    wait_pivot = fetched(pivot_early, pivot_late, pivot, sems.at[1], [flags[1]])
    scaled = times(rows[...], scale)
    wait_link()
    inner = times(dot_nt(scaled, link[...]), pivot_scale)
    wait_pivot()
    result[...] = (-dot_nt(inner, pivot[...])).astype(BF16)


def right_kernel(
    flags, own, pivot_scale, next_scale, prev_early, prev_late, pivot_early, pivot_late, ready,
    result, prev, pivot, sems,
):
    del ready
    wait_prev = fetched(prev_early, prev_late, prev, sems.at[0], [flags[1]])
    wait_pivot = fetched(pivot_early, pivot_late, pivot, sems.at[1], [flags[1]])
    wait_prev()
    across = jnp.where(flags[0] == 1, 0.0, -dot_nt(own[...], prev[...])).astype(BF16)
    across = times(across, pivot_scale)
    wait_pivot()
    columns = (-dot_nt(across, pivot[...])).astype(BF16)
    inner = dot_nn(times(columns, next_scale), pivot[...]) * pivot_scale[0:1].astype(F32)
    keep = jnp.where(flags[3] == 1, 1.0, 0.0)
    result[...] = (across.astype(F32) - inner * keep).astype(BF16)


def last_kernel(
    flags, rows, right, next_rows, mine, partial, pivot_scale, next_scale,
    early, late, pivot_early, pivot_late, form, new, link, pivot, sems,
):
    wait_pivot = fetched(pivot_early, pivot_late, pivot, sems.at[1], [flags[1]])
    wait_link = fetched(early, late, link, sems.at[0], [flags[1]])
    scaled = times(rows[...], next_scale)
    wait_pivot()
    inner = times(dot_nn(scaled, pivot[...]), pivot_scale)
    wait_link()
    last = dot_nn(inner, link[...]).astype(BF16)
    odd = jnp.where(flags[2] == 1, 0.0, 1.0)
    form[...] = partial[...] - odd * dot_nn(right[...], link[...])
    new[...] = jnp.where(flags[3] == 1, last, jnp.where(flags[2] == 1, mine[...], next_rows[...]))


def with_links(kernel, out_shapes, flags, blocks, arrays, links):
    order = arrays[0].shape[1]
    rows = arrays[1].shape[0]
    size = order // rows
    specs = [spec if spec is not None else whole_spec(block.shape) for block, spec in blocks]
    sems = (size,) if links == 1 else (links, size)
    return pl.pallas_call(
        kernel,
        out_shape=out_shapes,
        grid_spec=pltpu.PrefetchScalarGridSpec(
            num_scalar_prefetch=1,
            grid=(1,),
            in_specs=specs + [ANY] * len(arrays),
            out_specs=[whole_spec(out.shape) for out in out_shapes],
            scratch_shapes=[pltpu.VMEM((order, order), BF16)] * links + [pltpu.SemaphoreType.DMA(sems)],
        ),
        compiler_params=pltpu.CompilerParams(vmem_limit_bytes=32 * 1024 * 1024),
        cost_estimate=FREE,
    )(flags, *[block for block, _ in blocks], *arrays)


def on_device(sep_block, own_couple, prev_couple, inner_diag):
    separator = sep_block[0]
    own_rows = own_couple[0]
    prev_rows = prev_couple[0]
    reciprocal = 1.0 / inner_diag[0]
    rows, order = own_rows.shape
    place = lax.axis_index("space")
    size = lax.axis_size("space")
    row_start = place * rows
    partition = lax.axis_index("tm")
    parts = lax.axis_size("tm")

    def between(block, route):
        return lax.ppermute(block, "tm", [(a, b) for a, b in route if 0 <= b < parts])

    even = range(0, parts, 2)
    pivots = range(1, parts, 4)
    everyone = range(parts)

    def one_step(ahead, back, step):
        up = [(j, j + 1) for j in range(step - 1, size - 1)]
        down = [(j, j - 1) for j in range(1, size - step + 1)]
        return lax.ppermute(ahead, "space", up), lax.ppermute(back, "space", down)

    def block_at(arrived, spot):
        block = arrived[0][0]
        for step in range(1, len(arrived)):
            if spot + step < size:
                block = jnp.where(place == spot + step, arrived[step][0], block)
            if spot - step >= 0:
                block = jnp.where(place == spot - step, arrived[step][1], block)
        return block

    is_first = partition == 0
    is_pivot = partition % 2 == 0
    is_receiver = partition % 2 == 1
    is_last = partition % 4 == 3
    flags = jnp.stack(
        [is_first.astype(jnp.int32), place, is_pivot.astype(jnp.int32), is_last.astype(jnp.int32)]
    )
    own_long = opening(flags, own_rows, prev_rows, separator, rows_of(reciprocal))
    own_arrived = [(own_long, own_long)]
    prev_arrived = [(prev_rows, prev_rows)]
    for step in range(1, size):
        own_arrived.append(one_step(*own_arrived[-1], step))
        prev_arrived.append(one_step(*prev_arrived[-1], step))
    words_arrived = [tuple(block[rows:] for block in pair) for pair in own_arrived]

    left_side = place < size // 2
    late_start = jnp.where(left_side, size - 1, 0) * rows
    is_end = jnp.logical_or(place == 0, place == size - 1)
    prev_blocks = [block_at(prev_arrived[:-1], spot) for spot in range(size)]
    zero = jnp.zeros_like(prev_rows)
    prev_blocks[0] = jnp.where(place == size - 1, zero, prev_blocks[0])
    prev_blocks[-1] = jnp.where(place == 0, zero, prev_blocks[-1])
    prev_first = jnp.concatenate(prev_blocks)
    prev_far = jnp.where(left_side, prev_blocks[-1], prev_blocks[0])
    prev_first, prev_far = lax.optimization_barrier((prev_first, prev_far))
    words = [block_at(words_arrived, spot) for spot in range(size)]

    def pair_sum(block, at):
        return block[at].astype(F32) + block[at + 1].astype(F32)

    part_diag = sum(pair_sum(block, 0) for block in words)
    part_diag = part_diag - jnp.concatenate([pair_sum(block, 2)[:rows] for block in words])
    prev_diag = jnp.concatenate([pair_sum(block, 4)[:rows] for block in words])
    part_diag, prev_diag = lax.optimization_barrier((part_diag, prev_diag))
    diag = part_diag - between(prev_diag, [(p, p - 1) for p in everyone])
    pivot_diag = between(part_diag, [(p, p + 1) for p in even]) - prev_diag
    scale = (1.0 / jnp.maximum(diag, 1.0)).astype(BF16)
    pivot_scale = (1.0 / jnp.maximum(pivot_diag, 1.0)).astype(BF16)

    own_scaled = scaled_by(own_rows, reciprocal)
    sources = [own_long]
    for up, down in own_arrived[1:]:
        sources += [up, down]
    prev_first = scaled_by(prev_first, reciprocal)
    link, partial, prev_form, own_full, mine = early_forms(
        flags, prev_first, prev_rows, own_scaled, separator, sources
    )
    scale8, pivot_scale8 = rows_of(scale), rows_of(pivot_scale)
    update, left_diag, right_diag = level_forms(flags, link, mine, scale8, pivot_scale8, prev_form)

    from_below, from_above = prev_arrived[-1]
    late_scale = lax.dynamic_slice_in_dim(pivot_scale, late_start, rows, 0)
    late_scale = jnp.where(is_end, late_scale, jnp.zeros_like(late_scale))
    pivot_early = between(link, [(p, p + 1) for p in even])
    from_later = between(update, [(p, p - 1) for p in everyone])
    late, corner, prev_late, left_late, right_late = late_forms(
        flags, rows_of(reciprocal), prev_rows, mine, own_full, scale8, rows_of(late_scale),
        from_below, from_above, prev_far, right_diag,
    )
    left_diag = lax.dynamic_update_slice_in_dim(left_diag[0], left_late[0], late_start, 0)
    left_diag = between(left_diag, [(p, p - 1) for p in even])
    pivot_late = between(late, [(p, p + 1) for p in even])
    corner = between(corner, [(p, p - 1) for p in everyone])

    own_block = pl.BlockSpec((rows, order), lambda j, f: (f[1], 0), pipeline_mode=pl.Buffered(1))
    (next_rows,) = with_links(
        next_rows_kernel, [SHAPE((rows, order), BF16)], flags,
        [(pivot_early, own_block), (pivot_scale8, None)], [link, late], 1,
    )
    pivot_rows = between(next_rows, [(p, p + 2) for p in pivots if p != 1])
    next_diag = diag - left_diag - right_diag[0] - right_late[0]
    next_scale = (1.0 / jnp.maximum(next_diag, 1.0)).astype(BF16)
    next_pivot_scale = between(next_scale, [(p, p + 2) for p in pivots])

    links = [link, late, pivot_early, pivot_late]
    (left_next,) = with_links(
        level_2_kernel, [SHAPE((rows, order), BF16)], flags,
        [(next_rows, None), (rows_of(next_scale), None), (pivot_scale8, None)], links, 2,
    )
    from_pivot = between(left_next, [(p, p - 2) for p in pivots])
    next_scale8 = rows_of(next_pivot_scale)
    (right,) = with_links(
        right_kernel, [SHAPE((rows, order), BF16)], flags,
        [(own_rows, None), (pivot_scale8, None), (next_scale8, None)],
        [prev_first, prev_late, pivot_early, pivot_late, left_next], 2,
    )
    form, out_link = with_links(
        last_kernel, [SHAPE((rows, order), F32), SHAPE((rows, order), BF16)], flags,
        [
            (pivot_rows, None), (right, None), (next_rows, None), (mine, None), (partial, None),
            (pivot_scale8, None), (next_scale8, None),
        ],
        links, 2,
    )
    from_later = lax.dynamic_update_slice_in_dim(from_later, corner, late_start, 1)
    schur = form - from_later.astype(F32) - from_pivot.astype(F32)
    return (schur[None], out_link[None])


def solution(mesh):
    placed = (P("tm", "space", None), P("tm", "space", None), P("tm", "space", None), P("tm", None))
    return jax.shard_map(
        on_device,
        mesh=mesh,
        in_specs=placed,
        out_specs=(P("tm", "space", None), P("tm", "space", None)),
        check_vma=False,
    )
```

```python
import functools

import jax
import jax.numpy as jnp
from jax import lax
from jax.experimental import pallas as pl
from jax.experimental.pallas import tpu as pltpu
from jax.sharding import PartitionSpec as P

BF16 = jnp.bfloat16
F32 = jnp.float32
EXTRA = 16
WIDTH = 256

ANY = pl.BlockSpec(memory_space=pl.ANY)
SHAPE = jax.ShapeDtypeStruct
FREE = pl.CostEstimate(flops=0, bytes_accessed=0, transcendentals=0)


def after(block, *others):
    def body(*refs):
        del refs

    return pl.pallas_call(
        body,
        out_shape=SHAPE(block.shape, block.dtype),
        in_specs=[ANY] * (1 + len(others)),
        out_specs=ANY,
        input_output_aliases={0: 0},
    )(block, *others)


def scaled_by(matrix, factors):
    return (matrix.astype(F32) * factors.astype(F32)[None, :]).astype(BF16)


def row_scaled_by(matrix, factors):
    return (matrix.astype(F32) * factors.astype(F32)[:, None]).astype(BF16)


def dot_nt(left, right):
    return lax.dot_general(left, right, (((1,), (1,)), ((), ())), preferred_element_type=F32)


def dot_nn(left, right):
    return lax.dot_general(left, right, (((1,), (0,)), ((), ())), preferred_element_type=F32)


def dot_tn(left, right):
    return lax.dot_general(left, right, (((0,), (0,)), ((), ())), preferred_element_type=F32)


def rows_of(scale):
    return jnp.broadcast_to(scale[None, :], (8, scale.shape[0]))


def whole_spec(shape):
    return pl.BlockSpec(shape, lambda j, f: (0,) * len(shape), pipeline_mode=pl.Buffered(1))


def along_spec(count):
    return pl.BlockSpec((count, WIDTH), lambda j, f: (0, j))


def down_spec(count):
    return pl.BlockSpec((WIDTH, count), lambda j, f: (j, 0))


def opening_kernel(flags, own, prev, separator, reciprocal, long):
    rows, order = own.shape
    row_ids = lax.broadcasted_iota(jnp.int32, (rows, order), 0) + flags[1] * rows
    col_ids = lax.broadcasted_iota(jnp.int32, (rows, order), 1)
    on_diagonal = jnp.where(row_ids == col_ids, separator[...], 0.0)
    ones = jnp.ones((8, order), BF16)

    def split(value):
        high = value.astype(BF16)
        return high, (value - high.astype(F32)).astype(BF16)

    def form_diagonal(block):
        wide = block.astype(F32)
        high, low = split((wide * reciprocal[0:1]).astype(BF16).astype(F32) * wide)
        return (dot_nt(ones, high) + dot_nt(ones, low))[0:1]

    def placed(words, count):
        ids = lax.broadcasted_iota(jnp.int32, (EXTRA, count), 0)
        total = jnp.zeros((EXTRA, count), F32)
        for at, word in words.items():
            total = jnp.where(ids == at, word.astype(F32), total)
        return total.astype(BF16)

    long[0:rows, :] = own[...]
    high, low = split(jnp.sum(on_diagonal, axis=0, keepdims=True))
    long[rows:, :] = placed({0: high, 1: low}, order)
    own_high, own_low = split(form_diagonal(own[...]))
    prev_high, prev_low = split(form_diagonal(prev[...]))
    local = placed({2: own_high, 3: own_low, 4: prev_high, 5: prev_low}, rows)
    long[rows:, 0:rows] = long[rows:, 0:rows] + local


def opening(flags, own, prev, separator, reciprocal):
    rows, order = own.shape
    return pl.pallas_call(
        opening_kernel,
        out_shape=SHAPE((rows + EXTRA, order), BF16),
        grid_spec=pltpu.PrefetchScalarGridSpec(
            num_scalar_prefetch=1,
            grid=(1,),
            in_specs=[whole_spec((rows, order))] * 3 + [whole_spec((8, order))],
            out_specs=whole_spec((rows + EXTRA, order)),
        ),
        compiler_params=pltpu.CompilerParams(vmem_limit_bytes=32 * 1024 * 1024),
        cost_estimate=FREE,
    )(flags, own, prev, separator, reciprocal)


def early_kernel(size, flags, prev_whole, prev_rows, own_rows, separator, *refs):
    sources = refs[: 2 * size - 1]
    link, partial, form, own_out, mine, own, sems = refs[2 * size + 1 :]
    rows = separator.shape[0]
    step = pl.program_id(0)
    here = pl.ds(pl.multiple_of(step * WIDTH, WIDTH), WIDTH)

    def copies():
        for spot in range(size):
            for by, source in enumerate(sources):
                distance = (by + 1) // 2 if by % 2 else -(by // 2)
                target = own.at[pl.ds(spot * rows, rows)]
                copy = pltpu.make_async_copy(source.at[pl.ds(0, rows)], target, sems.at[spot])
                yield flags[1] - spot == distance, copy

    @pl.when(step == 0)
    def _():
        for chosen, copy in copies():
            pl.when(chosen)(copy.start)
        for chosen, copy in copies():
            pl.when(chosen)(copy.wait)

    block = own[here, :]
    own_out[...] = block
    link[...] = jnp.where(flags[0] == 1, 0.0, -dot_nt(prev_whole[...], block)).astype(BF16)
    mine[...] = link[pl.ds(pl.multiple_of(flags[1] * rows, rows), rows), :]
    partial[...] = separator[...] - dot_nt(own_rows[...], block)
    form[...] = dot_nt(prev_rows[...], prev_whole[here, :])


def early_forms(flags, prev_whole, prev_rows, own_rows, separator, sources):
    rows, order = own_rows.shape
    size = order // rows
    return pl.pallas_call(
        functools.partial(early_kernel, size),
        out_shape=[
            SHAPE((order, order), BF16),
            SHAPE((rows, order), F32),
            SHAPE((rows, order), F32),
            SHAPE((order, order), BF16),
            SHAPE((rows, order), BF16),
        ],
        grid_spec=pltpu.PrefetchScalarGridSpec(
            num_scalar_prefetch=1,
            grid=(order // WIDTH,),
            in_specs=[
                whole_spec((order, order)),
                whole_spec((rows, order)),
                whole_spec((rows, order)),
                along_spec(rows),
            ]
            + [ANY] * len(sources),
            out_specs=[along_spec(order), along_spec(rows), along_spec(rows), down_spec(order), along_spec(rows)],
            scratch_shapes=[pltpu.VMEM((order, order), BF16), pltpu.SemaphoreType.DMA((size,))],
        ),
        compiler_params=pltpu.CompilerParams(vmem_limit_bytes=26 * 1024 * 1024),
        cost_estimate=FREE,
    )(flags, prev_whole, prev_rows, own_rows, separator, *sources)


def late_kernel(
    size, flags, reciprocal, prev_rows, mine, own, scale, late_scale, from_below, from_above, far,
    ready, link, corner, scaled, left_diag, right_diag, raw, sem,
):
    del ready
    place = flags[1]
    step = pl.program_id(0)
    width = own.shape[0]
    here = pl.ds(pl.multiple_of(step * width, width), width)

    @pl.when(step == 0)
    def _():
        for chosen, source in (
            (place == 0, from_above),
            (place == size - 1, from_below),
            (jnp.logical_and(place != 0, place != size - 1), far),
        ):
            copy = pltpu.make_async_copy(source, raw, sem)
            pl.when(chosen)(copy.start)
            pl.when(chosen)(copy.wait)
        scaled[...] = (raw[...].astype(F32) * reciprocal[0:1]).astype(BF16)

    link[:, here] = jnp.where(flags[0] == 1, 0.0, -dot_nt(scaled[...], own[...])).astype(BF16)

    @pl.when(step == pl.num_programs(0) - 1)
    def _():
        late = link[...]
        square = late * late
        keep = jnp.where(flags[2] == 1, 1.0, 0.0)
        ours = mine[...] * scale[0:1]
        corner[...] = (dot_nt(prev_rows[...], scaled[...]) + keep * dot_nt(ours, late)).astype(BF16)
        left_diag[...] = dot_nt(scale[...], square)
        right_diag[...] = dot_nn(late_scale[...], square)


def late_forms(
    flags, reciprocal, prev_rows, mine, own, scale, late_scale, from_below, from_above, far, ready
):
    rows, order = prev_rows.shape
    size = order // rows
    width = 512
    return pl.pallas_call(
        functools.partial(late_kernel, size),
        out_shape=[
            SHAPE((rows, order), BF16),
            SHAPE((rows, rows), BF16),
            SHAPE((rows, order), BF16),
            SHAPE((8, rows), F32),
            SHAPE((8, order), F32),
        ],
        grid_spec=pltpu.PrefetchScalarGridSpec(
            num_scalar_prefetch=1,
            grid=(order // width,),
            in_specs=[
                whole_spec((8, order)),
                whole_spec((rows, order)),
                whole_spec((rows, order)),
                pl.BlockSpec((width, order), lambda j, f: (j, 0)),
                whole_spec((8, order)),
                whole_spec((8, rows)),
                ANY,
                ANY,
                ANY,
                ANY,
            ],
            out_specs=[
                whole_spec((rows, order)),
                whole_spec((rows, rows)),
                whole_spec((rows, order)),
                whole_spec((8, rows)),
                whole_spec((8, order)),
            ],
            scratch_shapes=[pltpu.VMEM((rows, order), BF16), pltpu.SemaphoreType.DMA],
        ),
        compiler_params=pltpu.CompilerParams(vmem_limit_bytes=18 * 1024 * 1024),
    )(
        flags, reciprocal, prev_rows, mine, own, scale, late_scale, from_below, from_above, far, ready
    )


def level_kernel(flags, link, mine, scale, pivot_scale, form, update, left_diag, right_diag):
    part = link[...]
    scaled = mine[...] * scale[0:1]
    keep = jnp.where(flags[2] == 1, 1.0, 0.0)
    update[...] = (form[...] + keep * dot_nt(scaled, part)).astype(BF16)
    square = part * part
    left_diag[...] = dot_nt(scale[...], square)

    @pl.when(pl.program_id(0) == 0)
    def _():
        right_diag[...] = jnp.zeros_like(right_diag)

    right_diag[...] += dot_nn(pivot_scale[...], square)


def level_forms(flags, link, mine, scale, pivot_scale, form):
    rows, order = form.shape
    width = 512
    along = lambda count: pl.BlockSpec((count, width), lambda j, f: (0, j))
    return pl.pallas_call(
        level_kernel,
        out_shape=[SHAPE((rows, order), BF16), SHAPE((8, order), F32), SHAPE((8, order), F32)],
        grid_spec=pltpu.PrefetchScalarGridSpec(
            num_scalar_prefetch=1,
            grid=(order // width,),
            in_specs=[
                pl.BlockSpec((width, order), lambda j, f: (j, 0)),
                whole_spec((rows, order)),
                whole_spec((8, order)),
                along(8),
                along(rows),
            ],
            out_specs=[along(rows), along(8), whole_spec((8, order))],
        ),
        compiler_params=pltpu.CompilerParams(vmem_limit_bytes=18 * 1024 * 1024),
        cost_estimate=FREE,
    )(flags, link, mine, scale, pivot_scale, form)


def fetched(early, late, whole, sems, at):
    rows, order = late.shape
    size = order // rows
    place = at[0]
    low = place < size // 2
    spans = [pl.ds(spot * rows, rows) for spot in range(size)]
    copies = []
    for spot, span in enumerate(spans):
        plain = pltpu.make_async_copy(early.at[span], whole.at[span], sems.at[spot])
        if spot not in (0, size - 1):
            copies.append((True, plain))
            continue
        is_late = low if spot else jnp.logical_not(low)
        copies.append((jnp.logical_not(is_late), plain))
        copies.append((is_late, pltpu.make_async_copy(late, whole.at[span], sems.at[spot])))
    for chosen, copy in copies:
        pl.when(chosen)(copy.start) if chosen is not True else copy.start()

    def wait():
        for chosen, copy in copies:
            pl.when(chosen)(copy.wait) if chosen is not True else copy.wait()

    return wait


def times(block, factors):
    return (block.astype(F32) * factors[0:1].astype(F32)).astype(BF16)


def next_rows_kernel(flags, pivot_rows, pivot_scale, early, late, *refs):
    result, token, link, sems = refs[-4:]
    token[...] = jnp.ones_like(token)
    wait = fetched(early, late, link, sems, [flags[1]])
    scaled = times(pivot_rows[...], pivot_scale)
    wait()
    result[...] = (-dot_nn(scaled, link[...])).astype(BF16)


def level_2_kernel(flags, rows, scale, pivot_scale, early, late, pivot_early, pivot_late, result, link, pivot, sems):
    wait_link = fetched(early, late, link, sems.at[0], [flags[1]])
    wait_pivot = fetched(pivot_early, pivot_late, pivot, sems.at[1], [flags[1]])
    scaled = times(rows[...], scale)
    wait_link()
    inner = times(dot_nt(scaled, link[...]), pivot_scale)
    wait_pivot()
    result[...] = (-dot_nt(inner, pivot[...])).astype(BF16)


def right_kernel(
    flags, own, pivot_scale, next_scale, prev_early, prev_late, pivot_early, pivot_late, ready,
    result, prev, pivot, sems,
):
    del ready
    wait_prev = fetched(prev_early, prev_late, prev, sems.at[0], [flags[1]])
    wait_pivot = fetched(pivot_early, pivot_late, pivot, sems.at[1], [flags[1]])
    wait_prev()
    across = jnp.where(flags[0] == 1, 0.0, -dot_nt(own[...], prev[...])).astype(BF16)
    across = times(across, pivot_scale)
    wait_pivot()
    columns = (-dot_nt(across, pivot[...])).astype(BF16)
    inner = dot_nn(times(columns, next_scale), pivot[...]) * pivot_scale[0:1].astype(F32)
    keep = jnp.where(flags[3] == 1, 1.0, 0.0)
    result[...] = (across.astype(F32) - inner * keep).astype(BF16)


def last_kernel(
    flags, rows, right, next_rows, mine, partial, pivot_scale, next_scale,
    early, late, pivot_early, pivot_late, form, new, link, pivot, sems,
):
    wait_pivot = fetched(pivot_early, pivot_late, pivot, sems.at[1], [flags[1]])
    wait_link = fetched(early, late, link, sems.at[0], [flags[1]])
    scaled = times(rows[...], next_scale)
    wait_pivot()
    inner = times(dot_nn(scaled, pivot[...]), pivot_scale)
    wait_link()
    last = dot_nn(inner, link[...]).astype(BF16)
    odd = jnp.where(flags[2] == 1, 0.0, 1.0)
    form[...] = partial[...] - odd * dot_nn(right[...], link[...])
    new[...] = jnp.where(flags[3] == 1, last, jnp.where(flags[2] == 1, mine[...], next_rows[...]))


def with_links(kernel, out_shapes, flags, blocks, arrays, links, megabytes):
    order = arrays[0].shape[1]
    rows = arrays[1].shape[0]
    size = order // rows
    specs = [spec if spec is not None else whole_spec(block.shape) for block, spec in blocks]
    sems = (size,) if links == 1 else (links, size)
    return pl.pallas_call(
        kernel,
        out_shape=out_shapes,
        grid_spec=pltpu.PrefetchScalarGridSpec(
            num_scalar_prefetch=1,
            grid=(1,),
            in_specs=specs + [ANY] * len(arrays),
            out_specs=[whole_spec(out.shape) for out in out_shapes],
            scratch_shapes=[pltpu.VMEM((order, order), BF16)] * links + [pltpu.SemaphoreType.DMA(sems)],
        ),
        compiler_params=pltpu.CompilerParams(vmem_limit_bytes=megabytes * 1024 * 1024),
        cost_estimate=FREE,
    )(flags, *[block for block, _ in blocks], *arrays)


def on_device(sep_block, own_couple, prev_couple, inner_diag):
    separator = sep_block[0]
    own_rows = own_couple[0]
    prev_rows = prev_couple[0]
    reciprocal = 1.0 / inner_diag[0]
    rows, order = own_rows.shape
    place = lax.axis_index("space")
    size = lax.axis_size("space")
    row_start = place * rows
    partition = lax.axis_index("tm")
    parts = lax.axis_size("tm")

    def between(block, route):
        return lax.ppermute(block, "tm", [(a, b) for a, b in route if 0 <= b < parts])

    even = range(0, parts, 2)
    pivots = range(1, parts, 4)
    everyone = range(parts)

    def one_step(ahead, back, step):
        up = [(j, j + 1) for j in range(step - 1, size - 1)]
        down = [(j, j - 1) for j in range(1, size - step + 1)]
        return lax.ppermute(ahead, "space", up), lax.ppermute(back, "space", down)

    def block_at(arrived, spot):
        block = arrived[0][0]
        for step in range(1, len(arrived)):
            if spot + step < size:
                block = jnp.where(place == spot + step, arrived[step][0], block)
            if spot - step >= 0:
                block = jnp.where(place == spot - step, arrived[step][1], block)
        return block

    is_first = partition == 0
    is_pivot = partition % 2 == 0
    is_receiver = partition % 2 == 1
    is_last = partition % 4 == 3
    flags = jnp.stack(
        [is_first.astype(jnp.int32), place, is_pivot.astype(jnp.int32), is_last.astype(jnp.int32)]
    )
    own_long = opening(flags, own_rows, prev_rows, separator, rows_of(reciprocal))
    own_arrived = [(own_long, own_long)]
    prev_arrived = [(prev_rows, prev_rows)]
    for step in range(1, size):
        blocks = prev_arrived[-1]
        if step == size - 1:
            went = [block[rows + EXTRA - 1, 0] == 0 for block in own_arrived[-1]]
            zero = jnp.zeros_like(prev_rows)
            blocks = [jnp.where(jnp.logical_and(*went), block, zero) for block in blocks]
        own_arrived.append(one_step(*own_arrived[-1], step))
        prev_arrived.append(one_step(*blocks, step))
    words_arrived = [tuple(block[rows:] for block in pair) for pair in own_arrived]

    left_side = place < size // 2
    late_start = jnp.where(left_side, size - 1, 0) * rows
    is_end = jnp.logical_or(place == 0, place == size - 1)
    prev_blocks = [block_at(prev_arrived[:-1], spot) for spot in range(size)]
    zero = jnp.zeros_like(prev_rows)
    prev_blocks[0] = jnp.where(place == size - 1, zero, prev_blocks[0])
    prev_blocks[-1] = jnp.where(place == 0, zero, prev_blocks[-1])
    prev_first = jnp.concatenate(prev_blocks)
    prev_far = jnp.where(left_side, prev_blocks[-1], prev_blocks[0])
    prev_first, prev_far = lax.optimization_barrier((prev_first, prev_far))
    words = [block_at(words_arrived, spot) for spot in range(size)]

    def pair_sum(block, at):
        return block[at].astype(F32) + block[at + 1].astype(F32)

    part_diag = sum(pair_sum(block, 0) for block in words)
    part_diag = part_diag - jnp.concatenate([pair_sum(block, 2)[:rows] for block in words])
    prev_diag = jnp.concatenate([pair_sum(block, 4)[:rows] for block in words])
    part_diag, prev_diag = lax.optimization_barrier((part_diag, prev_diag))
    diag = part_diag - between(prev_diag, [(p, p - 1) for p in everyone])
    pivot_diag = between(part_diag, [(p, p + 1) for p in even]) - prev_diag
    scale = (1.0 / jnp.maximum(diag, 1.0)).astype(BF16)
    pivot_scale = (1.0 / jnp.maximum(pivot_diag, 1.0)).astype(BF16)

    own_scaled = scaled_by(own_rows, reciprocal)
    sources = [own_long]
    for up, down in own_arrived[1:]:
        sources += [up, down]
    sources += [scale, pivot_scale]
    prev_first = scaled_by(prev_first, reciprocal)
    link, partial, prev_form, own_full, mine = early_forms(
        flags, prev_first, prev_rows, own_scaled, separator, sources
    )
    scale8, pivot_scale8 = rows_of(scale), rows_of(pivot_scale)
    update, left_diag, right_diag = level_forms(flags, link, mine, scale8, pivot_scale8, prev_form)

    from_below, from_above = prev_arrived[-1]
    late_scale = lax.dynamic_slice_in_dim(pivot_scale, late_start, rows, 0)
    late_scale = jnp.where(is_end, late_scale, jnp.zeros_like(late_scale))
    pivot_early = between(link, [(p, p + 1) for p in even])
    late, corner, prev_late, left_late, right_late = late_forms(
        flags, rows_of(reciprocal), prev_rows, mine, own_full, scale8, rows_of(late_scale),
        from_below, from_above, prev_far, right_diag,
    )
    pivot_late = between(late, [(p, p + 1) for p in even])
    left_diag = lax.dynamic_update_slice_in_dim(left_diag[0], left_late[0], late_start, 0)
    high = lax.reduce_precision(left_diag, 8, 7)
    words = jnp.pad(jnp.stack([high, left_diag - high]).astype(BF16), ((0, EXTRA - 2), (0, 0)))
    update = jnp.concatenate([lax.dynamic_update_slice_in_dim(update, corner, late_start, 1), words])
    from_later = between(update, [(p, p - 1) for p in everyone])

    own_block = pl.BlockSpec((rows, order), lambda j, f: (f[1], 0), pipeline_mode=pl.Buffered(1))
    next_rows, token = with_links(
        next_rows_kernel, [SHAPE((rows, order), BF16), SHAPE((8, 128), jnp.int32)], flags,
        [(pivot_early, own_block), (pivot_scale8, None)], [link, late], 1, 14,
    )
    pivot_rows = between(next_rows, [(p, p + 2) for p in pivots if p != 1])
    left_diag = jnp.where(token[0, 0] == 1, pair_sum(from_later[rows:], 0), 0.0)
    next_diag = diag - left_diag - right_diag[0] - right_late[0]
    next_scale = (1.0 / jnp.maximum(next_diag, 1.0)).astype(BF16)
    next_pivot_scale = between(next_scale, [(p, p + 2) for p in pivots])

    links = [link, late, pivot_early, pivot_late]
    (left_next,) = with_links(
        level_2_kernel, [SHAPE((rows, order), BF16)], flags,
        [(next_rows, None), (rows_of(next_scale), None), (pivot_scale8, None)], links, 2, 20,
    )
    from_pivot = between(left_next, [(p, p - 2) for p in pivots])
    next_scale8 = rows_of(next_pivot_scale)
    (right,) = with_links(
        right_kernel, [SHAPE((rows, order), BF16)], flags,
        [(own_rows, None), (pivot_scale8, None), (next_scale8, None)],
        [prev_first, prev_late, pivot_early, pivot_late, left_next], 2, 22,
    )
    form, out_link = with_links(
        last_kernel, [SHAPE((rows, order), F32), SHAPE((rows, order), BF16)], flags,
        [
            (pivot_rows, None), (right, None), (next_rows, None), (mine, None), (partial, None),
            (pivot_scale8, None), (next_scale8, None),
        ],
        links, 2, 26,
    )
    schur = form - from_later[:rows].astype(F32) - from_pivot.astype(F32)
    return (schur[None], out_link[None])


def solution(mesh):
    placed = (P("tm", "space", None), P("tm", "space", None), P("tm", "space", None), P("tm", None))
    return jax.shard_map(
        on_device,
        mesh=mesh,
        in_specs=placed,
        out_specs=(P("tm", "space", None), P("tm", "space", None)),
        check_vma=False,
    )
```

```python
import functools

import jax
import jax.numpy as jnp
from jax import lax
from jax.experimental import pallas as pl
from jax.experimental.pallas import tpu as pltpu
from jax.sharding import PartitionSpec as P

BF16 = jnp.bfloat16
F32 = jnp.float32
EXTRA = 16
WIDTH = 256

ANY = pl.BlockSpec(memory_space=pl.ANY)
SHAPE = jax.ShapeDtypeStruct
FREE = pl.CostEstimate(flops=0, bytes_accessed=0, transcendentals=0)


def after(block, *others):
    def body(*refs):
        del refs

    return pl.pallas_call(
        body,
        out_shape=SHAPE(block.shape, block.dtype),
        in_specs=[ANY] * (1 + len(others)),
        out_specs=ANY,
        input_output_aliases={0: 0},
    )(block, *others)


def scaled_by(matrix, factors):
    return (matrix.astype(F32) * factors.astype(F32)[None, :]).astype(BF16)


def row_scaled_by(matrix, factors):
    return (matrix.astype(F32) * factors.astype(F32)[:, None]).astype(BF16)


def dot_nt(left, right):
    return lax.dot_general(left, right, (((1,), (1,)), ((), ())), preferred_element_type=F32)


def dot_nn(left, right):
    return lax.dot_general(left, right, (((1,), (0,)), ((), ())), preferred_element_type=F32)


def dot_tn(left, right):
    return lax.dot_general(left, right, (((0,), (0,)), ((), ())), preferred_element_type=F32)


def rows_of(scale):
    return jnp.broadcast_to(scale[None, :], (8, scale.shape[0]))


def whole_spec(shape):
    return pl.BlockSpec(shape, lambda j, f: (0,) * len(shape), pipeline_mode=pl.Buffered(1))


def along_spec(count):
    return pl.BlockSpec((count, WIDTH), lambda j, f: (0, j))


def down_spec(count):
    return pl.BlockSpec((WIDTH, count), lambda j, f: (j, 0))


def opening_kernel(flags, own, prev, separator, reciprocal, long):
    rows, order = own.shape
    row_ids = lax.broadcasted_iota(jnp.int32, (rows, order), 0) + flags[1] * rows
    col_ids = lax.broadcasted_iota(jnp.int32, (rows, order), 1)
    on_diagonal = jnp.where(row_ids == col_ids, separator[...], 0.0)
    ones = jnp.ones((8, order), BF16)

    def split(value):
        high = value.astype(BF16)
        return high, (value - high.astype(F32)).astype(BF16)

    def form_diagonal(block):
        wide = block.astype(F32)
        high, low = split((wide * reciprocal[0:1]).astype(BF16).astype(F32) * wide)
        return (dot_nt(ones, high) + dot_nt(ones, low))[0:1]

    def placed(words, count):
        ids = lax.broadcasted_iota(jnp.int32, (EXTRA, count), 0)
        total = jnp.zeros((EXTRA, count), F32)
        for at, word in words.items():
            total = jnp.where(ids == at, word.astype(F32), total)
        return total.astype(BF16)

    long[0:rows, :] = own[...]
    high, low = split(jnp.sum(on_diagonal, axis=0, keepdims=True))
    long[rows:, :] = placed({0: high, 1: low}, order)
    own_high, own_low = split(form_diagonal(own[...]))
    prev_high, prev_low = split(form_diagonal(prev[...]))
    local = placed({2: own_high, 3: own_low, 4: prev_high, 5: prev_low}, rows)
    long[rows:, 0:rows] = long[rows:, 0:rows] + local


def opening(flags, own, prev, separator, reciprocal):
    rows, order = own.shape
    return pl.pallas_call(
        opening_kernel,
        out_shape=SHAPE((rows + EXTRA, order), BF16),
        grid_spec=pltpu.PrefetchScalarGridSpec(
            num_scalar_prefetch=1,
            grid=(1,),
            in_specs=[whole_spec((rows, order))] * 3 + [whole_spec((8, order))],
            out_specs=whole_spec((rows + EXTRA, order)),
        ),
        compiler_params=pltpu.CompilerParams(vmem_limit_bytes=32 * 1024 * 1024),
        cost_estimate=FREE,
    )(flags, own, prev, separator, reciprocal)


def early_kernel(size, flags, prev_whole, prev_rows, own_rows, separator, *refs):
    sources = refs[: 2 * size - 1]
    link, partial, form, own_out, mine, own, sems = refs[2 * size - 1 :]
    rows = separator.shape[0]
    step = pl.program_id(0)
    here = pl.ds(pl.multiple_of(step * WIDTH, WIDTH), WIDTH)

    def copies():
        for spot in range(size):
            for by, source in enumerate(sources):
                distance = (by + 1) // 2 if by % 2 else -(by // 2)
                target = own.at[pl.ds(spot * rows, rows)]
                copy = pltpu.make_async_copy(source.at[pl.ds(0, rows)], target, sems.at[spot])
                yield flags[1] - spot == distance, copy

    @pl.when(step == 0)
    def _():
        for chosen, copy in copies():
            pl.when(chosen)(copy.start)
        for chosen, copy in copies():
            pl.when(chosen)(copy.wait)

    block = own[here, :]
    own_out[...] = block
    link[...] = jnp.where(flags[0] == 1, 0.0, -dot_nt(prev_whole[...], block)).astype(BF16)
    mine[...] = link[pl.ds(pl.multiple_of(flags[1] * rows, rows), rows), :]
    partial[...] = separator[...] - dot_nt(own_rows[...], block)
    form[...] = dot_nt(prev_rows[...], prev_whole[here, :])


def early_forms(flags, prev_whole, prev_rows, own_rows, separator, sources):
    rows, order = own_rows.shape
    size = order // rows
    return pl.pallas_call(
        functools.partial(early_kernel, size),
        out_shape=[
            SHAPE((order, order), BF16),
            SHAPE((rows, order), F32),
            SHAPE((rows, order), F32),
            SHAPE((order, order), BF16),
            SHAPE((rows, order), BF16),
        ],
        grid_spec=pltpu.PrefetchScalarGridSpec(
            num_scalar_prefetch=1,
            grid=(order // WIDTH,),
            in_specs=[
                whole_spec((order, order)),
                whole_spec((rows, order)),
                whole_spec((rows, order)),
                along_spec(rows),
            ]
            + [ANY] * len(sources),
            out_specs=[along_spec(order), along_spec(rows), along_spec(rows), down_spec(order), along_spec(rows)],
            scratch_shapes=[pltpu.VMEM((order, order), BF16), pltpu.SemaphoreType.DMA((size,))],
        ),
        compiler_params=pltpu.CompilerParams(vmem_limit_bytes=26 * 1024 * 1024),
        cost_estimate=FREE,
    )(flags, prev_whole, prev_rows, own_rows, separator, *sources)


def late_kernel(
    size, flags, reciprocal, prev_rows, mine, own, scale, late_scale, from_below, from_above, far,
    ready, link, corner, scaled, left_diag, right_diag, raw, sem,
):
    del ready
    place = flags[1]
    step = pl.program_id(0)
    width = own.shape[0]
    here = pl.ds(pl.multiple_of(step * width, width), width)

    @pl.when(step == 0)
    def _():
        for chosen, source in (
            (place == 0, from_above),
            (place == size - 1, from_below),
            (jnp.logical_and(place != 0, place != size - 1), far),
        ):
            copy = pltpu.make_async_copy(source, raw, sem)
            pl.when(chosen)(copy.start)
            pl.when(chosen)(copy.wait)
        scaled[...] = (raw[...].astype(F32) * reciprocal[0:1]).astype(BF16)

    link[:, here] = jnp.where(flags[0] == 1, 0.0, -dot_nt(scaled[...], own[...])).astype(BF16)

    @pl.when(step == pl.num_programs(0) - 1)
    def _():
        late = link[...]
        square = late * late
        keep = jnp.where(flags[2] == 1, 1.0, 0.0)
        ours = mine[...] * scale[0:1]
        corner[...] = (dot_nt(prev_rows[...], scaled[...]) + keep * dot_nt(ours, late)).astype(BF16)
        left_diag[...] = dot_nt(scale[...], square)
        right_diag[...] = dot_nn(late_scale[...], square)


def late_forms(
    flags, reciprocal, prev_rows, mine, own, scale, late_scale, from_below, from_above, far, ready
):
    rows, order = prev_rows.shape
    size = order // rows
    width = 512
    return pl.pallas_call(
        functools.partial(late_kernel, size),
        out_shape=[
            SHAPE((rows, order), BF16),
            SHAPE((rows, rows), BF16),
            SHAPE((rows, order), BF16),
            SHAPE((8, rows), F32),
            SHAPE((8, order), F32),
        ],
        grid_spec=pltpu.PrefetchScalarGridSpec(
            num_scalar_prefetch=1,
            grid=(order // width,),
            in_specs=[
                whole_spec((8, order)),
                whole_spec((rows, order)),
                whole_spec((rows, order)),
                pl.BlockSpec((width, order), lambda j, f: (j, 0)),
                whole_spec((8, order)),
                whole_spec((8, rows)),
                ANY,
                ANY,
                ANY,
                ANY,
            ],
            out_specs=[
                whole_spec((rows, order)),
                whole_spec((rows, rows)),
                whole_spec((rows, order)),
                whole_spec((8, rows)),
                whole_spec((8, order)),
            ],
            scratch_shapes=[pltpu.VMEM((rows, order), BF16), pltpu.SemaphoreType.DMA],
        ),
        compiler_params=pltpu.CompilerParams(vmem_limit_bytes=18 * 1024 * 1024),
    )(
        flags, reciprocal, prev_rows, mine, own, scale, late_scale, from_below, from_above, far, ready
    )


def level_kernel(flags, link, mine, scale, pivot_scale, form, update, left_diag, right_diag):
    part = link[...]
    scaled = mine[...] * scale[0:1]
    keep = jnp.where(flags[2] == 1, 1.0, 0.0)
    update[...] = (form[...] + keep * dot_nt(scaled, part)).astype(BF16)
    square = part * part
    left_diag[...] = dot_nt(scale[...], square)

    @pl.when(pl.program_id(0) == 0)
    def _():
        right_diag[...] = jnp.zeros_like(right_diag)

    right_diag[...] += dot_nn(pivot_scale[...], square)


def level_forms(flags, link, mine, scale, pivot_scale, form):
    rows, order = form.shape
    width = 512
    along = lambda count: pl.BlockSpec((count, width), lambda j, f: (0, j))
    return pl.pallas_call(
        level_kernel,
        out_shape=[SHAPE((rows, order), BF16), SHAPE((8, order), F32), SHAPE((8, order), F32)],
        grid_spec=pltpu.PrefetchScalarGridSpec(
            num_scalar_prefetch=1,
            grid=(order // width,),
            in_specs=[
                pl.BlockSpec((width, order), lambda j, f: (j, 0)),
                whole_spec((rows, order)),
                whole_spec((8, order)),
                along(8),
                along(rows),
            ],
            out_specs=[along(rows), along(8), whole_spec((8, order))],
        ),
        compiler_params=pltpu.CompilerParams(vmem_limit_bytes=18 * 1024 * 1024),
        cost_estimate=FREE,
    )(flags, link, mine, scale, pivot_scale, form)


def fetched(early, late, whole, sems, at):
    rows, order = late.shape
    size = order // rows
    place = at[0]
    low = place < size // 2
    spans = [pl.ds(spot * rows, rows) for spot in range(size)]
    copies = []
    for spot, span in enumerate(spans):
        plain = pltpu.make_async_copy(early.at[span], whole.at[span], sems.at[spot])
        if spot not in (0, size - 1):
            copies.append((True, plain))
            continue
        is_late = low if spot else jnp.logical_not(low)
        copies.append((jnp.logical_not(is_late), plain))
        copies.append((is_late, pltpu.make_async_copy(late, whole.at[span], sems.at[spot])))
    for chosen, copy in copies:
        pl.when(chosen)(copy.start) if chosen is not True else copy.start()

    def wait():
        for chosen, copy in copies:
            pl.when(chosen)(copy.wait) if chosen is not True else copy.wait()

    return wait


def times(block, factors):
    return (block.astype(F32) * factors[0:1].astype(F32)).astype(BF16)


def columns_kernel(
    flags, own, pivot_scale, prev_early, prev_late, pivot_whole, update, ready,
    right, columns, moved, prev, pivot, sems, pivot_sem, move_sem,
):
    del ready
    move = pltpu.make_async_copy(update, moved, move_sem)
    move.start()
    wait_prev = fetched(prev_early, prev_late, prev, sems, [flags[1]])
    copy = pltpu.make_async_copy(pivot_whole, pivot, pivot_sem)
    copy.start()
    wait_prev()
    across = jnp.where(flags[0] == 1, 0.0, -dot_nt(own[...], prev[...])).astype(BF16)
    across = times(across, pivot_scale)
    right[...] = across
    copy.wait()
    columns[...] = (-dot_nt(across, pivot[...])).astype(BF16)
    move.wait()


def columns_forms(flags, own, pivot_scale, prev_early, prev_late, pivot, update, ready):
    rows, order = own.shape
    out = SHAPE((rows, order), BF16)
    return pl.pallas_call(
        columns_kernel,
        out_shape=[out, out, out],
        grid_spec=pltpu.PrefetchScalarGridSpec(
            num_scalar_prefetch=1,
            grid=(1,),
            in_specs=[whole_spec((rows, order)), whole_spec((8, order))] + [ANY] * 5,
            out_specs=[whole_spec((rows, order)), whole_spec((rows, order)), ANY],
            scratch_shapes=[
                pltpu.VMEM((order, order), BF16),
                pltpu.VMEM((order, order), BF16),
                pltpu.SemaphoreType.DMA((order // rows,)),
                pltpu.SemaphoreType.DMA,
                pltpu.SemaphoreType.DMA,
            ],
        ),
        compiler_params=pltpu.CompilerParams(vmem_limit_bytes=22 * 1024 * 1024),
        cost_estimate=FREE,
    )(flags, own, pivot_scale, prev_early, prev_late, pivot, update, ready)


def last_kernel(
    flags, pivot_rows, right, columns, next_rows, mine, partial, pivot_scale,
    link_whole, pivot_whole, form, new, link, pivot, sems,
):
    rows = right.shape[0]
    copies = [
        pltpu.make_async_copy(pivot_whole, pivot, sems.at[0]),
        pltpu.make_async_copy(link_whole, link, sems.at[1]),
    ]
    for copy in copies:
        copy.start()
    scale = pivot_rows[rows : rows + 8, :]
    both = jnp.concatenate([times(columns[...], scale), times(pivot_rows[0:rows, :], scale)])
    copies[0].wait()
    inner = dot_nn(both, pivot[...]) * pivot_scale[0:1].astype(F32)
    keep = jnp.where(flags[3] == 1, 1.0, 0.0)
    factor = (right[...].astype(F32) - inner[0:rows] * keep).astype(BF16)
    both = jnp.concatenate([factor, inner[rows:].astype(BF16)])
    copies[1].wait()
    both = dot_nn(both, link[...])
    odd = jnp.where(flags[2] == 1, 0.0, 1.0)
    form[...] = partial[...] - odd * both[0:rows]
    last = both[rows:].astype(BF16)
    new[...] = jnp.where(flags[3] == 1, last, jnp.where(flags[2] == 1, mine[...], next_rows[...]))


def last_forms(flags, pivot_rows, right, columns, next_rows, mine, partial, pivot_scale, link, pivot):
    rows, order = right.shape
    return pl.pallas_call(
        last_kernel,
        out_shape=[SHAPE((rows, order), F32), SHAPE((rows, order), BF16)],
        grid_spec=pltpu.PrefetchScalarGridSpec(
            num_scalar_prefetch=1,
            grid=(1,),
            in_specs=[whole_spec(pivot_rows.shape)]
            + [whole_spec((rows, order))] * 5
            + [whole_spec((8, order)), ANY, ANY],
            out_specs=[whole_spec((rows, order)), whole_spec((rows, order))],
            scratch_shapes=[
                pltpu.VMEM((order, order), BF16),
                pltpu.VMEM((order, order), BF16),
                pltpu.SemaphoreType.DMA((2,)),
            ],
        ),
        compiler_params=pltpu.CompilerParams(vmem_limit_bytes=36 * 1024 * 1024),
        cost_estimate=FREE,
    )(flags, pivot_rows, right, columns, next_rows, mine, partial, pivot_scale, link, pivot)


def on_device(sep_block, own_couple, prev_couple, inner_diag):
    separator = sep_block[0]
    own_rows = own_couple[0]
    prev_rows = prev_couple[0]
    reciprocal = 1.0 / inner_diag[0]
    rows, order = own_rows.shape
    place = lax.axis_index("space")
    size = lax.axis_size("space")
    row_start = place * rows
    partition = lax.axis_index("tm")
    parts = lax.axis_size("tm")

    def between(block, route):
        return lax.ppermute(block, "tm", [(a, b) for a, b in route if 0 <= b < parts])

    even = range(0, parts, 2)
    pivots = range(1, parts, 4)
    everyone = range(parts)

    def one_step(ahead, back, step):
        up = [(j, j + 1) for j in range(step - 1, size - 1)]
        down = [(j, j - 1) for j in range(1, size - step + 1)]
        return lax.ppermute(ahead, "space", up), lax.ppermute(back, "space", down)

    def block_at(arrived, spot):
        block = arrived[0][0]
        for step in range(1, len(arrived)):
            if spot + step < size:
                block = jnp.where(place == spot + step, arrived[step][0], block)
            if spot - step >= 0:
                block = jnp.where(place == spot - step, arrived[step][1], block)
        return block

    is_first = partition == 0
    is_pivot = partition % 2 == 0
    is_receiver = partition % 2 == 1
    is_last = partition % 4 == 3
    flags = jnp.stack(
        [is_first.astype(jnp.int32), place, is_pivot.astype(jnp.int32), is_last.astype(jnp.int32)]
    )
    own_long = opening(flags, own_rows, prev_rows, separator, rows_of(reciprocal))
    own_arrived = [(own_long, own_long)]
    prev_arrived = [(prev_rows, prev_rows)]
    for step in range(1, size):
        own_arrived.append(one_step(*own_arrived[-1], step))
        prev_arrived.append(one_step(*prev_arrived[-1], step))
    words_arrived = [tuple(block[rows:] for block in pair) for pair in own_arrived]

    left_side = place < size // 2
    late_start = jnp.where(left_side, size - 1, 0) * rows
    is_end = jnp.logical_or(place == 0, place == size - 1)
    prev_blocks = [block_at(prev_arrived[:-1], spot) for spot in range(size)]
    zero = jnp.zeros_like(prev_rows)
    prev_blocks[0] = jnp.where(place == size - 1, zero, prev_blocks[0])
    prev_blocks[-1] = jnp.where(place == 0, zero, prev_blocks[-1])
    prev_first = jnp.concatenate(prev_blocks)
    prev_far = jnp.where(left_side, prev_blocks[-1], prev_blocks[0])
    prev_first, prev_far = lax.optimization_barrier((prev_first, prev_far))
    words = [block_at(words_arrived, spot) for spot in range(size)]

    def pair_sum(block, at):
        return block[at].astype(F32) + block[at + 1].astype(F32)

    part_diag = sum(pair_sum(block, 0) for block in words)
    part_diag = part_diag - jnp.concatenate([pair_sum(block, 2)[:rows] for block in words])
    prev_diag = jnp.concatenate([pair_sum(block, 4)[:rows] for block in words])
    part_diag, prev_diag = lax.optimization_barrier((part_diag, prev_diag))
    diag = part_diag - between(prev_diag, [(p, p - 1) for p in everyone])
    pivot_diag = between(part_diag, [(p, p + 1) for p in even]) - prev_diag
    scale = (1.0 / jnp.maximum(diag, 1.0)).astype(BF16)
    pivot_scale = (1.0 / jnp.maximum(pivot_diag, 1.0)).astype(BF16)

    own_scaled = scaled_by(own_rows, reciprocal)
    sources = [own_long]
    for up, down in own_arrived[1:]:
        sources += [up, down]
    prev_first = scaled_by(prev_first, reciprocal)
    link, partial, prev_form, own_full, mine = early_forms(
        flags, prev_first, prev_rows, own_scaled, separator, sources
    )
    scale8, pivot_scale8 = rows_of(scale), rows_of(pivot_scale)
    update, left_diag, right_diag = level_forms(flags, link, mine, scale8, pivot_scale8, prev_form)

    from_below, from_above = prev_arrived[-1]
    late_scale = lax.dynamic_slice_in_dim(pivot_scale, late_start, rows, 0)
    late_scale = jnp.where(is_end, late_scale, jnp.zeros_like(late_scale))
    late, corner, prev_late, left_late, right_late = late_forms(
        flags, rows_of(reciprocal), prev_rows, mine, own_full, scale8, rows_of(late_scale),
        from_below, from_above, prev_far, right_diag,
    )
    link = lax.dynamic_update_slice_in_dim(link, late, late_start, 0)
    pivot_link = between(link, [(p, p + 1) for p in even])
    update = lax.dynamic_update_slice_in_dim(update, corner, late_start, 1)
    left_diag = lax.dynamic_update_slice_in_dim(left_diag[0], left_late[0], late_start, 0)
    right_diag = right_diag[0] + right_late[0]

    left_diag = between(left_diag, [(p, p - 1) for p in even])
    from_even = between(update, [(p, p - 1) for p in even])
    next_diag = diag - left_diag - right_diag
    next_scale = (1.0 / jnp.maximum(next_diag, 1.0)).astype(BF16)
    pivot_rows = lax.dynamic_slice_in_dim(pivot_link, row_start, rows, 0)
    pivot_rows = lax.optimization_barrier(scaled_by(pivot_rows, pivot_scale))
    next_rows = (-dot_nn(pivot_rows, link)).astype(BF16)
    next_long = jnp.concatenate([next_rows, jnp.broadcast_to(next_scale[None, :], (EXTRA, order))])
    pivot_long = between(next_long, [(p, p + 2) for p in pivots])

    left_next = scaled_by(dot_nt(scaled_by(next_rows, next_scale), link), pivot_scale)
    left_next = lax.optimization_barrier(left_next)
    left_next = (-dot_nt(left_next, pivot_link)).astype(BF16)
    from_pivot = between(left_next, [(p, p - 2) for p in pivots])
    right, columns, own_update = columns_forms(
        flags, own_rows, pivot_scale8, prev_first, prev_late, pivot_link, update, left_next
    )
    from_odd = between(own_update, [(p, p - 1) for p in range(1, parts, 2)])
    form, out_link = last_forms(
        flags, pivot_long, right, columns, next_rows, mine, partial, pivot_scale8, link, pivot_link
    )
    schur = form - (from_even + from_odd).astype(F32) - from_pivot.astype(F32)
    return (schur[None], out_link[None])


def solution(mesh):
    placed = (P("tm", "space", None), P("tm", "space", None), P("tm", "space", None), P("tm", None))
    return jax.shard_map(
        on_device,
        mesh=mesh,
        in_specs=placed,
        out_specs=(P("tm", "space", None), P("tm", "space", None)),
        check_vma=False,
    )
```

```python
import functools

import jax
import jax.numpy as jnp
from jax import lax
from jax.experimental import pallas as pl
from jax.experimental.pallas import tpu as pltpu
from jax.sharding import PartitionSpec as P

BF16 = jnp.bfloat16
F32 = jnp.float32
EXTRA = 16
WIDTH = 256

ANY = pl.BlockSpec(memory_space=pl.ANY)
SHAPE = jax.ShapeDtypeStruct
FREE = pl.CostEstimate(flops=0, bytes_accessed=0, transcendentals=0)


def after(block, *others):
    def body(*refs):
        del refs

    return pl.pallas_call(
        body,
        out_shape=SHAPE(block.shape, block.dtype),
        in_specs=[ANY] * (1 + len(others)),
        out_specs=ANY,
        input_output_aliases={0: 0},
    )(block, *others)


def scaled_by(matrix, factors):
    return (matrix.astype(F32) * factors.astype(F32)[None, :]).astype(BF16)


def row_scaled_by(matrix, factors):
    return (matrix.astype(F32) * factors.astype(F32)[:, None]).astype(BF16)


def dot_nt(left, right):
    return lax.dot_general(left, right, (((1,), (1,)), ((), ())), preferred_element_type=F32)


def dot_nn(left, right):
    return lax.dot_general(left, right, (((1,), (0,)), ((), ())), preferred_element_type=F32)


def dot_tn(left, right):
    return lax.dot_general(left, right, (((0,), (0,)), ((), ())), preferred_element_type=F32)


def rows_of(scale):
    return jnp.broadcast_to(scale[None, :], (8, scale.shape[0]))


def products_cost(rows, order, count):
    return pl.CostEstimate(
        flops=2 * count * rows * order * order, bytes_accessed=2 * count * order * order, transcendentals=0
    )


def whole_spec(shape):
    return pl.BlockSpec(shape, lambda j, f: (0,) * len(shape), pipeline_mode=pl.Buffered(1))


def along_spec(count):
    return pl.BlockSpec((count, WIDTH), lambda j, f: (0, j))


def down_spec(count):
    return pl.BlockSpec((WIDTH, count), lambda j, f: (j, 0))


def opening_kernel(flags, own, prev, separator, reciprocal, long):
    rows, order = own.shape
    row_ids = lax.broadcasted_iota(jnp.int32, (rows, rows), 0)
    col_ids = lax.broadcasted_iota(jnp.int32, (rows, rows), 1)
    on_diagonal = jnp.where(row_ids == col_ids, separator[...], 0.0)
    ones = jnp.ones((8, order), BF16)

    def split(value):
        high = value.astype(BF16)
        return high, (value - high.astype(F32)).astype(BF16)

    def form_diagonal(block):
        wide = block.astype(F32)
        high, low = split((wide * reciprocal[0:1]).astype(BF16).astype(F32) * wide)
        return (dot_nt(ones, high) + dot_nt(ones, low))[0:1]

    def placed(words, count):
        ids = lax.broadcasted_iota(jnp.int32, (EXTRA, count), 0)
        total = jnp.zeros((EXTRA, count), F32)
        for at, word in words.items():
            total = jnp.where(ids == at, word.astype(F32), total)
        return total.astype(BF16)

    long[0:rows, :] = own[...]
    long[rows:, :] = jnp.zeros((EXTRA, order), BF16)
    own_high, own_low = split(jnp.sum(on_diagonal, axis=0, keepdims=True) - form_diagonal(own[...]))
    prev_high, prev_low = split(form_diagonal(prev[...]))
    long[rows:, 0:rows] = placed({0: own_high, 1: own_low, 2: prev_high, 3: prev_low}, rows)


def opening(flags, own, prev, separator, reciprocal):
    rows, order = own.shape
    return pl.pallas_call(
        opening_kernel,
        out_shape=SHAPE((rows + EXTRA, order), BF16),
        grid_spec=pltpu.PrefetchScalarGridSpec(
            num_scalar_prefetch=1,
            grid=(1,),
            in_specs=[whole_spec((rows, order))] * 2 + [whole_spec((rows, rows)), whole_spec((8, order))],
            out_specs=whole_spec((rows + EXTRA, order)),
        ),
        compiler_params=pltpu.CompilerParams(vmem_limit_bytes=32 * 1024 * 1024),
        cost_estimate=FREE,
    )(flags, own, prev, separator, reciprocal)


def early_kernel(size, flags, prev_whole, prev_rows, own_rows, separator, *refs):
    sources = refs[: 2 * size - 1]
    link, partial, form, own_out, mine, own, sems = refs[2 * size + 1 :]
    rows = separator.shape[0]
    step = pl.program_id(0)
    here = pl.ds(pl.multiple_of(step * WIDTH, WIDTH), WIDTH)

    def copies():
        for spot in range(size):
            for by, source in enumerate(sources):
                distance = (by + 1) // 2 if by % 2 else -(by // 2)
                target = own.at[pl.ds(spot * rows, rows)]
                copy = pltpu.make_async_copy(source.at[pl.ds(0, rows)], target, sems.at[spot])
                yield flags[1] - spot == distance, copy

    @pl.when(step == 0)
    def _():
        for chosen, copy in copies():
            pl.when(chosen)(copy.start)
        for chosen, copy in copies():
            pl.when(chosen)(copy.wait)

    block = own[here, :]
    own_out[...] = block
    link[...] = jnp.where(flags[0] == 1, 0.0, -dot_nt(prev_whole[...], block)).astype(BF16)
    mine[...] = link[pl.ds(pl.multiple_of(flags[1] * rows, rows), rows), :]
    partial[...] = separator[...] - dot_nt(own_rows[...], block)
    form[...] = dot_nt(prev_rows[...], prev_whole[here, :])


def early_forms(flags, prev_whole, prev_rows, own_rows, separator, sources):
    rows, order = own_rows.shape
    size = order // rows
    return pl.pallas_call(
        functools.partial(early_kernel, size),
        out_shape=[
            SHAPE((order, order), BF16),
            SHAPE((rows, order), F32),
            SHAPE((rows, order), F32),
            SHAPE((order, order), BF16),
            SHAPE((rows, order), BF16),
        ],
        grid_spec=pltpu.PrefetchScalarGridSpec(
            num_scalar_prefetch=1,
            grid=(order // WIDTH,),
            in_specs=[
                whole_spec((order, order)),
                whole_spec((rows, order)),
                whole_spec((rows, order)),
                along_spec(rows),
            ]
            + [ANY] * len(sources),
            out_specs=[along_spec(order), along_spec(rows), along_spec(rows), down_spec(order), along_spec(rows)],
            scratch_shapes=[pltpu.VMEM((order, order), BF16), pltpu.SemaphoreType.DMA((size,))],
        ),
        compiler_params=pltpu.CompilerParams(vmem_limit_bytes=26 * 1024 * 1024),
        cost_estimate=FREE,
    )(flags, prev_whole, prev_rows, own_rows, separator, *sources)


def late_kernel(
    size, flags, reciprocal, prev_rows, own, from_below, from_above, far, link, corner, scaled, raw, sem
):
    place = flags[1]
    step = pl.program_id(0)
    width = own.shape[0]
    here = pl.ds(pl.multiple_of(step * width, width), width)

    @pl.when(step == 0)
    def _():
        for chosen, source in (
            (place == 0, from_above),
            (place == size - 1, from_below),
            (jnp.logical_and(place != 0, place != size - 1), far),
        ):
            copy = pltpu.make_async_copy(source, raw, sem)
            pl.when(chosen)(copy.start)
            pl.when(chosen)(copy.wait)
        scaled[...] = (raw[...].astype(F32) * reciprocal[0:1]).astype(BF16)
        corner[...] = dot_nt(prev_rows[...], scaled[...])

    link[:, here] = jnp.where(flags[0] == 1, 0.0, -dot_nt(scaled[...], own[...])).astype(BF16)


def late_forms(flags, reciprocal, prev_rows, own, from_below, from_above, far):
    rows, order = prev_rows.shape
    size = order // rows
    width = 512
    return pl.pallas_call(
        functools.partial(late_kernel, size),
        out_shape=[SHAPE((rows, order), BF16), SHAPE((rows, rows), F32), SHAPE((rows, order), BF16)],
        grid_spec=pltpu.PrefetchScalarGridSpec(
            num_scalar_prefetch=1,
            grid=(order // width,),
            in_specs=[
                whole_spec((8, order)),
                whole_spec((rows, order)),
                pl.BlockSpec((width, order), lambda j, f: (j, 0)),
                ANY,
                ANY,
                ANY,
            ],
            out_specs=[whole_spec((rows, order)), whole_spec((rows, rows)), whole_spec((rows, order))],
            scratch_shapes=[pltpu.VMEM((rows, order), BF16), pltpu.SemaphoreType.DMA],
        ),
        compiler_params=pltpu.CompilerParams(vmem_limit_bytes=18 * 1024 * 1024),
    )(flags, reciprocal, prev_rows, own, from_below, from_above, far)


def level_kernel(flags, link, mine, scale, pivot_scale, form, update, left_diag, right_diag):
    part = link[...]
    scaled = mine[...] * scale[0:1]
    keep = jnp.where(flags[2] == 1, 1.0, 0.0)
    update[...] = (form[...] + keep * dot_nt(scaled, part)).astype(BF16)
    square = part * part
    left_diag[...] = dot_nt(scale[...], square)

    @pl.when(pl.program_id(0) == 0)
    def _():
        right_diag[...] = jnp.zeros_like(right_diag)

    right_diag[...] += dot_nn(pivot_scale[...], square)


def level_forms(flags, link, mine, scale, pivot_scale, form):
    rows, order = form.shape
    width = 512
    along = lambda count: pl.BlockSpec((count, width), lambda j, f: (0, j))
    return pl.pallas_call(
        level_kernel,
        out_shape=[SHAPE((rows, order), BF16), SHAPE((8, order), F32), SHAPE((8, order), F32)],
        grid_spec=pltpu.PrefetchScalarGridSpec(
            num_scalar_prefetch=1,
            grid=(order // width,),
            in_specs=[
                pl.BlockSpec((width, order), lambda j, f: (j, 0)),
                whole_spec((rows, order)),
                whole_spec((8, order)),
                along(8),
                along(rows),
            ],
            out_specs=[along(rows), along(8), whole_spec((8, order))],
        ),
        compiler_params=pltpu.CompilerParams(vmem_limit_bytes=18 * 1024 * 1024),
        cost_estimate=FREE,
    )(flags, link, mine, scale, pivot_scale, form)


def fetched(early, late, whole, sems, at):
    rows, order = late.shape
    size = order // rows
    place = at[0]
    low = place < size // 2
    spans = [pl.ds(spot * rows, rows) for spot in range(size)]
    copies = []
    for spot, span in enumerate(spans):
        plain = pltpu.make_async_copy(early.at[span], whole.at[span], sems.at[spot])
        if spot not in (0, size - 1):
            copies.append((True, plain))
            continue
        is_late = low if spot else jnp.logical_not(low)
        copies.append((jnp.logical_not(is_late), plain))
        copies.append((is_late, pltpu.make_async_copy(late, whole.at[span], sems.at[spot])))
    for chosen, copy in copies:
        pl.when(chosen)(copy.start) if chosen is not True else copy.start()

    def wait():
        for chosen, copy in copies:
            pl.when(chosen)(copy.wait) if chosen is not True else copy.wait()

    return wait


def times(block, factors):
    return (block.astype(F32) * factors[0:1].astype(F32)).astype(BF16)


def columns_kernel(
    flags, own, pivot_scale, prev_early, prev_late, pivot_whole, update, ready,
    right, columns, moved, prev, pivot, sems, pivot_sem, move_sem,
):
    del ready
    move = pltpu.make_async_copy(update, moved, move_sem)
    move.start()
    wait_prev = fetched(prev_early, prev_late, prev, sems, [flags[1]])
    copy = pltpu.make_async_copy(pivot_whole, pivot, pivot_sem)
    copy.start()
    wait_prev()
    across = jnp.where(flags[0] == 1, 0.0, -dot_nt(own[...], prev[...])).astype(BF16)
    across = times(across, pivot_scale)
    right[...] = across
    copy.wait()
    columns[...] = (-dot_nt(across, pivot[...])).astype(BF16)
    move.wait()


def columns_forms(flags, own, pivot_scale, prev_early, prev_late, pivot, update, ready):
    rows, order = own.shape
    out = SHAPE((rows, order), BF16)
    return pl.pallas_call(
        columns_kernel,
        out_shape=[out, out, out],
        grid_spec=pltpu.PrefetchScalarGridSpec(
            num_scalar_prefetch=1,
            grid=(1,),
            in_specs=[whole_spec((rows, order)), whole_spec((8, order))] + [ANY] * 5,
            out_specs=[whole_spec((rows, order)), whole_spec((rows, order)), ANY],
            scratch_shapes=[
                pltpu.VMEM((order, order), BF16),
                pltpu.VMEM((order, order), BF16),
                pltpu.SemaphoreType.DMA((order // rows,)),
                pltpu.SemaphoreType.DMA,
                pltpu.SemaphoreType.DMA,
            ],
        ),
        compiler_params=pltpu.CompilerParams(vmem_limit_bytes=22 * 1024 * 1024),
        cost_estimate=products_cost(rows, order, 2),
    )(flags, own, pivot_scale, prev_early, prev_late, pivot, update, ready)


def last_kernel(
    flags, pivot_rows, right, columns, next_rows, mine, partial, pivot_scale,
    link_whole, pivot_whole, form, new, link, pivot, sems,
):
    rows = right.shape[0]
    copies = [
        pltpu.make_async_copy(pivot_whole, pivot, sems.at[0]),
        pltpu.make_async_copy(link_whole, link, sems.at[1]),
    ]
    for copy in copies:
        copy.start()
    scale = pivot_rows[rows : rows + 8, :]
    both = jnp.concatenate([times(columns[...], scale), times(pivot_rows[0:rows, :], scale)])
    copies[0].wait()
    inner = dot_nn(both, pivot[...]) * pivot_scale[0:1].astype(F32)
    keep = jnp.where(flags[3] == 1, 1.0, 0.0)
    factor = (right[...].astype(F32) - inner[0:rows] * keep).astype(BF16)
    both = jnp.concatenate([factor, inner[rows:].astype(BF16)])
    copies[1].wait()
    both = dot_nn(both, link[...])
    odd = jnp.where(flags[2] == 1, 0.0, 1.0)
    form[...] = partial[...] - odd * both[0:rows]
    last = both[rows:].astype(BF16)
    new[...] = jnp.where(flags[3] == 1, last, jnp.where(flags[2] == 1, mine[...], next_rows[...]))


def last_forms(flags, pivot_rows, right, columns, next_rows, mine, partial, pivot_scale, link, pivot):
    rows, order = right.shape
    return pl.pallas_call(
        last_kernel,
        out_shape=[SHAPE((rows, order), F32), SHAPE((rows, order), BF16)],
        grid_spec=pltpu.PrefetchScalarGridSpec(
            num_scalar_prefetch=1,
            grid=(1,),
            in_specs=[whole_spec(pivot_rows.shape)]
            + [whole_spec((rows, order))] * 5
            + [whole_spec((8, order)), ANY, ANY],
            out_specs=[whole_spec((rows, order)), whole_spec((rows, order))],
            scratch_shapes=[
                pltpu.VMEM((order, order), BF16),
                pltpu.VMEM((order, order), BF16),
                pltpu.SemaphoreType.DMA((2,)),
            ],
        ),
        compiler_params=pltpu.CompilerParams(vmem_limit_bytes=36 * 1024 * 1024),
        cost_estimate=products_cost(rows, order, 4),
    )(flags, pivot_rows, right, columns, next_rows, mine, partial, pivot_scale, link, pivot)


def on_device(sep_block, own_couple, prev_couple, inner_diag):
    separator = sep_block[0]
    own_rows = own_couple[0]
    prev_rows = prev_couple[0]
    reciprocal = 1.0 / inner_diag[0]
    rows, order = own_rows.shape
    place = lax.axis_index("space")
    size = lax.axis_size("space")
    row_start = place * rows
    partition = lax.axis_index("tm")
    parts = lax.axis_size("tm")

    def between(block, route):
        return lax.ppermute(block, "tm", [(a, b) for a, b in route if 0 <= b < parts])

    even = range(0, parts, 2)
    pivots = range(1, parts, 4)
    everyone = range(parts)

    def one_step(ahead, back, step):
        up = [(j, j + 1) for j in range(step - 1, size - 1)]
        down = [(j, j - 1) for j in range(1, size - step + 1)]
        return lax.ppermute(ahead, "space", up), lax.ppermute(back, "space", down)

    def block_at(arrived, spot):
        block = arrived[0][0]
        for step in range(1, len(arrived)):
            if spot + step < size:
                block = jnp.where(place == spot + step, arrived[step][0], block)
            if spot - step >= 0:
                block = jnp.where(place == spot - step, arrived[step][1], block)
        return block

    is_first = partition == 0
    is_pivot = partition % 2 == 0
    is_receiver = partition % 2 == 1
    is_last = partition % 4 == 3
    flags = jnp.stack(
        [is_first.astype(jnp.int32), place, is_pivot.astype(jnp.int32), is_last.astype(jnp.int32)]
    )
    diagonal_block = lax.dynamic_slice_in_dim(separator, row_start, rows, 1)
    own_long = opening(flags, own_rows, prev_rows, diagonal_block, rows_of(reciprocal))
    own_arrived = [(own_long, own_long)]
    prev_arrived = [(prev_rows, prev_rows)]
    for step in range(1, size):
        own_arrived.append(one_step(*own_arrived[-1], step))
        prev_arrived.append(one_step(*prev_arrived[-1], step))
    words_arrived = [tuple(block[rows:] for block in pair) for pair in own_arrived]

    left_side = place < size // 2
    late_start = jnp.where(left_side, size - 1, 0) * rows
    is_end = jnp.logical_or(place == 0, place == size - 1)
    prev_blocks = [block_at(prev_arrived[:-1], spot) for spot in range(size)]
    zero = jnp.zeros_like(prev_rows)
    prev_blocks[0] = jnp.where(place == size - 1, zero, prev_blocks[0])
    prev_blocks[-1] = jnp.where(place == 0, zero, prev_blocks[-1])
    prev_first = jnp.concatenate(prev_blocks)
    prev_far = jnp.where(left_side, prev_blocks[-1], prev_blocks[0])
    prev_first, prev_far = lax.optimization_barrier((prev_first, prev_far))
    words = [block_at(words_arrived, spot) for spot in range(size)]

    def pair_sum(block, at):
        return block[at].astype(F32) + block[at + 1].astype(F32)

    part_diag = jnp.concatenate([pair_sum(block, 0)[:rows] for block in words])
    prev_diag = jnp.concatenate([pair_sum(block, 2)[:rows] for block in words])
    part_diag, prev_diag = lax.optimization_barrier((part_diag, prev_diag))
    diag = part_diag - between(prev_diag, [(p, p - 1) for p in everyone])
    pivot_diag = between(part_diag, [(p, p + 1) for p in even]) - prev_diag
    scale = (1.0 / jnp.maximum(diag, 1.0)).astype(BF16)
    pivot_scale = (1.0 / jnp.maximum(pivot_diag, 1.0)).astype(BF16)

    own_scaled = scaled_by(own_rows, reciprocal)
    sources = [own_long]
    for up, down in own_arrived[1:]:
        sources += [up, down]
    sources += [scale, pivot_scale]
    prev_first = scaled_by(prev_first, reciprocal)
    link, partial, prev_form, own_full, mine = early_forms(
        flags, prev_first, prev_rows, own_scaled, separator, sources
    )
    scale8, pivot_scale8 = rows_of(scale), rows_of(pivot_scale)

    from_below, from_above = prev_arrived[-1]
    late, corner, prev_late = late_forms(
        flags, rows_of(reciprocal), prev_rows, own_full, from_below, from_above, prev_far
    )
    link = lax.dynamic_update_slice_in_dim(link, late, late_start, 0)
    pivot_link = between(link, [(p, p + 1) for p in even])
    prev_form = lax.dynamic_update_slice_in_dim(prev_form, corner, late_start, 1)
    update, left_diag, right_diag = level_forms(flags, link, mine, scale8, pivot_scale8, prev_form)
    left_diag, right_diag = left_diag[0], right_diag[0]

    left_diag = between(left_diag, [(p, p - 1) for p in even])
    from_even = between(update, [(p, p - 1) for p in even])
    next_diag = diag - left_diag - right_diag
    next_scale = (1.0 / jnp.maximum(next_diag, 1.0)).astype(BF16)
    pivot_rows = lax.dynamic_slice_in_dim(pivot_link, row_start, rows, 0)
    pivot_rows = lax.optimization_barrier(scaled_by(pivot_rows, pivot_scale))
    next_rows = (-dot_nn(pivot_rows, link)).astype(BF16)
    next_long = jnp.concatenate([next_rows, jnp.broadcast_to(next_scale[None, :], (EXTRA, order))])
    pivot_long = between(next_long, [(p, p + 2) for p in pivots])

    left_next = scaled_by(dot_nt(scaled_by(next_rows, next_scale), link), pivot_scale)
    left_next = lax.optimization_barrier(left_next)
    left_next = (-dot_nt(left_next, pivot_link)).astype(BF16)
    from_pivot = between(left_next, [(p, p - 2) for p in pivots])
    right, columns, own_update = columns_forms(
        flags, own_rows, pivot_scale8, prev_first, prev_late, pivot_link, update, left_next
    )
    from_odd = between(own_update, [(p, p - 1) for p in range(1, parts, 2)])
    form, out_link = last_forms(
        flags, pivot_long, right, columns, next_rows, mine, partial, pivot_scale8, link, pivot_link
    )
    schur = form - (from_even + from_odd).astype(F32) - from_pivot.astype(F32)
    return (schur[None], out_link[None])


def solution(mesh):
    placed = (P("tm", "space", None), P("tm", "space", None), P("tm", "space", None), P("tm", None))
    return jax.shard_map(
        on_device,
        mesh=mesh,
        in_specs=placed,
        out_specs=(P("tm", "space", None), P("tm", "space", None)),
        check_vma=False,
    )
```

```python
import functools

import jax
import jax.numpy as jnp
from jax import lax
from jax.experimental import pallas as pl
from jax.experimental.pallas import tpu as pltpu
from jax.sharding import PartitionSpec as P

BF16 = jnp.bfloat16
F32 = jnp.float32
EXTRA = 16
WIDTH = 256

ANY = pl.BlockSpec(memory_space=pl.ANY)
SHAPE = jax.ShapeDtypeStruct
FREE = pl.CostEstimate(flops=0, bytes_accessed=0, transcendentals=0)


def after(block, *others):
    def body(*refs):
        del refs

    return pl.pallas_call(
        body,
        out_shape=SHAPE(block.shape, block.dtype),
        in_specs=[ANY] * (1 + len(others)),
        out_specs=ANY,
        input_output_aliases={0: 0},
    )(block, *others)


def scaled_by(matrix, factors):
    return (matrix.astype(F32) * factors.astype(F32)[None, :]).astype(BF16)


def row_scaled_by(matrix, factors):
    return (matrix.astype(F32) * factors.astype(F32)[:, None]).astype(BF16)


def dot_nt(left, right):
    return lax.dot_general(left, right, (((1,), (1,)), ((), ())), preferred_element_type=F32)


def dot_nn(left, right):
    return lax.dot_general(left, right, (((1,), (0,)), ((), ())), preferred_element_type=F32)


def dot_tn(left, right):
    return lax.dot_general(left, right, (((0,), (0,)), ((), ())), preferred_element_type=F32)


def rows_of(scale):
    return jnp.broadcast_to(scale[None, :], (8, scale.shape[0]))


def products_cost(rows, order, count):
    return pl.CostEstimate(
        flops=2 * count * rows * order * order, bytes_accessed=2 * count * order * order, transcendentals=0
    )


def whole_spec(shape):
    return pl.BlockSpec(shape, lambda j, f: (0,) * len(shape), pipeline_mode=pl.Buffered(1))


def along_spec(count):
    return pl.BlockSpec((count, WIDTH), lambda j, f: (0, j))


def down_spec(count):
    return pl.BlockSpec((WIDTH, count), lambda j, f: (j, 0))


def opening_kernel(flags, own, prev, separator, reciprocal, long):
    rows, order = own.shape
    row_ids = lax.broadcasted_iota(jnp.int32, (rows, rows), 0)
    col_ids = lax.broadcasted_iota(jnp.int32, (rows, rows), 1)
    on_diagonal = jnp.where(row_ids == col_ids, separator[...], 0.0)
    ones = jnp.ones((8, order), BF16)

    def split(value):
        high = value.astype(BF16)
        return high, (value - high.astype(F32)).astype(BF16)

    def form_diagonal(block):
        wide = block.astype(F32)
        high, low = split((wide * reciprocal[0:1]).astype(BF16).astype(F32) * wide)
        return (dot_nt(ones, high) + dot_nt(ones, low))[0:1]

    def placed(words, count):
        ids = lax.broadcasted_iota(jnp.int32, (EXTRA, count), 0)
        total = jnp.zeros((EXTRA, count), F32)
        for at, word in words.items():
            total = jnp.where(ids == at, word.astype(F32), total)
        return total.astype(BF16)

    long[0:rows, :] = own[...]
    long[rows:, :] = jnp.zeros((EXTRA, order), BF16)
    own_high, own_low = split(jnp.sum(on_diagonal, axis=0, keepdims=True) - form_diagonal(own[...]))
    prev_high, prev_low = split(form_diagonal(prev[...]))
    long[rows:, 0:rows] = placed({0: own_high, 1: own_low, 2: prev_high, 3: prev_low}, rows)


def opening(flags, own, prev, separator, reciprocal):
    rows, order = own.shape
    return pl.pallas_call(
        opening_kernel,
        out_shape=SHAPE((rows + EXTRA, order), BF16),
        grid_spec=pltpu.PrefetchScalarGridSpec(
            num_scalar_prefetch=1,
            grid=(1,),
            in_specs=[whole_spec((rows, order))] * 2 + [whole_spec((rows, rows)), whole_spec((8, order))],
            out_specs=whole_spec((rows + EXTRA, order)),
        ),
        compiler_params=pltpu.CompilerParams(vmem_limit_bytes=32 * 1024 * 1024),
        cost_estimate=FREE,
    )(flags, own, prev, separator, reciprocal)


def early_kernel(size, flags, prev_whole, prev_rows, own_rows, separator, *refs):
    sources = refs[: 2 * size - 1]
    link, partial, form, own_out, mine, own, sems = refs[2 * size + 1 :]
    rows = separator.shape[0]
    step = pl.program_id(0)
    here = pl.ds(pl.multiple_of(step * WIDTH, WIDTH), WIDTH)

    def copies():
        for spot in range(size):
            for by, source in enumerate(sources):
                distance = (by + 1) // 2 if by % 2 else -(by // 2)
                target = own.at[pl.ds(spot * rows, rows)]
                copy = pltpu.make_async_copy(source.at[pl.ds(0, rows)], target, sems.at[spot])
                yield flags[1] - spot == distance, copy

    @pl.when(step == 0)
    def _():
        for chosen, copy in copies():
            pl.when(chosen)(copy.start)
        for chosen, copy in copies():
            pl.when(chosen)(copy.wait)

    block = own[here, :]
    own_out[...] = block
    link[...] = jnp.where(flags[0] == 1, 0.0, -dot_nt(prev_whole[...], block)).astype(BF16)
    mine[...] = link[pl.ds(pl.multiple_of(flags[1] * rows, rows), rows), :]
    partial[...] = separator[...] - dot_nt(own_rows[...], block)
    form[...] = dot_nt(prev_rows[...], prev_whole[here, :])


def early_forms(flags, prev_whole, prev_rows, own_rows, separator, sources):
    rows, order = own_rows.shape
    size = order // rows
    return pl.pallas_call(
        functools.partial(early_kernel, size),
        out_shape=[
            SHAPE((order, order), BF16),
            SHAPE((rows, order), F32),
            SHAPE((rows, order), F32),
            SHAPE((order, order), BF16),
            SHAPE((rows, order), BF16),
        ],
        grid_spec=pltpu.PrefetchScalarGridSpec(
            num_scalar_prefetch=1,
            grid=(order // WIDTH,),
            in_specs=[
                whole_spec((order, order)),
                whole_spec((rows, order)),
                whole_spec((rows, order)),
                along_spec(rows),
            ]
            + [ANY] * len(sources),
            out_specs=[along_spec(order), along_spec(rows), along_spec(rows), down_spec(order), along_spec(rows)],
            scratch_shapes=[pltpu.VMEM((order, order), BF16), pltpu.SemaphoreType.DMA((size,))],
        ),
        compiler_params=pltpu.CompilerParams(vmem_limit_bytes=26 * 1024 * 1024),
        cost_estimate=FREE,
    )(flags, prev_whole, prev_rows, own_rows, separator, *sources)


def late_kernel(
    size, flags, reciprocal, prev_rows, own, from_below, from_above, far, link, corner, scaled, raw, sem
):
    place = flags[1]
    step = pl.program_id(0)
    width = own.shape[0]
    here = pl.ds(pl.multiple_of(step * width, width), width)

    @pl.when(step == 0)
    def _():
        for chosen, source in (
            (place == 0, from_above),
            (place == size - 1, from_below),
            (jnp.logical_and(place != 0, place != size - 1), far),
        ):
            copy = pltpu.make_async_copy(source, raw, sem)
            pl.when(chosen)(copy.start)
            pl.when(chosen)(copy.wait)
        scaled[...] = (raw[...].astype(F32) * reciprocal[0:1]).astype(BF16)
        corner[...] = dot_nt(prev_rows[...], scaled[...])

    link[:, here] = jnp.where(flags[0] == 1, 0.0, -dot_nt(scaled[...], own[...])).astype(BF16)


def late_forms(flags, reciprocal, prev_rows, own, from_below, from_above, far):
    rows, order = prev_rows.shape
    size = order // rows
    width = 512
    return pl.pallas_call(
        functools.partial(late_kernel, size),
        out_shape=[SHAPE((rows, order), BF16), SHAPE((rows, rows), F32), SHAPE((rows, order), BF16)],
        grid_spec=pltpu.PrefetchScalarGridSpec(
            num_scalar_prefetch=1,
            grid=(order // width,),
            in_specs=[
                whole_spec((8, order)),
                whole_spec((rows, order)),
                pl.BlockSpec((width, order), lambda j, f: (j, 0)),
                ANY,
                ANY,
                ANY,
            ],
            out_specs=[whole_spec((rows, order)), whole_spec((rows, rows)), whole_spec((rows, order))],
            scratch_shapes=[pltpu.VMEM((rows, order), BF16), pltpu.SemaphoreType.DMA],
        ),
        compiler_params=pltpu.CompilerParams(vmem_limit_bytes=18 * 1024 * 1024),
    )(flags, reciprocal, prev_rows, own, from_below, from_above, far)


def level_kernel(flags, link, mine, scale, pivot_scale, form, update, left_diag, right_diag):
    part = link[...]
    scaled = mine[...] * scale[0:1]
    keep = jnp.where(flags[2] == 1, 1.0, 0.0)
    update[...] = (form[...] + keep * dot_nt(scaled, part)).astype(BF16)
    square = part * part
    left_diag[...] = dot_nt(scale[...], square)

    @pl.when(pl.program_id(0) == 0)
    def _():
        right_diag[...] = jnp.zeros_like(right_diag)

    right_diag[...] += dot_nn(pivot_scale[...], square)


def level_forms(flags, link, mine, scale, pivot_scale, form):
    rows, order = form.shape
    width = 512
    along = lambda count: pl.BlockSpec((count, width), lambda j, f: (0, j))
    return pl.pallas_call(
        level_kernel,
        out_shape=[SHAPE((rows, order), BF16), SHAPE((8, order), F32), SHAPE((8, order), F32)],
        grid_spec=pltpu.PrefetchScalarGridSpec(
            num_scalar_prefetch=1,
            grid=(order // width,),
            in_specs=[
                pl.BlockSpec((width, order), lambda j, f: (j, 0)),
                whole_spec((rows, order)),
                whole_spec((8, order)),
                along(8),
                along(rows),
            ],
            out_specs=[along(rows), along(8), whole_spec((8, order))],
        ),
        compiler_params=pltpu.CompilerParams(vmem_limit_bytes=18 * 1024 * 1024),
        cost_estimate=FREE,
    )(flags, link, mine, scale, pivot_scale, form)


def fetched(early, late, whole, sems, at):
    rows, order = late.shape
    size = order // rows
    place = at[0]
    low = place < size // 2
    spans = [pl.ds(spot * rows, rows) for spot in range(size)]
    copies = []
    for spot, span in enumerate(spans):
        plain = pltpu.make_async_copy(early.at[span], whole.at[span], sems.at[spot])
        if spot not in (0, size - 1):
            copies.append((True, plain))
            continue
        is_late = low if spot else jnp.logical_not(low)
        copies.append((jnp.logical_not(is_late), plain))
        copies.append((is_late, pltpu.make_async_copy(late, whole.at[span], sems.at[spot])))
    for chosen, copy in copies:
        pl.when(chosen)(copy.start) if chosen is not True else copy.start()

    def wait():
        for chosen, copy in copies:
            pl.when(chosen)(copy.wait) if chosen is not True else copy.wait()

    return wait


def times(block, factors):
    return (block.astype(F32) * factors[0:1].astype(F32)).astype(BF16)


def columns_kernel(
    flags, own, pivot_scale, prev_early, prev_late, pivot_whole, update, received, ready,
    right, columns, moved, passed, prev, pivot, sems, pivot_sem, move_sems,
):
    del ready
    moves = [
        pltpu.make_async_copy(update, moved, move_sems.at[0]),
        pltpu.make_async_copy(received, passed, move_sems.at[1]),
    ]
    for move in moves:
        move.start()
    wait_prev = fetched(prev_early, prev_late, prev, sems, [flags[1]])
    copy = pltpu.make_async_copy(pivot_whole, pivot, pivot_sem)
    copy.start()
    wait_prev()
    across = jnp.where(flags[0] == 1, 0.0, -dot_nt(own[...], prev[...])).astype(BF16)
    across = times(across, pivot_scale)
    right[...] = across
    copy.wait()
    columns[...] = (-dot_nt(across, pivot[...])).astype(BF16)
    for move in moves:
        move.wait()


def columns_forms(flags, own, pivot_scale, prev_early, prev_late, pivot, update, received, ready):
    rows, order = own.shape
    out = SHAPE((rows, order), BF16)
    return pl.pallas_call(
        columns_kernel,
        out_shape=[out, out, out, out],
        grid_spec=pltpu.PrefetchScalarGridSpec(
            num_scalar_prefetch=1,
            grid=(1,),
            in_specs=[whole_spec((rows, order)), whole_spec((8, order))] + [ANY] * 6,
            out_specs=[whole_spec((rows, order)), whole_spec((rows, order)), ANY, ANY],
            scratch_shapes=[
                pltpu.VMEM((order, order), BF16),
                pltpu.VMEM((order, order), BF16),
                pltpu.SemaphoreType.DMA((order // rows,)),
                pltpu.SemaphoreType.DMA,
                pltpu.SemaphoreType.DMA((2,)),
            ],
        ),
        compiler_params=pltpu.CompilerParams(vmem_limit_bytes=22 * 1024 * 1024),
        cost_estimate=products_cost(rows, order, 2),
    )(flags, own, pivot_scale, prev_early, prev_late, pivot, update, received, ready)


def last_kernel(
    flags, pivot_rows, right, columns, pivot_scale, next_rows, mine, partial, link_whole, pivot_whole,
    form, new, link, pivot, last, sems,
):
    rows = right.shape[0]
    even, final = flags[2] == 1, flags[3] == 1
    other = jnp.logical_not(jnp.logical_or(even, final))
    fetch = [
        pltpu.make_async_copy(pivot_whole, pivot, sems.at[0]),
        pltpu.make_async_copy(link_whole, link, sems.at[1]),
        pltpu.make_async_copy(partial, form, sems.at[2]),
    ]
    for copy in fetch:
        copy.start()
    plain = [(even, pltpu.make_async_copy(mine, new, sems.at[3]))]
    plain.append((other, pltpu.make_async_copy(next_rows, new, sems.at[3])))
    for chosen, copy in plain:
        pl.when(chosen)(copy.start)
    scale = pivot_rows[rows : rows + EXTRA, :]
    wide = pivot_scale[0:1].astype(F32)
    fetch[0].wait()
    inner = dot_nn(times(columns[...], scale), pivot[...]) * wide
    keep = jnp.where(final, 1.0, 0.0)
    factor = (right[...].astype(F32) - inner * keep).astype(BF16)
    inner = (dot_nn(times(pivot_rows[0:rows, :], scale), pivot[...]) * wide).astype(BF16)
    fetch[1].wait()
    last[...] = dot_nn(inner, link[...]).astype(BF16)
    store = pltpu.make_async_copy(last, new, sems.at[3])
    pl.when(final)(store.start)
    fetch[2].wait()
    odd = jnp.where(even, 0.0, 1.0)
    form[...] -= odd * dot_nn(factor, link[...])
    for chosen, copy in plain + [(final, store)]:
        pl.when(chosen)(copy.wait)


def last_forms(flags, pivot_rows, right, columns, next_rows, mine, partial, pivot_scale, link, pivot):
    rows, order = right.shape
    return pl.pallas_call(
        last_kernel,
        out_shape=[SHAPE((rows, order), F32), SHAPE((rows, order), BF16)],
        grid_spec=pltpu.PrefetchScalarGridSpec(
            num_scalar_prefetch=1,
            grid=(1,),
            in_specs=[
                whole_spec(pivot_rows.shape),
                whole_spec((rows, order)),
                whole_spec((rows, order)),
                whole_spec((8, order)),
            ]
            + [ANY] * 5,
            out_specs=[whole_spec((rows, order)), ANY],
            scratch_shapes=[
                pltpu.VMEM((order, order), BF16),
                pltpu.VMEM((order, order), BF16),
                pltpu.VMEM((rows, order), BF16),
                pltpu.SemaphoreType.DMA((4,)),
            ],
        ),
        compiler_params=pltpu.CompilerParams(vmem_limit_bytes=28 * 1024 * 1024),
        cost_estimate=products_cost(rows, order, 4),
    )(flags, pivot_rows, right, columns, pivot_scale, next_rows, mine, partial, link, pivot)


def on_device(sep_block, own_couple, prev_couple, inner_diag):
    separator = sep_block[0]
    own_rows = own_couple[0]
    prev_rows = prev_couple[0]
    reciprocal = 1.0 / inner_diag[0]
    rows, order = own_rows.shape
    place = lax.axis_index("space")
    size = lax.axis_size("space")
    row_start = place * rows
    partition = lax.axis_index("tm")
    parts = lax.axis_size("tm")

    def between(block, route):
        return lax.ppermute(block, "tm", [(a, b) for a, b in route if 0 <= b < parts])

    even = range(0, parts, 2)
    pivots = range(1, parts, 4)
    everyone = range(parts)

    def one_step(ahead, back, step):
        up = [(j, j + 1) for j in range(step - 1, size - 1)]
        down = [(j, j - 1) for j in range(1, size - step + 1)]
        return lax.ppermute(ahead, "space", up), lax.ppermute(back, "space", down)

    def block_at(arrived, spot):
        block = arrived[0][0]
        for step in range(1, len(arrived)):
            if spot + step < size:
                block = jnp.where(place == spot + step, arrived[step][0], block)
            if spot - step >= 0:
                block = jnp.where(place == spot - step, arrived[step][1], block)
        return block

    is_first = partition == 0
    is_pivot = partition % 2 == 0
    is_receiver = partition % 2 == 1
    is_last = partition % 4 == 3
    flags = jnp.stack(
        [is_first.astype(jnp.int32), place, is_pivot.astype(jnp.int32), is_last.astype(jnp.int32)]
    )
    diagonal_block = lax.dynamic_slice_in_dim(separator, row_start, rows, 1)
    own_long = opening(flags, own_rows, prev_rows, diagonal_block, rows_of(reciprocal))
    own_arrived = [(own_long, own_long)]
    prev_arrived = [(prev_rows, prev_rows)]
    for step in range(1, size):
        own_arrived.append(one_step(*own_arrived[-1], step))
        prev_arrived.append(one_step(*prev_arrived[-1], step))
    words_arrived = [tuple(block[rows:] for block in pair) for pair in own_arrived]

    left_side = place < size // 2
    late_start = jnp.where(left_side, size - 1, 0) * rows
    is_end = jnp.logical_or(place == 0, place == size - 1)
    prev_blocks = [block_at(prev_arrived[:-1], spot) for spot in range(size)]
    zero = jnp.zeros_like(prev_rows)
    prev_blocks[0] = jnp.where(place == size - 1, zero, prev_blocks[0])
    prev_blocks[-1] = jnp.where(place == 0, zero, prev_blocks[-1])
    prev_first = jnp.concatenate(prev_blocks)
    prev_far = jnp.where(left_side, prev_blocks[-1], prev_blocks[0])
    prev_first, prev_far = lax.optimization_barrier((prev_first, prev_far))
    words = [block_at(words_arrived, spot) for spot in range(size)]

    def pair_sum(block, at):
        return block[at].astype(F32) + block[at + 1].astype(F32)

    part_diag = jnp.concatenate([pair_sum(block, 0)[:rows] for block in words])
    prev_diag = jnp.concatenate([pair_sum(block, 2)[:rows] for block in words])
    part_diag, prev_diag = lax.optimization_barrier((part_diag, prev_diag))
    diag = part_diag - between(prev_diag, [(p, p - 1) for p in everyone])
    pivot_diag = between(part_diag, [(p, p + 1) for p in even]) - prev_diag
    scale = (1.0 / jnp.maximum(diag, 1.0)).astype(BF16)
    pivot_scale = (1.0 / jnp.maximum(pivot_diag, 1.0)).astype(BF16)

    own_scaled = scaled_by(own_rows, reciprocal)
    sources = [own_long]
    for up, down in own_arrived[1:]:
        sources += [up, down]
    sources += [scale, pivot_scale]
    prev_first = scaled_by(prev_first, reciprocal)
    link, partial, prev_form, own_full, mine = early_forms(
        flags, prev_first, prev_rows, own_scaled, separator, sources
    )
    scale8, pivot_scale8 = rows_of(scale), rows_of(pivot_scale)

    from_below, from_above = prev_arrived[-1]
    late, corner, prev_late = late_forms(
        flags, rows_of(reciprocal), prev_rows, own_full, from_below, from_above, prev_far
    )
    link = lax.dynamic_update_slice_in_dim(link, late, late_start, 0)
    pivot_link = between(link, [(p, p + 1) for p in even])
    prev_form = lax.dynamic_update_slice_in_dim(prev_form, corner, late_start, 1)
    update, left_diag, right_diag = level_forms(flags, link, mine, scale8, pivot_scale8, prev_form)
    left_diag, right_diag = left_diag[0], right_diag[0]

    left_diag = between(left_diag, [(p, p - 1) for p in even])
    from_even = between(
        update, [(p, p - 1) for p in range(2, parts, 4)] + [(p, p - 4) for p in range(4, parts, 4)]
    )
    next_diag = diag - left_diag - right_diag
    next_scale = (1.0 / jnp.maximum(next_diag, 1.0)).astype(BF16)
    pivot_rows = lax.dynamic_slice_in_dim(pivot_link, row_start, rows, 0)
    pivot_rows = lax.optimization_barrier(scaled_by(pivot_rows, pivot_scale))
    next_rows = (-dot_nn(pivot_rows, link)).astype(BF16)
    next_long = jnp.concatenate([next_rows, jnp.broadcast_to(next_scale[None, :], (EXTRA, order))])
    pivot_long = between(next_long, [(p, p + 2) for p in pivots])

    left_next = scaled_by(dot_nt(scaled_by(next_rows, next_scale), link), pivot_scale)
    left_next = lax.optimization_barrier(left_next)
    left_next = (-dot_nt(left_next, pivot_link)).astype(BF16)
    from_pivot = between(left_next, [(p, p - 2) for p in pivots])
    right, columns, own_update, passed = columns_forms(
        flags, own_rows, pivot_scale8, prev_first, prev_late, pivot_link, update, from_even, left_next
    )
    from_far = between(passed, [(p - 4, p - 1) for p in range(4, parts, 4)])
    from_odd = between(own_update, [(p, p - 1) for p in range(1, parts, 2)])
    form, out_link = last_forms(
        flags, pivot_long, right, columns, next_rows, mine, partial, pivot_scale8, link, pivot_link
    )
    from_even = jnp.where(is_receiver, from_even + from_far, jnp.zeros_like(from_even))
    schur = form - (from_even + from_odd).astype(F32) - from_pivot.astype(F32)
    return (schur[None], out_link[None])


def solution(mesh):
    placed = (P("tm", "space", None), P("tm", "space", None), P("tm", "space", None), P("tm", None))
    return jax.shard_map(
        on_device,
        mesh=mesh,
        in_specs=placed,
        out_specs=(P("tm", "space", None), P("tm", "space", None)),
        check_vma=False,
    )
```

```python
import functools

import jax
import jax.numpy as jnp
from jax import lax
from jax.experimental import pallas as pl
from jax.experimental.pallas import tpu as pltpu
from jax.sharding import PartitionSpec as P

BF16 = jnp.bfloat16
F32 = jnp.float32
EXTRA = 16
WIDTH = 256

ANY = pl.BlockSpec(memory_space=pl.ANY)
HBM = pl.BlockSpec(memory_space=pltpu.HBM)
SHAPE = jax.ShapeDtypeStruct
FREE = pl.CostEstimate(flops=0, bytes_accessed=0, transcendentals=0)


def after(block, *others):
    def body(*refs):
        del refs

    return pl.pallas_call(
        body,
        out_shape=SHAPE(block.shape, block.dtype),
        in_specs=[ANY] * (1 + len(others)),
        out_specs=ANY,
        input_output_aliases={0: 0},
    )(block, *others)


def scaled_by(matrix, factors):
    return (matrix.astype(F32) * factors.astype(F32)[None, :]).astype(BF16)


def row_scaled_by(matrix, factors):
    return (matrix.astype(F32) * factors.astype(F32)[:, None]).astype(BF16)


def dot_nt(left, right):
    return lax.dot_general(left, right, (((1,), (1,)), ((), ())), preferred_element_type=F32)


def dot_nn(left, right):
    return lax.dot_general(left, right, (((1,), (0,)), ((), ())), preferred_element_type=F32)


def dot_tn(left, right):
    return lax.dot_general(left, right, (((0,), (0,)), ((), ())), preferred_element_type=F32)


def rows_of(scale):
    return jnp.broadcast_to(scale[None, :], (8, scale.shape[0]))


def products_cost(rows, order, count):
    return pl.CostEstimate(
        flops=2 * count * rows * order * order, bytes_accessed=2 * count * order * order, transcendentals=0
    )


def whole_spec(shape):
    return pl.BlockSpec(shape, lambda j, f: (0,) * len(shape), pipeline_mode=pl.Buffered(1))


def along_spec(count):
    return pl.BlockSpec((count, WIDTH), lambda j, f: (0, j))


def down_spec(count):
    return pl.BlockSpec((WIDTH, count), lambda j, f: (j, 0))


def opening_kernel(flags, own, prev, separator, reciprocal, long):
    rows, order = own.shape
    row_ids = lax.broadcasted_iota(jnp.int32, (rows, rows), 0)
    col_ids = lax.broadcasted_iota(jnp.int32, (rows, rows), 1)
    on_diagonal = jnp.where(row_ids == col_ids, separator[...], 0.0)
    ones = jnp.ones((8, order), BF16)

    def split(value):
        high = value.astype(BF16)
        return high, (value - high.astype(F32)).astype(BF16)

    def form_diagonal(block):
        wide = block.astype(F32)
        high, low = split((wide * reciprocal[0:1]).astype(BF16).astype(F32) * wide)
        return (dot_nt(ones, high) + dot_nt(ones, low))[0:1]

    def placed(words, count):
        ids = lax.broadcasted_iota(jnp.int32, (EXTRA, count), 0)
        total = jnp.zeros((EXTRA, count), F32)
        for at, word in words.items():
            total = jnp.where(ids == at, word.astype(F32), total)
        return total.astype(BF16)

    long[0:rows, :] = own[...]
    long[rows:, :] = jnp.zeros((EXTRA, order), BF16)
    own_high, own_low = split(jnp.sum(on_diagonal, axis=0, keepdims=True) - form_diagonal(own[...]))
    prev_high, prev_low = split(form_diagonal(prev[...]))
    long[rows:, 0:rows] = placed({0: own_high, 1: own_low, 2: prev_high, 3: prev_low}, rows)


def opening(flags, own, prev, separator, reciprocal):
    rows, order = own.shape
    return pl.pallas_call(
        opening_kernel,
        out_shape=SHAPE((rows + EXTRA, order), BF16),
        grid_spec=pltpu.PrefetchScalarGridSpec(
            num_scalar_prefetch=1,
            grid=(1,),
            in_specs=[whole_spec((rows, order))] * 2 + [whole_spec((rows, rows)), whole_spec((8, order))],
            out_specs=whole_spec((rows + EXTRA, order)),
        ),
        compiler_params=pltpu.CompilerParams(vmem_limit_bytes=32 * 1024 * 1024),
        cost_estimate=FREE,
    )(flags, own, prev, separator, reciprocal)


def early_kernel(size, flags, prev_whole, prev_rows, own_rows, separator, *refs):
    sources = refs[: 2 * size - 1]
    link, partial, form, own_out, mine, own, sems = refs[2 * size + 1 :]
    rows = separator.shape[0]
    step = pl.program_id(0)
    here = pl.ds(pl.multiple_of(step * WIDTH, WIDTH), WIDTH)

    def copies():
        for spot in range(size):
            for by, source in enumerate(sources):
                distance = (by + 1) // 2 if by % 2 else -(by // 2)
                target = own.at[pl.ds(spot * rows, rows)]
                copy = pltpu.make_async_copy(source.at[pl.ds(0, rows)], target, sems.at[spot])
                yield flags[1] - spot == distance, copy

    @pl.when(step == 0)
    def _():
        for chosen, copy in copies():
            pl.when(chosen)(copy.start)
        for chosen, copy in copies():
            pl.when(chosen)(copy.wait)

    block = own[here, :]
    own_out[...] = block
    link[...] = jnp.where(flags[0] == 1, 0.0, -dot_nt(prev_whole[...], block)).astype(BF16)
    mine[...] = link[pl.ds(pl.multiple_of(flags[1] * rows, rows), rows), :]
    partial[...] = separator[...] - dot_nt(own_rows[...], block)
    form[...] = dot_nt(prev_rows[...], prev_whole[here, :])


def early_forms(flags, prev_whole, prev_rows, own_rows, separator, sources):
    rows, order = own_rows.shape
    size = order // rows
    return pl.pallas_call(
        functools.partial(early_kernel, size),
        out_shape=[
            SHAPE((order, order), BF16),
            SHAPE((rows, order), F32),
            SHAPE((rows, order), F32),
            SHAPE((order, order), BF16),
            SHAPE((rows, order), BF16),
        ],
        grid_spec=pltpu.PrefetchScalarGridSpec(
            num_scalar_prefetch=1,
            grid=(order // WIDTH,),
            in_specs=[
                whole_spec((order, order)),
                whole_spec((rows, order)),
                whole_spec((rows, order)),
                along_spec(rows),
            ]
            + [ANY] * len(sources),
            out_specs=[along_spec(order), along_spec(rows), along_spec(rows), down_spec(order), along_spec(rows)],
            scratch_shapes=[pltpu.VMEM((order, order), BF16), pltpu.SemaphoreType.DMA((size,))],
        ),
        compiler_params=pltpu.CompilerParams(vmem_limit_bytes=26 * 1024 * 1024),
        cost_estimate=FREE,
    )(flags, prev_whole, prev_rows, own_rows, separator, *sources)


def late_kernel(
    size, flags, reciprocal, prev_rows, own, from_below, from_above, far, link, corner, scaled, raw, sem
):
    place = flags[1]
    step = pl.program_id(0)
    width = own.shape[0]
    here = pl.ds(pl.multiple_of(step * width, width), width)

    @pl.when(step == 0)
    def _():
        for chosen, source in (
            (place == 0, from_above),
            (place == size - 1, from_below),
            (jnp.logical_and(place != 0, place != size - 1), far),
        ):
            copy = pltpu.make_async_copy(source, raw, sem)
            pl.when(chosen)(copy.start)
            pl.when(chosen)(copy.wait)
        scaled[...] = (raw[...].astype(F32) * reciprocal[0:1]).astype(BF16)
        corner[...] = dot_nt(prev_rows[...], scaled[...])

    link[:, here] = jnp.where(flags[0] == 1, 0.0, -dot_nt(scaled[...], own[...])).astype(BF16)


def late_forms(flags, reciprocal, prev_rows, own, from_below, from_above, far):
    rows, order = prev_rows.shape
    size = order // rows
    width = 512
    return pl.pallas_call(
        functools.partial(late_kernel, size),
        out_shape=[SHAPE((rows, order), BF16), SHAPE((rows, rows), F32), SHAPE((rows, order), BF16)],
        grid_spec=pltpu.PrefetchScalarGridSpec(
            num_scalar_prefetch=1,
            grid=(order // width,),
            in_specs=[
                whole_spec((8, order)),
                whole_spec((rows, order)),
                pl.BlockSpec((width, order), lambda j, f: (j, 0)),
                ANY,
                ANY,
                ANY,
            ],
            out_specs=[whole_spec((rows, order)), whole_spec((rows, rows)), whole_spec((rows, order))],
            scratch_shapes=[pltpu.VMEM((rows, order), BF16), pltpu.SemaphoreType.DMA],
        ),
        compiler_params=pltpu.CompilerParams(vmem_limit_bytes=18 * 1024 * 1024),
    )(flags, reciprocal, prev_rows, own, from_below, from_above, far)


def level_kernel(flags, link, mine, scale, pivot_scale, form, update, left_diag, right_diag):
    part = link[...]
    scaled = mine[...] * scale[0:1]
    keep = jnp.where(flags[2] == 1, 1.0, 0.0)
    update[...] = (form[...] + keep * dot_nt(scaled, part)).astype(BF16)
    square = part * part
    left_diag[...] = dot_nt(scale[...], square)

    @pl.when(pl.program_id(0) == 0)
    def _():
        right_diag[...] = jnp.zeros_like(right_diag)

    right_diag[...] += dot_nn(pivot_scale[...], square)


def level_forms(flags, link, mine, scale, pivot_scale, form):
    rows, order = form.shape
    width = 512
    along = lambda count: pl.BlockSpec((count, width), lambda j, f: (0, j))
    return pl.pallas_call(
        level_kernel,
        out_shape=[SHAPE((rows, order), BF16), SHAPE((8, order), F32), SHAPE((8, order), F32)],
        grid_spec=pltpu.PrefetchScalarGridSpec(
            num_scalar_prefetch=1,
            grid=(order // width,),
            in_specs=[
                pl.BlockSpec((width, order), lambda j, f: (j, 0)),
                whole_spec((rows, order)),
                whole_spec((8, order)),
                along(8),
                along(rows),
            ],
            out_specs=[along(rows), along(8), whole_spec((8, order))],
        ),
        compiler_params=pltpu.CompilerParams(vmem_limit_bytes=18 * 1024 * 1024),
        cost_estimate=FREE,
    )(flags, link, mine, scale, pivot_scale, form)


def fetched(early, late, whole, sems, at):
    rows, order = late.shape
    size = order // rows
    place = at[0]
    low = place < size // 2
    spans = [pl.ds(spot * rows, rows) for spot in range(size)]
    copies = []
    for spot, span in enumerate(spans):
        plain = pltpu.make_async_copy(early.at[span], whole.at[span], sems.at[spot])
        if spot not in (0, size - 1):
            copies.append((True, plain))
            continue
        is_late = low if spot else jnp.logical_not(low)
        copies.append((jnp.logical_not(is_late), plain))
        copies.append((is_late, pltpu.make_async_copy(late, whole.at[span], sems.at[spot])))
    for chosen, copy in copies:
        pl.when(chosen)(copy.start) if chosen is not True else copy.start()

    def wait():
        for chosen, copy in copies:
            pl.when(chosen)(copy.wait) if chosen is not True else copy.wait()

    return wait


def times(block, factors):
    return (block.astype(F32) * factors[0:1].astype(F32)).astype(BF16)


def columns_kernel(
    flags, own, pivot_scale, prev_early, prev_late, pivot_whole, update, ready,
    right, columns, moved, prev, pivot, results, sems, more_sems,
):
    del ready
    move = pltpu.make_async_copy(update, moved, more_sems.at[0])
    move.start()
    wait_prev = fetched(prev_early, prev_late, prev, sems, [flags[1]])
    copy = pltpu.make_async_copy(pivot_whole, pivot, more_sems.at[1])
    copy.start()
    wait_prev()
    across = jnp.where(flags[0] == 1, 0.0, -dot_nt(own[...], prev[...])).astype(BF16)
    across = times(across, pivot_scale)
    results[0] = across
    store = pltpu.make_async_copy(results.at[0], right, more_sems.at[2])
    store.start()
    copy.wait()
    results[1] = (-dot_nt(across, pivot[...])).astype(BF16)
    last = pltpu.make_async_copy(results.at[1], columns, more_sems.at[3])
    last.start()
    for copy in (move, store, last):
        copy.wait()


def columns_forms(flags, own, pivot_scale, prev_early, prev_late, pivot, update, ready):
    rows, order = own.shape
    out = SHAPE((rows, order), BF16)
    return pl.pallas_call(
        columns_kernel,
        out_shape=[out, out, out],
        grid_spec=pltpu.PrefetchScalarGridSpec(
            num_scalar_prefetch=1,
            grid=(1,),
            in_specs=[whole_spec((rows, order)), whole_spec((8, order))] + [ANY] * 5,
            out_specs=[HBM, HBM, HBM],
            scratch_shapes=[
                pltpu.VMEM((order, order), BF16),
                pltpu.VMEM((order, order), BF16),
                pltpu.VMEM((2, rows, order), BF16),
                pltpu.SemaphoreType.DMA((order // rows,)),
                pltpu.SemaphoreType.DMA((4,)),
            ],
        ),
        compiler_params=pltpu.CompilerParams(vmem_limit_bytes=22 * 1024 * 1024),
        cost_estimate=products_cost(rows, order, 2),
    )(flags, own, pivot_scale, prev_early, prev_late, pivot, update, ready)


def last_kernel(
    flags, pivot_scale, pivot_rows, right_whole, columns_whole, next_rows, mine, partial, link_whole, pivot_whole,
    form, new, link, pivot, last, long, right, columns, sems,
):
    rows = right.shape[0]
    small = [
        pltpu.make_async_copy(pivot_rows, long, sems.at[4]),
        pltpu.make_async_copy(columns_whole, columns, sems.at[5]),
        pltpu.make_async_copy(right_whole, right, sems.at[6]),
    ]
    for copy in small:
        copy.start()
    even, final = flags[2] == 1, flags[3] == 1
    other = jnp.logical_not(jnp.logical_or(even, final))
    fetch = [
        pltpu.make_async_copy(pivot_whole, pivot, sems.at[0]),
        pltpu.make_async_copy(link_whole, link, sems.at[1]),
        pltpu.make_async_copy(partial, form, sems.at[2]),
    ]
    for copy in fetch:
        copy.start()
    plain = [(even, pltpu.make_async_copy(mine, new, sems.at[3]))]
    plain.append((other, pltpu.make_async_copy(next_rows, new, sems.at[3])))
    for chosen, copy in plain:
        pl.when(chosen)(copy.start)
    wide = pivot_scale[0:1].astype(F32)
    for copy in small:
        copy.wait()
    scale = long[rows : rows + EXTRA, :]
    fetch[0].wait()
    inner = dot_nn(times(columns[...], scale), pivot[...]) * wide
    keep = jnp.where(final, 1.0, 0.0)
    factor = (right[...].astype(F32) - inner * keep).astype(BF16)
    inner = (dot_nn(times(long[0:rows, :], scale), pivot[...]) * wide).astype(BF16)
    fetch[1].wait()
    last[...] = dot_nn(inner, link[...]).astype(BF16)
    store = pltpu.make_async_copy(last, new, sems.at[3])
    pl.when(final)(store.start)
    fetch[2].wait()
    odd = jnp.where(even, 0.0, 1.0)
    form[...] -= odd * dot_nn(factor, link[...])
    for chosen, copy in plain + [(final, store)]:
        pl.when(chosen)(copy.wait)


def last_forms(flags, pivot_rows, right, columns, next_rows, mine, partial, pivot_scale, link, pivot):
    rows, order = right.shape
    return pl.pallas_call(
        last_kernel,
        out_shape=[SHAPE((rows, order), F32), SHAPE((rows, order), BF16)],
        grid_spec=pltpu.PrefetchScalarGridSpec(
            num_scalar_prefetch=1,
            grid=(1,),
            in_specs=[whole_spec((8, order))] + [HBM] * 8,
            out_specs=[whole_spec((rows, order)), ANY],
            scratch_shapes=[
                pltpu.VMEM((order, order), BF16),
                pltpu.VMEM((order, order), BF16),
                pltpu.VMEM((rows, order), BF16),
                pltpu.VMEM(pivot_rows.shape, BF16),
                pltpu.VMEM((rows, order), BF16),
                pltpu.VMEM((rows, order), BF16),
                pltpu.SemaphoreType.DMA((7,)),
            ],
        ),
        compiler_params=pltpu.CompilerParams(vmem_limit_bytes=28 * 1024 * 1024),
        cost_estimate=products_cost(rows, order, 4),
    )(flags, pivot_scale, pivot_rows, right, columns, next_rows, mine, partial, link, pivot)


def on_device(sep_block, own_couple, prev_couple, inner_diag):
    separator = sep_block[0]
    own_rows = own_couple[0]
    prev_rows = prev_couple[0]
    reciprocal = 1.0 / inner_diag[0]
    rows, order = own_rows.shape
    place = lax.axis_index("space")
    size = lax.axis_size("space")
    row_start = place * rows
    partition = lax.axis_index("tm")
    parts = lax.axis_size("tm")

    def between(block, route):
        return lax.ppermute(block, "tm", [(a, b) for a, b in route if 0 <= b < parts])

    even = range(0, parts, 2)
    pivots = range(1, parts, 4)
    everyone = range(parts)

    def one_step(ahead, back, step):
        up = [(j, j + 1) for j in range(step - 1, size - 1)]
        down = [(j, j - 1) for j in range(1, size - step + 1)]
        return lax.ppermute(ahead, "space", up), lax.ppermute(back, "space", down)

    def block_at(arrived, spot):
        block = arrived[0][0]
        for step in range(1, len(arrived)):
            if spot + step < size:
                block = jnp.where(place == spot + step, arrived[step][0], block)
            if spot - step >= 0:
                block = jnp.where(place == spot - step, arrived[step][1], block)
        return block

    is_first = partition == 0
    is_pivot = partition % 2 == 0
    is_receiver = partition % 2 == 1
    is_last = partition % 4 == 3
    flags = jnp.stack(
        [is_first.astype(jnp.int32), place, is_pivot.astype(jnp.int32), is_last.astype(jnp.int32)]
    )
    diagonal_block = lax.dynamic_slice_in_dim(separator, row_start, rows, 1)
    own_long = opening(flags, own_rows, prev_rows, diagonal_block, rows_of(reciprocal))
    own_arrived = [(own_long, own_long)]
    prev_arrived = [(prev_rows, prev_rows)]
    for step in range(1, size):
        own_arrived.append(one_step(*own_arrived[-1], step))
        prev_arrived.append(one_step(*prev_arrived[-1], step))
    words_arrived = [tuple(block[rows:] for block in pair) for pair in own_arrived]

    left_side = place < size // 2
    late_start = jnp.where(left_side, size - 1, 0) * rows
    is_end = jnp.logical_or(place == 0, place == size - 1)
    prev_blocks = [block_at(prev_arrived[:-1], spot) for spot in range(size)]
    zero = jnp.zeros_like(prev_rows)
    prev_blocks[0] = jnp.where(place == size - 1, zero, prev_blocks[0])
    prev_blocks[-1] = jnp.where(place == 0, zero, prev_blocks[-1])
    prev_first = jnp.concatenate(prev_blocks)
    prev_far = jnp.where(left_side, prev_blocks[-1], prev_blocks[0])
    prev_first, prev_far = lax.optimization_barrier((prev_first, prev_far))
    words = [block_at(words_arrived, spot) for spot in range(size)]

    def pair_sum(block, at):
        return block[at].astype(F32) + block[at + 1].astype(F32)

    part_diag = jnp.concatenate([pair_sum(block, 0)[:rows] for block in words])
    prev_diag = jnp.concatenate([pair_sum(block, 2)[:rows] for block in words])
    part_diag, prev_diag = lax.optimization_barrier((part_diag, prev_diag))
    diag = part_diag - between(prev_diag, [(p, p - 1) for p in everyone])
    pivot_diag = between(part_diag, [(p, p + 1) for p in even]) - prev_diag
    scale = (1.0 / jnp.maximum(diag, 1.0)).astype(BF16)
    pivot_scale = (1.0 / jnp.maximum(pivot_diag, 1.0)).astype(BF16)

    own_scaled = scaled_by(own_rows, reciprocal)
    sources = [own_long]
    for up, down in own_arrived[1:]:
        sources += [up, down]
    sources += [scale, pivot_scale]
    prev_first = scaled_by(prev_first, reciprocal)
    link, partial, prev_form, own_full, mine = early_forms(
        flags, prev_first, prev_rows, own_scaled, separator, sources
    )
    scale8, pivot_scale8 = rows_of(scale), rows_of(pivot_scale)

    from_below, from_above = prev_arrived[-1]
    late, corner, prev_late = late_forms(
        flags, rows_of(reciprocal), prev_rows, own_full, from_below, from_above, prev_far
    )
    link = lax.dynamic_update_slice_in_dim(link, late, late_start, 0)
    pivot_link = between(link, [(p, p + 1) for p in even])
    prev_form = lax.dynamic_update_slice_in_dim(prev_form, corner, late_start, 1)
    update, left_diag, right_diag = level_forms(flags, link, mine, scale8, pivot_scale8, prev_form)
    left_diag, right_diag = left_diag[0], right_diag[0]

    left_diag = between(left_diag, [(p, p - 1) for p in even])
    from_even = between(update, [(p, p - 1) for p in even])
    next_diag = diag - left_diag - right_diag
    next_scale = (1.0 / jnp.maximum(next_diag, 1.0)).astype(BF16)
    pivot_rows = lax.dynamic_slice_in_dim(pivot_link, row_start, rows, 0)
    pivot_rows = lax.optimization_barrier(scaled_by(pivot_rows, pivot_scale))
    next_rows = (-dot_nn(pivot_rows, link)).astype(BF16)
    next_long = jnp.concatenate([next_rows, jnp.broadcast_to(next_scale[None, :], (EXTRA, order))])
    pivot_long = between(next_long, [(p, p + 2) for p in pivots])

    left_next = scaled_by(dot_nt(scaled_by(next_rows, next_scale), link), pivot_scale)
    left_next = lax.optimization_barrier(left_next)
    left_next = (-dot_nt(left_next, pivot_link)).astype(BF16)
    from_pivot = between(left_next, [(p, p - 2) for p in pivots])
    right, columns, own_update = columns_forms(
        flags, own_rows, pivot_scale8, prev_first, prev_late, pivot_link, update, left_next
    )
    from_odd = between(own_update, [(p, p - 1) for p in range(1, parts, 2)])
    form, out_link = last_forms(
        flags, pivot_long, right, columns, next_rows, mine, partial, pivot_scale8, link, pivot_link
    )
    schur = form - (from_even + from_odd).astype(F32) - from_pivot.astype(F32)
    return (schur[None], out_link[None])


def solution(mesh):
    placed = (P("tm", "space", None), P("tm", "space", None), P("tm", "space", None), P("tm", None))
    return jax.shard_map(
        on_device,
        mesh=mesh,
        in_specs=placed,
        out_specs=(P("tm", "space", None), P("tm", "space", None)),
        check_vma=False,
    )
```

```python
import functools

import jax
import jax.numpy as jnp
from jax import lax
from jax.experimental import pallas as pl
from jax.experimental.pallas import tpu as pltpu
from jax.sharding import PartitionSpec as P

BF16 = jnp.bfloat16
F32 = jnp.float32
EXTRA = 16
WIDTH = 256

ANY = pl.BlockSpec(memory_space=pl.ANY)
HBM = pl.BlockSpec(memory_space=pltpu.HBM)
SHAPE = jax.ShapeDtypeStruct
FREE = pl.CostEstimate(flops=0, bytes_accessed=0, transcendentals=0)


def after(block, *others):
    def body(*refs):
        del refs

    return pl.pallas_call(
        body,
        out_shape=SHAPE(block.shape, block.dtype),
        in_specs=[ANY] * (1 + len(others)),
        out_specs=ANY,
        input_output_aliases={0: 0},
    )(block, *others)


def scaled_by(matrix, factors):
    return (matrix.astype(F32) * factors.astype(F32)[None, :]).astype(BF16)


def row_scaled_by(matrix, factors):
    return (matrix.astype(F32) * factors.astype(F32)[:, None]).astype(BF16)


def dot_nt(left, right):
    return lax.dot_general(left, right, (((1,), (1,)), ((), ())), preferred_element_type=F32)


def dot_nn(left, right):
    return lax.dot_general(left, right, (((1,), (0,)), ((), ())), preferred_element_type=F32)


def dot_tn(left, right):
    return lax.dot_general(left, right, (((0,), (0,)), ((), ())), preferred_element_type=F32)


def rows_of(scale):
    return jnp.broadcast_to(scale[None, :], (8, scale.shape[0]))


def whole_spec(shape):
    return pl.BlockSpec(shape, lambda j, f: (0,) * len(shape), pipeline_mode=pl.Buffered(1))


def along_spec(count):
    return pl.BlockSpec((count, WIDTH), lambda j, f: (0, j))


def down_spec(count):
    return pl.BlockSpec((WIDTH, count), lambda j, f: (j, 0))


def opening_kernel(flags, own, prev, separator, reciprocal, long):
    rows, order = own.shape
    row_ids = lax.broadcasted_iota(jnp.int32, (rows, rows), 0)
    col_ids = lax.broadcasted_iota(jnp.int32, (rows, rows), 1)
    on_diagonal = jnp.where(row_ids == col_ids, separator[...], 0.0)
    ones = jnp.ones((8, order), BF16)

    def split(value):
        high = value.astype(BF16)
        return high, (value - high.astype(F32)).astype(BF16)

    def form_diagonal(block):
        wide = block.astype(F32)
        high, low = split((wide * reciprocal[0:1]).astype(BF16).astype(F32) * wide)
        return (dot_nt(ones, high) + dot_nt(ones, low))[0:1]

    def placed(words, count):
        ids = lax.broadcasted_iota(jnp.int32, (EXTRA, count), 0)
        total = jnp.zeros((EXTRA, count), F32)
        for at, word in words.items():
            total = jnp.where(ids == at, word.astype(F32), total)
        return total.astype(BF16)

    long[0:rows, :] = own[...]
    long[rows:, :] = jnp.zeros((EXTRA, order), BF16)
    own_high, own_low = split(jnp.sum(on_diagonal, axis=0, keepdims=True) - form_diagonal(own[...]))
    prev_high, prev_low = split(form_diagonal(prev[...]))
    long[rows:, 0:rows] = placed({0: own_high, 1: own_low, 2: prev_high, 3: prev_low}, rows)


def opening(flags, own, prev, separator, reciprocal):
    rows, order = own.shape
    return pl.pallas_call(
        opening_kernel,
        out_shape=SHAPE((rows + EXTRA, order), BF16),
        grid_spec=pltpu.PrefetchScalarGridSpec(
            num_scalar_prefetch=1,
            grid=(1,),
            in_specs=[whole_spec((rows, order))] * 2 + [whole_spec((rows, rows)), whole_spec((8, order))],
            out_specs=whole_spec((rows + EXTRA, order)),
        ),
        compiler_params=pltpu.CompilerParams(vmem_limit_bytes=32 * 1024 * 1024),
        cost_estimate=FREE,
    )(flags, own, prev, separator, reciprocal)


def early_kernel(size, flags, prev_whole, prev_rows, own_rows, separator, *refs):
    sources = refs[: 2 * size - 1]
    link, partial, form, own_out, mine, own, sems = refs[2 * size + 1 :]
    rows = separator.shape[0]
    step = pl.program_id(0)
    here = pl.ds(pl.multiple_of(step * WIDTH, WIDTH), WIDTH)

    def copies():
        for spot in range(size):
            for by, source in enumerate(sources):
                distance = (by + 1) // 2 if by % 2 else -(by // 2)
                target = own.at[pl.ds(spot * rows, rows)]
                copy = pltpu.make_async_copy(source.at[pl.ds(0, rows)], target, sems.at[spot])
                yield flags[1] - spot == distance, copy

    @pl.when(step == 0)
    def _():
        for chosen, copy in copies():
            pl.when(chosen)(copy.start)
        for chosen, copy in copies():
            pl.when(chosen)(copy.wait)

    block = own[here, :]
    own_out[...] = block
    link[...] = jnp.where(flags[0] == 1, 0.0, -dot_nt(prev_whole[...], block)).astype(BF16)
    mine[...] = link[pl.ds(pl.multiple_of(flags[1] * rows, rows), rows), :]
    partial[...] = separator[...] - dot_nt(own_rows[...], block)
    form[...] = dot_nt(prev_rows[...], prev_whole[here, :])


def early_forms(flags, prev_whole, prev_rows, own_rows, separator, sources):
    rows, order = own_rows.shape
    size = order // rows
    return pl.pallas_call(
        functools.partial(early_kernel, size),
        out_shape=[
            SHAPE((order, order), BF16),
            SHAPE((rows, order), F32),
            SHAPE((rows, order), F32),
            SHAPE((order, order), BF16),
            SHAPE((rows, order), BF16),
        ],
        grid_spec=pltpu.PrefetchScalarGridSpec(
            num_scalar_prefetch=1,
            grid=(order // WIDTH,),
            in_specs=[
                whole_spec((order, order)),
                whole_spec((rows, order)),
                whole_spec((rows, order)),
                along_spec(rows),
            ]
            + [ANY] * len(sources),
            out_specs=[along_spec(order), along_spec(rows), along_spec(rows), down_spec(order), along_spec(rows)],
            scratch_shapes=[pltpu.VMEM((order, order), BF16), pltpu.SemaphoreType.DMA((size,))],
        ),
        compiler_params=pltpu.CompilerParams(vmem_limit_bytes=26 * 1024 * 1024),
        cost_estimate=FREE,
    )(flags, prev_whole, prev_rows, own_rows, separator, *sources)


def late_kernel(
    size, flags, reciprocal, prev_rows, own, from_below, from_above, far, link, corner, scaled, raw, sem
):
    place = flags[1]
    step = pl.program_id(0)
    width = own.shape[0]
    here = pl.ds(pl.multiple_of(step * width, width), width)

    @pl.when(step == 0)
    def _():
        for chosen, source in (
            (place == 0, from_above),
            (place == size - 1, from_below),
            (jnp.logical_and(place != 0, place != size - 1), far),
        ):
            copy = pltpu.make_async_copy(source, raw, sem)
            pl.when(chosen)(copy.start)
            pl.when(chosen)(copy.wait)
        scaled[...] = (raw[...].astype(F32) * reciprocal[0:1]).astype(BF16)
        corner[...] = dot_nt(prev_rows[...], scaled[...])

    link[:, here] = jnp.where(flags[0] == 1, 0.0, -dot_nt(scaled[...], own[...])).astype(BF16)


def late_forms(flags, reciprocal, prev_rows, own, from_below, from_above, far):
    rows, order = prev_rows.shape
    size = order // rows
    width = 512
    return pl.pallas_call(
        functools.partial(late_kernel, size),
        out_shape=[SHAPE((rows, order), BF16), SHAPE((rows, rows), F32), SHAPE((rows, order), BF16)],
        grid_spec=pltpu.PrefetchScalarGridSpec(
            num_scalar_prefetch=1,
            grid=(order // width,),
            in_specs=[
                whole_spec((8, order)),
                whole_spec((rows, order)),
                pl.BlockSpec((width, order), lambda j, f: (j, 0)),
                ANY,
                ANY,
                ANY,
            ],
            out_specs=[whole_spec((rows, order)), whole_spec((rows, rows)), whole_spec((rows, order))],
            scratch_shapes=[pltpu.VMEM((rows, order), BF16), pltpu.SemaphoreType.DMA],
        ),
        compiler_params=pltpu.CompilerParams(vmem_limit_bytes=18 * 1024 * 1024),
    )(flags, reciprocal, prev_rows, own, from_below, from_above, far)


def level_kernel(flags, link, mine, scale, pivot_scale, form, update, left_diag, right_diag):
    part = link[...]
    scaled = mine[...] * scale[0:1]
    keep = jnp.where(flags[2] == 1, 1.0, 0.0)
    update[...] = (form[...] + keep * dot_nt(scaled, part)).astype(BF16)
    square = part * part
    left_diag[...] = dot_nt(scale[...], square)

    @pl.when(pl.program_id(0) == 0)
    def _():
        right_diag[...] = jnp.zeros_like(right_diag)

    right_diag[...] += dot_nn(pivot_scale[...], square)


def level_forms(flags, link, mine, scale, pivot_scale, form):
    rows, order = form.shape
    width = 512
    along = lambda count: pl.BlockSpec((count, width), lambda j, f: (0, j))
    return pl.pallas_call(
        level_kernel,
        out_shape=[SHAPE((rows, order), BF16), SHAPE((8, order), F32), SHAPE((8, order), F32)],
        grid_spec=pltpu.PrefetchScalarGridSpec(
            num_scalar_prefetch=1,
            grid=(order // width,),
            in_specs=[
                pl.BlockSpec((width, order), lambda j, f: (j, 0)),
                whole_spec((rows, order)),
                whole_spec((8, order)),
                along(8),
                along(rows),
            ],
            out_specs=[along(rows), along(8), whole_spec((8, order))],
        ),
        compiler_params=pltpu.CompilerParams(vmem_limit_bytes=18 * 1024 * 1024),
        cost_estimate=FREE,
    )(flags, link, mine, scale, pivot_scale, form)


def fetched(early, late, whole, sems, at):
    rows, order = late.shape
    size = order // rows
    place = at[0]
    low = place < size // 2
    spans = [pl.ds(spot * rows, rows) for spot in range(size)]
    copies = []
    for spot, span in enumerate(spans):
        plain = pltpu.make_async_copy(early.at[span], whole.at[span], sems.at[spot])
        if spot not in (0, size - 1):
            copies.append((True, plain))
            continue
        is_late = low if spot else jnp.logical_not(low)
        copies.append((jnp.logical_not(is_late), plain))
        copies.append((is_late, pltpu.make_async_copy(late, whole.at[span], sems.at[spot])))
    for chosen, copy in copies:
        pl.when(chosen)(copy.start) if chosen is not True else copy.start()

    def wait():
        for chosen, copy in copies:
            pl.when(chosen)(copy.wait) if chosen is not True else copy.wait()

    return wait


def times(block, factors):
    return (block.astype(F32) * factors[0:1].astype(F32)).astype(BF16)


def columns_kernel(
    flags, own, pivot_scale, prev_early, prev_late, pivot_whole, update, ready,
    right, columns, moved, prev, pivot, results, sems, more_sems,
):
    del ready
    move = pltpu.make_async_copy(update, moved, more_sems.at[0])
    move.start()
    wait_prev = fetched(prev_early, prev_late, prev, sems, [flags[1]])
    copy = pltpu.make_async_copy(pivot_whole, pivot, more_sems.at[1])
    copy.start()
    wait_prev()
    across = jnp.where(flags[0] == 1, 0.0, -dot_nt(own[...], prev[...])).astype(BF16)
    across = times(across, pivot_scale)
    results[0] = across
    store = pltpu.make_async_copy(results.at[0], right, more_sems.at[2])
    store.start()
    copy.wait()
    results[1] = (-dot_nt(across, pivot[...])).astype(BF16)
    last = pltpu.make_async_copy(results.at[1], columns, more_sems.at[3])
    last.start()
    for copy in (move, store, last):
        copy.wait()


def columns_forms(flags, own, pivot_scale, prev_early, prev_late, pivot, update, ready):
    rows, order = own.shape
    out = SHAPE((rows, order), BF16)
    return pl.pallas_call(
        columns_kernel,
        out_shape=[out, out, out],
        grid_spec=pltpu.PrefetchScalarGridSpec(
            num_scalar_prefetch=1,
            grid=(1,),
            in_specs=[whole_spec((rows, order)), whole_spec((8, order))] + [ANY] * 5,
            out_specs=[HBM, HBM, HBM],
            scratch_shapes=[
                pltpu.VMEM((order, order), BF16),
                pltpu.VMEM((order, order), BF16),
                pltpu.VMEM((2, rows, order), BF16),
                pltpu.SemaphoreType.DMA((order // rows,)),
                pltpu.SemaphoreType.DMA((4,)),
            ],
        ),
        compiler_params=pltpu.CompilerParams(vmem_limit_bytes=22 * 1024 * 1024),
        cost_estimate=FREE,
    )(flags, own, pivot_scale, prev_early, prev_late, pivot, update, ready)


def last_kernel(
    flags, pivot_scale, pivot_rows, right_whole, columns_whole, next_rows, mine, partial, link_whole, pivot_whole,
    form, new, link, pivot, last, long, right, columns, sems,
):
    rows = right.shape[0]
    small = [
        pltpu.make_async_copy(pivot_rows, long, sems.at[4]),
        pltpu.make_async_copy(columns_whole, columns, sems.at[5]),
        pltpu.make_async_copy(right_whole, right, sems.at[6]),
    ]
    for copy in small:
        copy.start()
    even, final = flags[2] == 1, flags[3] == 1
    other = jnp.logical_not(jnp.logical_or(even, final))
    fetch = [
        pltpu.make_async_copy(pivot_whole, pivot, sems.at[0]),
        pltpu.make_async_copy(link_whole, link, sems.at[1]),
        pltpu.make_async_copy(partial, form, sems.at[2]),
    ]
    for copy in fetch:
        copy.start()
    plain = [(even, pltpu.make_async_copy(mine, new, sems.at[3]))]
    plain.append((other, pltpu.make_async_copy(next_rows, new, sems.at[3])))
    for chosen, copy in plain:
        pl.when(chosen)(copy.start)
    wide = pivot_scale[0:1].astype(F32)
    for copy in small:
        copy.wait()
    scale = long[rows : rows + EXTRA, :]
    fetch[0].wait()
    inner = dot_nn(times(columns[...], scale), pivot[...]) * wide
    keep = jnp.where(final, 1.0, 0.0)
    factor = (right[...].astype(F32) - inner * keep).astype(BF16)
    inner = (dot_nn(times(long[0:rows, :], scale), pivot[...]) * wide).astype(BF16)
    fetch[1].wait()
    last[...] = dot_nn(inner, link[...]).astype(BF16)
    store = pltpu.make_async_copy(last, new, sems.at[3])
    pl.when(final)(store.start)
    fetch[2].wait()
    odd = jnp.where(even, 0.0, 1.0)
    form[...] -= odd * dot_nn(factor, link[...])
    for chosen, copy in plain + [(final, store)]:
        pl.when(chosen)(copy.wait)


def last_forms(flags, pivot_rows, right, columns, next_rows, mine, partial, pivot_scale, link, pivot):
    rows, order = right.shape
    return pl.pallas_call(
        last_kernel,
        out_shape=[SHAPE((rows, order), F32), SHAPE((rows, order), BF16)],
        grid_spec=pltpu.PrefetchScalarGridSpec(
            num_scalar_prefetch=1,
            grid=(1,),
            in_specs=[whole_spec((8, order))] + [HBM] * 8,
            out_specs=[whole_spec((rows, order)), ANY],
            scratch_shapes=[
                pltpu.VMEM((order, order), BF16),
                pltpu.VMEM((order, order), BF16),
                pltpu.VMEM((rows, order), BF16),
                pltpu.VMEM(pivot_rows.shape, BF16),
                pltpu.VMEM((rows, order), BF16),
                pltpu.VMEM((rows, order), BF16),
                pltpu.SemaphoreType.DMA((7,)),
            ],
        ),
        compiler_params=pltpu.CompilerParams(vmem_limit_bytes=28 * 1024 * 1024),
        cost_estimate=FREE,
    )(flags, pivot_scale, pivot_rows, right, columns, next_rows, mine, partial, link, pivot)


def on_device(sep_block, own_couple, prev_couple, inner_diag):
    separator = sep_block[0]
    own_rows = own_couple[0]
    prev_rows = prev_couple[0]
    reciprocal = 1.0 / inner_diag[0]
    rows, order = own_rows.shape
    place = lax.axis_index("space")
    size = lax.axis_size("space")
    row_start = place * rows
    partition = lax.axis_index("tm")
    parts = lax.axis_size("tm")

    def between(block, route):
        return lax.ppermute(block, "tm", [(a, b) for a, b in route if 0 <= b < parts])

    even = range(0, parts, 2)
    pivots = range(1, parts, 4)
    everyone = range(parts)

    def one_step(ahead, back, step):
        up = [(j, j + 1) for j in range(step - 1, size - 1)]
        down = [(j, j - 1) for j in range(1, size - step + 1)]
        return lax.ppermute(ahead, "space", up), lax.ppermute(back, "space", down)

    def block_at(arrived, spot):
        block = arrived[0][0]
        for step in range(1, len(arrived)):
            if spot + step < size:
                block = jnp.where(place == spot + step, arrived[step][0], block)
            if spot - step >= 0:
                block = jnp.where(place == spot - step, arrived[step][1], block)
        return block

    is_first = partition == 0
    is_pivot = partition % 2 == 0
    is_receiver = partition % 2 == 1
    is_last = partition % 4 == 3
    flags = jnp.stack(
        [is_first.astype(jnp.int32), place, is_pivot.astype(jnp.int32), is_last.astype(jnp.int32)]
    )
    diagonal_block = lax.dynamic_slice_in_dim(separator, row_start, rows, 1)
    own_long = opening(flags, own_rows, prev_rows, diagonal_block, rows_of(reciprocal))
    own_arrived = [(own_long, own_long)]
    prev_arrived = [(prev_rows, prev_rows)]
    for step in range(1, size):
        own_arrived.append(one_step(*own_arrived[-1], step))
        prev_arrived.append(one_step(*prev_arrived[-1], step))
    words_arrived = [tuple(block[rows:] for block in pair) for pair in own_arrived]

    left_side = place < size // 2
    late_start = jnp.where(left_side, size - 1, 0) * rows
    is_end = jnp.logical_or(place == 0, place == size - 1)
    prev_blocks = [block_at(prev_arrived[:-1], spot) for spot in range(size)]
    zero = jnp.zeros_like(prev_rows)
    prev_blocks[0] = jnp.where(place == size - 1, zero, prev_blocks[0])
    prev_blocks[-1] = jnp.where(place == 0, zero, prev_blocks[-1])
    prev_first = jnp.concatenate(prev_blocks)
    prev_far = jnp.where(left_side, prev_blocks[-1], prev_blocks[0])
    prev_first, prev_far = lax.optimization_barrier((prev_first, prev_far))
    words = [block_at(words_arrived, spot) for spot in range(size)]

    def pair_sum(block, at):
        return block[at].astype(F32) + block[at + 1].astype(F32)

    part_diag = jnp.concatenate([pair_sum(block, 0)[:rows] for block in words])
    prev_diag = jnp.concatenate([pair_sum(block, 2)[:rows] for block in words])
    part_diag, prev_diag = lax.optimization_barrier((part_diag, prev_diag))
    diag = part_diag - between(prev_diag, [(p, p - 1) for p in everyone])
    pivot_diag = between(part_diag, [(p, p + 1) for p in even]) - prev_diag
    scale = (1.0 / jnp.maximum(diag, 1.0)).astype(BF16)
    pivot_scale = (1.0 / jnp.maximum(pivot_diag, 1.0)).astype(BF16)

    own_scaled = scaled_by(own_rows, reciprocal)
    sources = [own_long]
    for up, down in own_arrived[1:]:
        sources += [up, down]
    sources += [scale, pivot_scale]
    prev_first = scaled_by(prev_first, reciprocal)
    link, partial, prev_form, own_full, mine = early_forms(
        flags, prev_first, prev_rows, own_scaled, separator, sources
    )
    scale8, pivot_scale8 = rows_of(scale), rows_of(pivot_scale)

    from_below, from_above = prev_arrived[-1]
    late, corner, prev_late = late_forms(
        flags, rows_of(reciprocal), prev_rows, own_full, from_below, from_above, prev_far
    )
    link = lax.dynamic_update_slice_in_dim(link, late, late_start, 0)
    pivot_link = between(link, [(p, p + 1) for p in even])
    prev_form = lax.dynamic_update_slice_in_dim(prev_form, corner, late_start, 1)
    update, left_diag, right_diag = level_forms(flags, link, mine, scale8, pivot_scale8, prev_form)
    left_diag, right_diag = left_diag[0], right_diag[0]

    left_diag = between(left_diag, [(p, p - 1) for p in even])
    from_even = between(update, [(p, p - 1) for p in even])
    next_diag = diag - left_diag - right_diag
    next_scale = (1.0 / jnp.maximum(next_diag, 1.0)).astype(BF16)
    pivot_rows = lax.dynamic_slice_in_dim(pivot_link, row_start, rows, 0)
    pivot_rows = lax.optimization_barrier(scaled_by(pivot_rows, pivot_scale))
    next_rows = (-dot_nn(pivot_rows, link)).astype(BF16)
    next_long = jnp.concatenate([next_rows, jnp.broadcast_to(next_scale[None, :], (EXTRA, order))])
    pivot_long = between(next_long, [(p, p + 2) for p in pivots])

    left_next = scaled_by(dot_nt(scaled_by(next_rows, next_scale), link), pivot_scale)
    left_next = lax.optimization_barrier(left_next)
    left_next = (-dot_nt(left_next, pivot_link)).astype(BF16)
    from_pivot = between(left_next, [(p, p - 2) for p in pivots])
    right, columns, own_update = columns_forms(
        flags, own_rows, pivot_scale8, prev_first, prev_late, pivot_link, update, left_next
    )
    from_odd = between(own_update, [(p, p - 1) for p in range(1, parts, 2)])
    form, out_link = last_forms(
        flags, pivot_long, right, columns, next_rows, mine, partial, pivot_scale8, link, pivot_link
    )
    schur = form - (from_even + from_odd).astype(F32) - from_pivot.astype(F32)
    return (schur[None], out_link[None])


def solution(mesh):
    placed = (P("tm", "space", None), P("tm", "space", None), P("tm", "space", None), P("tm", None))
    return jax.shard_map(
        on_device,
        mesh=mesh,
        in_specs=placed,
        out_specs=(P("tm", "space", None), P("tm", "space", None)),
        check_vma=False,
    )
```

```python
import functools

import jax
import jax.numpy as jnp
from jax import lax
from jax.experimental import pallas as pl
from jax.experimental.pallas import tpu as pltpu
from jax.sharding import PartitionSpec as P

BF16 = jnp.bfloat16
F32 = jnp.float32
EXTRA = 16
WIDTH = 384

ANY = pl.BlockSpec(memory_space=pl.ANY)
HBM = pl.BlockSpec(memory_space=pltpu.HBM)
SHAPE = jax.ShapeDtypeStruct
FREE = pl.CostEstimate(flops=0, bytes_accessed=0, transcendentals=0)


def after(block, *others):
    def body(*refs):
        del refs

    return pl.pallas_call(
        body,
        out_shape=SHAPE(block.shape, block.dtype),
        in_specs=[ANY] * (1 + len(others)),
        out_specs=ANY,
        input_output_aliases={0: 0},
    )(block, *others)


def scaled_by(matrix, factors):
    return (matrix.astype(F32) * factors.astype(F32)[None, :]).astype(BF16)


def row_scaled_by(matrix, factors):
    return (matrix.astype(F32) * factors.astype(F32)[:, None]).astype(BF16)


def dot_nt(left, right):
    return lax.dot_general(left, right, (((1,), (1,)), ((), ())), preferred_element_type=F32)


def dot_nn(left, right):
    return lax.dot_general(left, right, (((1,), (0,)), ((), ())), preferred_element_type=F32)


def dot_tn(left, right):
    return lax.dot_general(left, right, (((0,), (0,)), ((), ())), preferred_element_type=F32)


def rows_of(scale):
    return jnp.broadcast_to(scale[None, :], (8, scale.shape[0]))


def whole_spec(shape):
    return pl.BlockSpec(shape, lambda j, f: (0,) * len(shape), pipeline_mode=pl.Buffered(1))


def along_spec(count):
    return pl.BlockSpec((count, WIDTH), lambda j, f: (0, j))


def down_spec(count):
    return pl.BlockSpec((WIDTH, count), lambda j, f: (j, 0))


def opening_kernel(flags, own, prev, separator, reciprocal, long):
    rows, order = own.shape
    row_ids = lax.broadcasted_iota(jnp.int32, (rows, rows), 0)
    col_ids = lax.broadcasted_iota(jnp.int32, (rows, rows), 1)
    on_diagonal = jnp.where(row_ids == col_ids, separator[...], 0.0)
    ones = jnp.ones((8, order), BF16)

    def split(value):
        high = value.astype(BF16)
        return high, (value - high.astype(F32)).astype(BF16)

    def form_diagonal(block):
        wide = block.astype(F32)
        high, low = split((wide * reciprocal[0:1]).astype(BF16).astype(F32) * wide)
        return (dot_nt(ones, high) + dot_nt(ones, low))[0:1]

    def placed(words, count):
        ids = lax.broadcasted_iota(jnp.int32, (EXTRA, count), 0)
        total = jnp.zeros((EXTRA, count), F32)
        for at, word in words.items():
            total = jnp.where(ids == at, word.astype(F32), total)
        return total.astype(BF16)

    long[0:rows, :] = own[...]
    long[rows:, :] = jnp.zeros((EXTRA, order), BF16)
    own_high, own_low = split(jnp.sum(on_diagonal, axis=0, keepdims=True) - form_diagonal(own[...]))
    prev_high, prev_low = split(form_diagonal(prev[...]))
    long[rows:, 0:rows] = placed({0: own_high, 1: own_low, 2: prev_high, 3: prev_low}, rows)


def opening(flags, own, prev, separator, reciprocal):
    rows, order = own.shape
    return pl.pallas_call(
        opening_kernel,
        out_shape=SHAPE((rows + EXTRA, order), BF16),
        grid_spec=pltpu.PrefetchScalarGridSpec(
            num_scalar_prefetch=1,
            grid=(1,),
            in_specs=[whole_spec((rows, order))] * 2 + [whole_spec((rows, rows)), whole_spec((8, order))],
            out_specs=whole_spec((rows + EXTRA, order)),
        ),
        compiler_params=pltpu.CompilerParams(vmem_limit_bytes=32 * 1024 * 1024),
        cost_estimate=FREE,
    )(flags, own, prev, separator, reciprocal)


def early_kernel(size, flags, prev_whole, prev_rows, own_rows, separator, *refs):
    sources = refs[: 2 * size - 1]
    link, partial, form, own_out, mine, own, sems = refs[2 * size + 1 :]
    rows = separator.shape[0]
    step = pl.program_id(0)
    here = pl.ds(pl.multiple_of(step * WIDTH, WIDTH), WIDTH)

    def copies():
        for spot in range(size):
            for by, source in enumerate(sources):
                distance = (by + 1) // 2 if by % 2 else -(by // 2)
                target = own.at[pl.ds(spot * rows, rows)]
                copy = pltpu.make_async_copy(source.at[pl.ds(0, rows)], target, sems.at[spot])
                yield flags[1] - spot == distance, copy

    @pl.when(step == 0)
    def _():
        for chosen, copy in copies():
            pl.when(chosen)(copy.start)
        for chosen, copy in copies():
            pl.when(chosen)(copy.wait)

    block = own[here, :]
    own_out[...] = block
    link[...] = jnp.where(flags[0] == 1, 0.0, -dot_nt(prev_whole[...], block)).astype(BF16)
    mine[...] = link[pl.ds(pl.multiple_of(flags[1] * rows, rows), rows), :]
    partial[...] = separator[...] - dot_nt(own_rows[...], block)
    form[...] = dot_nt(prev_rows[...], prev_whole[here, :])


def early_forms(flags, prev_whole, prev_rows, own_rows, separator, sources):
    rows, order = own_rows.shape
    size = order // rows
    return pl.pallas_call(
        functools.partial(early_kernel, size),
        out_shape=[
            SHAPE((order, order), BF16),
            SHAPE((rows, order), F32),
            SHAPE((rows, order), F32),
            SHAPE((order, order), BF16),
            SHAPE((rows, order), BF16),
        ],
        grid_spec=pltpu.PrefetchScalarGridSpec(
            num_scalar_prefetch=1,
            grid=(order // WIDTH,),
            in_specs=[
                whole_spec((order, order)),
                whole_spec((rows, order)),
                whole_spec((rows, order)),
                along_spec(rows),
            ]
            + [ANY] * len(sources),
            out_specs=[along_spec(order), along_spec(rows), along_spec(rows), down_spec(order), along_spec(rows)],
            scratch_shapes=[pltpu.VMEM((order, order), BF16), pltpu.SemaphoreType.DMA((size,))],
        ),
        compiler_params=pltpu.CompilerParams(vmem_limit_bytes=30 * 1024 * 1024),
        cost_estimate=FREE,
    )(flags, prev_whole, prev_rows, own_rows, separator, *sources)


def late_kernel(
    size, flags, reciprocal, prev_rows, own, from_below, from_above, far, link, corner, scaled, raw, sem
):
    place = flags[1]
    step = pl.program_id(0)
    width = own.shape[0]
    here = pl.ds(pl.multiple_of(step * width, width), width)

    @pl.when(step == 0)
    def _():
        for chosen, source in (
            (place == 0, from_above),
            (place == size - 1, from_below),
            (jnp.logical_and(place != 0, place != size - 1), far),
        ):
            copy = pltpu.make_async_copy(source, raw, sem)
            pl.when(chosen)(copy.start)
            pl.when(chosen)(copy.wait)
        scaled[...] = (raw[...].astype(F32) * reciprocal[0:1]).astype(BF16)
        corner[...] = dot_nt(prev_rows[...], scaled[...])

    link[:, here] = jnp.where(flags[0] == 1, 0.0, -dot_nt(scaled[...], own[...])).astype(BF16)


def late_forms(flags, reciprocal, prev_rows, own, from_below, from_above, far):
    rows, order = prev_rows.shape
    size = order // rows
    width = 512
    return pl.pallas_call(
        functools.partial(late_kernel, size),
        out_shape=[SHAPE((rows, order), BF16), SHAPE((rows, rows), F32), SHAPE((rows, order), BF16)],
        grid_spec=pltpu.PrefetchScalarGridSpec(
            num_scalar_prefetch=1,
            grid=(order // width,),
            in_specs=[
                whole_spec((8, order)),
                whole_spec((rows, order)),
                pl.BlockSpec((width, order), lambda j, f: (j, 0)),
                ANY,
                ANY,
                ANY,
            ],
            out_specs=[whole_spec((rows, order)), whole_spec((rows, rows)), whole_spec((rows, order))],
            scratch_shapes=[pltpu.VMEM((rows, order), BF16), pltpu.SemaphoreType.DMA],
        ),
        compiler_params=pltpu.CompilerParams(vmem_limit_bytes=18 * 1024 * 1024),
    )(flags, reciprocal, prev_rows, own, from_below, from_above, far)


def level_kernel(flags, link, mine, scale, pivot_scale, form, update, left_diag, right_diag):
    part = link[...]
    scaled = mine[...] * scale[0:1]
    keep = jnp.where(flags[2] == 1, 1.0, 0.0)
    update[...] = (form[...] + keep * dot_nt(scaled, part)).astype(BF16)
    square = part * part
    left_diag[...] = dot_nt(scale[...], square)

    @pl.when(pl.program_id(0) == 0)
    def _():
        right_diag[...] = jnp.zeros_like(right_diag)

    right_diag[...] += dot_nn(pivot_scale[...], square)


def level_forms(flags, link, mine, scale, pivot_scale, form):
    rows, order = form.shape
    width = 512
    along = lambda count: pl.BlockSpec((count, width), lambda j, f: (0, j))
    return pl.pallas_call(
        level_kernel,
        out_shape=[SHAPE((rows, order), BF16), SHAPE((8, order), F32), SHAPE((8, order), F32)],
        grid_spec=pltpu.PrefetchScalarGridSpec(
            num_scalar_prefetch=1,
            grid=(order // width,),
            in_specs=[
                pl.BlockSpec((width, order), lambda j, f: (j, 0)),
                whole_spec((rows, order)),
                whole_spec((8, order)),
                along(8),
                along(rows),
            ],
            out_specs=[along(rows), along(8), whole_spec((8, order))],
        ),
        compiler_params=pltpu.CompilerParams(vmem_limit_bytes=18 * 1024 * 1024),
        cost_estimate=FREE,
    )(flags, link, mine, scale, pivot_scale, form)


def fetched(early, late, whole, sems, at):
    rows, order = late.shape
    size = order // rows
    place = at[0]
    low = place < size // 2
    spans = [pl.ds(spot * rows, rows) for spot in range(size)]
    copies = []
    for spot, span in enumerate(spans):
        plain = pltpu.make_async_copy(early.at[span], whole.at[span], sems.at[spot])
        if spot not in (0, size - 1):
            copies.append((True, plain))
            continue
        is_late = low if spot else jnp.logical_not(low)
        copies.append((jnp.logical_not(is_late), plain))
        copies.append((is_late, pltpu.make_async_copy(late, whole.at[span], sems.at[spot])))
    for chosen, copy in copies:
        pl.when(chosen)(copy.start) if chosen is not True else copy.start()

    def wait():
        for chosen, copy in copies:
            pl.when(chosen)(copy.wait) if chosen is not True else copy.wait()

    return wait


def times(block, factors):
    return (block.astype(F32) * factors[0:1].astype(F32)).astype(BF16)


def columns_kernel(
    flags, own, pivot_scale, prev_early, prev_late, pivot_whole, update, ready,
    right, columns, moved, prev, pivot, results, sems, more_sems,
):
    del ready
    move = pltpu.make_async_copy(update, moved, more_sems.at[0])
    move.start()
    wait_prev = fetched(prev_early, prev_late, prev, sems, [flags[1]])
    copy = pltpu.make_async_copy(pivot_whole, pivot, more_sems.at[1])
    copy.start()
    wait_prev()
    across = jnp.where(flags[0] == 1, 0.0, -dot_nt(own[...], prev[...])).astype(BF16)
    across = times(across, pivot_scale)
    results[0] = across
    store = pltpu.make_async_copy(results.at[0], right, more_sems.at[2])
    store.start()
    copy.wait()
    results[1] = (-dot_nt(across, pivot[...])).astype(BF16)
    last = pltpu.make_async_copy(results.at[1], columns, more_sems.at[3])
    last.start()
    for copy in (move, store, last):
        copy.wait()


def columns_forms(flags, own, pivot_scale, prev_early, prev_late, pivot, update, ready):
    rows, order = own.shape
    out = SHAPE((rows, order), BF16)
    return pl.pallas_call(
        columns_kernel,
        out_shape=[out, out, out],
        grid_spec=pltpu.PrefetchScalarGridSpec(
            num_scalar_prefetch=1,
            grid=(1,),
            in_specs=[whole_spec((rows, order)), whole_spec((8, order))] + [ANY] * 5,
            out_specs=[HBM, HBM, HBM],
            scratch_shapes=[
                pltpu.VMEM((order, order), BF16),
                pltpu.VMEM((order, order), BF16),
                pltpu.VMEM((2, rows, order), BF16),
                pltpu.SemaphoreType.DMA((order // rows,)),
                pltpu.SemaphoreType.DMA((4,)),
            ],
        ),
        compiler_params=pltpu.CompilerParams(vmem_limit_bytes=22 * 1024 * 1024),
        cost_estimate=FREE,
    )(flags, own, pivot_scale, prev_early, prev_late, pivot, update, ready)


def last_kernel(
    flags, pivot_scale, pivot_rows, right_whole, columns_whole, next_rows, mine, partial, link_whole, pivot_whole,
    form, new, link, pivot, last, long, right, columns, sems,
):
    rows = right.shape[0]
    small = [
        pltpu.make_async_copy(pivot_rows, long, sems.at[4]),
        pltpu.make_async_copy(columns_whole, columns, sems.at[5]),
        pltpu.make_async_copy(right_whole, right, sems.at[6]),
    ]
    for copy in small:
        copy.start()
    even, final = flags[2] == 1, flags[3] == 1
    other = jnp.logical_not(jnp.logical_or(even, final))
    fetch = [
        pltpu.make_async_copy(pivot_whole, pivot, sems.at[0]),
        pltpu.make_async_copy(link_whole, link, sems.at[1]),
        pltpu.make_async_copy(partial, form, sems.at[2]),
    ]
    for copy in fetch:
        copy.start()
    plain = [(even, pltpu.make_async_copy(mine, new, sems.at[3]))]
    plain.append((other, pltpu.make_async_copy(next_rows, new, sems.at[3])))
    for chosen, copy in plain:
        pl.when(chosen)(copy.start)
    wide = pivot_scale[0:1].astype(F32)
    for copy in small:
        copy.wait()
    scale = long[rows : rows + EXTRA, :]
    fetch[0].wait()
    inner = dot_nn(times(columns[...], scale), pivot[...]) * wide
    keep = jnp.where(final, 1.0, 0.0)
    factor = (right[...].astype(F32) - inner * keep).astype(BF16)
    inner = (dot_nn(times(long[0:rows, :], scale), pivot[...]) * wide).astype(BF16)
    fetch[1].wait()
    last[...] = dot_nn(inner, link[...]).astype(BF16)
    store = pltpu.make_async_copy(last, new, sems.at[3])
    pl.when(final)(store.start)
    fetch[2].wait()
    odd = jnp.where(even, 0.0, 1.0)
    form[...] -= odd * dot_nn(factor, link[...])
    for chosen, copy in plain + [(final, store)]:
        pl.when(chosen)(copy.wait)


def last_forms(flags, pivot_rows, right, columns, next_rows, mine, partial, pivot_scale, link, pivot):
    rows, order = right.shape
    return pl.pallas_call(
        last_kernel,
        out_shape=[SHAPE((rows, order), F32), SHAPE((rows, order), BF16)],
        grid_spec=pltpu.PrefetchScalarGridSpec(
            num_scalar_prefetch=1,
            grid=(1,),
            in_specs=[whole_spec((8, order))] + [HBM] * 8,
            out_specs=[whole_spec((rows, order)), ANY],
            scratch_shapes=[
                pltpu.VMEM((order, order), BF16),
                pltpu.VMEM((order, order), BF16),
                pltpu.VMEM((rows, order), BF16),
                pltpu.VMEM(pivot_rows.shape, BF16),
                pltpu.VMEM((rows, order), BF16),
                pltpu.VMEM((rows, order), BF16),
                pltpu.SemaphoreType.DMA((7,)),
            ],
        ),
        compiler_params=pltpu.CompilerParams(vmem_limit_bytes=28 * 1024 * 1024),
        cost_estimate=FREE,
    )(flags, pivot_scale, pivot_rows, right, columns, next_rows, mine, partial, link, pivot)


def on_device(sep_block, own_couple, prev_couple, inner_diag):
    separator = sep_block[0]
    own_rows = own_couple[0]
    prev_rows = prev_couple[0]
    reciprocal = 1.0 / inner_diag[0]
    rows, order = own_rows.shape
    place = lax.axis_index("space")
    size = lax.axis_size("space")
    row_start = place * rows
    partition = lax.axis_index("tm")
    parts = lax.axis_size("tm")

    def between(block, route):
        return lax.ppermute(block, "tm", [(a, b) for a, b in route if 0 <= b < parts])

    even = range(0, parts, 2)
    pivots = range(1, parts, 4)
    everyone = range(parts)

    def one_step(ahead, back, step):
        up = [(j, j + 1) for j in range(step - 1, size - 1)]
        down = [(j, j - 1) for j in range(1, size - step + 1)]
        return lax.ppermute(ahead, "space", up), lax.ppermute(back, "space", down)

    def block_at(arrived, spot):
        block = arrived[0][0]
        for step in range(1, len(arrived)):
            if spot + step < size:
                block = jnp.where(place == spot + step, arrived[step][0], block)
            if spot - step >= 0:
                block = jnp.where(place == spot - step, arrived[step][1], block)
        return block

    is_first = partition == 0
    is_pivot = partition % 2 == 0
    is_receiver = partition % 2 == 1
    is_last = partition % 4 == 3
    flags = jnp.stack(
        [is_first.astype(jnp.int32), place, is_pivot.astype(jnp.int32), is_last.astype(jnp.int32)]
    )
    diagonal_block = lax.dynamic_slice_in_dim(separator, row_start, rows, 1)
    own_long = opening(flags, own_rows, prev_rows, diagonal_block, rows_of(reciprocal))
    own_arrived = [(own_long, own_long)]
    prev_arrived = [(prev_rows, prev_rows)]
    for step in range(1, size):
        own_arrived.append(one_step(*own_arrived[-1], step))
        prev_arrived.append(one_step(*prev_arrived[-1], step))
    words_arrived = [tuple(block[rows:] for block in pair) for pair in own_arrived]

    left_side = place < size // 2
    late_start = jnp.where(left_side, size - 1, 0) * rows
    is_end = jnp.logical_or(place == 0, place == size - 1)
    prev_blocks = [block_at(prev_arrived[:-1], spot) for spot in range(size)]
    zero = jnp.zeros_like(prev_rows)
    prev_blocks[0] = jnp.where(place == size - 1, zero, prev_blocks[0])
    prev_blocks[-1] = jnp.where(place == 0, zero, prev_blocks[-1])
    prev_first = jnp.concatenate(prev_blocks)
    prev_far = jnp.where(left_side, prev_blocks[-1], prev_blocks[0])
    prev_first, prev_far = lax.optimization_barrier((prev_first, prev_far))
    words = [block_at(words_arrived, spot) for spot in range(size)]

    def pair_sum(block, at):
        return block[at].astype(F32) + block[at + 1].astype(F32)

    part_diag = jnp.concatenate([pair_sum(block, 0)[:rows] for block in words])
    prev_diag = jnp.concatenate([pair_sum(block, 2)[:rows] for block in words])
    part_diag, prev_diag = lax.optimization_barrier((part_diag, prev_diag))
    diag = part_diag - between(prev_diag, [(p, p - 1) for p in everyone])
    pivot_diag = between(part_diag, [(p, p + 1) for p in even]) - prev_diag
    scale = (1.0 / jnp.maximum(diag, 1.0)).astype(BF16)
    pivot_scale = (1.0 / jnp.maximum(pivot_diag, 1.0)).astype(BF16)

    own_scaled = scaled_by(own_rows, reciprocal)
    sources = [own_long]
    for up, down in own_arrived[1:]:
        sources += [up, down]
    sources += [scale, pivot_scale]
    prev_first = scaled_by(prev_first, reciprocal)
    link, partial, prev_form, own_full, mine = early_forms(
        flags, prev_first, prev_rows, own_scaled, separator, sources
    )
    scale8, pivot_scale8 = rows_of(scale), rows_of(pivot_scale)

    from_below, from_above = prev_arrived[-1]
    late, corner, prev_late = late_forms(
        flags, rows_of(reciprocal), prev_rows, own_full, from_below, from_above, prev_far
    )
    link = lax.dynamic_update_slice_in_dim(link, late, late_start, 0)
    pivot_link = between(link, [(p, p + 1) for p in even])
    prev_form = lax.dynamic_update_slice_in_dim(prev_form, corner, late_start, 1)
    update, left_diag, right_diag = level_forms(flags, link, mine, scale8, pivot_scale8, prev_form)
    left_diag, right_diag = left_diag[0], right_diag[0]

    left_diag = between(left_diag, [(p, p - 1) for p in even])
    from_even = between(update, [(p, p - 1) for p in even])
    next_diag = diag - left_diag - right_diag
    next_scale = (1.0 / jnp.maximum(next_diag, 1.0)).astype(BF16)
    pivot_rows = lax.dynamic_slice_in_dim(pivot_link, row_start, rows, 0)
    pivot_rows = lax.optimization_barrier(scaled_by(pivot_rows, pivot_scale))
    next_rows = (-dot_nn(pivot_rows, link)).astype(BF16)
    next_long = jnp.concatenate([next_rows, jnp.broadcast_to(next_scale[None, :], (EXTRA, order))])
    pivot_long = between(next_long, [(p, p + 2) for p in pivots])

    left_next = scaled_by(dot_nt(scaled_by(next_rows, next_scale), link), pivot_scale)
    left_next = lax.optimization_barrier(left_next)
    left_next = (-dot_nt(left_next, pivot_link)).astype(BF16)
    from_pivot = between(left_next, [(p, p - 2) for p in pivots])
    right, columns, own_update = columns_forms(
        flags, own_rows, pivot_scale8, prev_first, prev_late, pivot_link, update, left_next
    )
    from_odd = between(own_update, [(p, p - 1) for p in range(1, parts, 2)])
    form, out_link = last_forms(
        flags, pivot_long, right, columns, next_rows, mine, partial, pivot_scale8, link, pivot_link
    )
    schur = form - (from_even + from_odd).astype(F32) - from_pivot.astype(F32)
    return (schur[None], out_link[None])


def solution(mesh):
    placed = (P("tm", "space", None), P("tm", "space", None), P("tm", "space", None), P("tm", None))
    return jax.shard_map(
        on_device,
        mesh=mesh,
        in_specs=placed,
        out_specs=(P("tm", "space", None), P("tm", "space", None)),
        check_vma=False,
    )
```
